32 devices in a mesh: grp: 4 (over y, core), seq: 8 (over z, x).
Axes of the slice: x: 2, y: 2, z: 4, core: 2. Of those that a mesh axis runs over, the one named last changes fastest.
Arguments:
- hidden_in: bfloat16 [4096, 1024], P(('grp', 'seq')), may hold values from -6 to 6
- skips: bfloat16 [4096, 1024], P(('grp', 'seq')), may hold values from -6 to 6
- lengths: int32 [4, 8], P('grp'), may hold values from 1 to 896, as said below
- times: int32 [4, 8], P('grp'), may hold values from 0 to 999
- skip_weight: bfloat16 [2048, 1024], P('seq'), may hold values from -0.125 to 0.125
- cond_weight: bfloat16 [1024, 2048], P('seq'), may hold values from -0.1875 to 0.1875
- qkv_weight: bfloat16 [1024, 3072], P('seq'), may hold values from -0.1875 to 0.1875
- out_weight: bfloat16 [1024, 1024], P('seq'), may hold values from -1.5 to 1.5
- up_weight: bfloat16 [1024, 4096], P('seq'), may hold values from -0.1875 to 0.1875
- down_weight: bfloat16 [4096, 1024], P('seq'), may hold values from -0.09375 to 0.09375
- cotangent: bfloat16 [4096, 1024], P(('grp', 'seq')), may hold values from -6 to 6
Outputs:
- block_out: bfloat16 [4096, 1024], P(('grp', 'seq'))
- in_grad: bfloat16 [4096, 1024], P(('grp', 'seq'))
- skip_grad: bfloat16 [4096, 1024], P(('grp', 'seq'))
- skip_weight_grad: float32 [2048, 1024], P('seq')
- cond_weight_grad: float32 [1024, 2048], P('seq')
- qkv_weight_grad: float32 [1024, 3072], P('seq')
- out_weight_grad: float32 [1024, 1024], P('seq')
- up_weight_grad: float32 [1024, 4096], P('seq')
- down_weight_grad: float32 [4096, 1024], P('seq')
The draws below stay inside these ranges and needn't reach their ends.
Inputs may be any that keep to these rules, and one draw needn't show every extreme that they name: Each row holds one group's 8 utterance lengths in frame order, summing to 1024; exactly one of them, never the first or the last, has 896 frames, and the others together have 128.
All inputs are finite; a program needn't handle non-finite values.
Results may differ from the reference program's by a relative error of at most 0.029.
Values may be sent and summed in bfloat16 or wider, within the bound.
No kernel may reach another device: no remote copies, remote signals or barrier semaphores. Data moves between devices by JAX's collectives and lax.ppermute only.
A program may use at most 256 MiB of HBM per device.

```python
import math
import jax
import jax.numpy as jnp
from jax import lax

D = 1024
HEADS = 16
HEAD = 64
FF = 4096
TOK_DEV = 128
UTT = 8
GROUP = 1024
GROUPS = 4
FRAMES = 4096
N_GRP = 4
N_SEQ = 8


def draw_lengths(key, part):
    key = jax.random.fold_in(key, 11)
    table = []
    for group_idx in range(N_GRP):
        group_key = jax.random.fold_in(key, group_idx)
        cut_key, place_key = jax.random.split(group_key)
        cut_points = jnp.sort(jax.random.permutation(cut_key, TOK_DEV - 1)[:UTT - 2] + 1).astype(jnp.int32)
        edges = jnp.concatenate([jnp.zeros((1,), jnp.int32), cut_points, jnp.full((1,), TOK_DEV, jnp.int32)])
        short_lens = edges[1:] - edges[:-1]
        place = jax.random.randint(place_key, (), 1, UTT - 1)
        index = jnp.arange(UTT, dtype=jnp.int32)
        source = jnp.clip(jnp.where(index < place, index, index - 1), 0, UTT - 2)
        gathered = short_lens[source]
        long_len = (N_SEQ - 1) * TOK_DEV
        table.append(jnp.where(index == place, long_len, gathered))
    return jnp.stack(table).astype(jnp.int32)


def touch_ends(values, rng, smallest, top_value):
    extent = values.shape
    index_at = [jax.random.randint(jax.random.fold_in(rng, axis), (), 0, extent[axis]) for axis in range(len(extent))]
    values = values.at[tuple(index_at)].set(smallest)
    longest = extent.index(max(extent))
    index_at[longest] = (index_at[longest] + 1) % extent[longest]
    return values.at[tuple(index_at)].set(top_value)


def level_of(key, extent, shards, least, top_value):
    def one(position, blocks):
        heights = jax.random.uniform(jax.random.fold_in(jax.random.fold_in(key, 6), position), (blocks,), jnp.float32, least / len(shards), top_value / len(shards))
        return jnp.repeat(jnp.exp(heights), extent[position] // blocks).reshape((-1,) + (1,) * (len(extent) - position - 1))

    factor_of = one(*shards[0])
    for cut in shards[1:]:
        factor_of = factor_of * one(*cut)
    return factor_of


def normal_values(own_key, shape, scale, limit, shards=(), held_as=jnp.bfloat16):
    values = scale * jax.random.normal(own_key, shape, jnp.float32)
    if shards:
        values = values * level_of(own_key, shape, shards, -0.22, 0.18)
    return jnp.clip(values, -limit, limit).astype(held_as)


def setup_inputs(seed: int = 0) -> dict:
    splits = jax.random.split(jax.random.key(seed), 12)
    return {
        "hidden_in": normal_values(splits[0], (FRAMES, D), 1.0, 6.0, ((0, 32),)),
        "skips": normal_values(splits[1], (FRAMES, D), 1.0, 6.0, ((0, 32),)),
        "lengths": draw_lengths(jax.random.fold_in(splits[11], 71), 0),
        "times": touch_ends(jax.random.randint(splits[3], (GROUPS, UTT), 0, 1000), jax.random.fold_in(splits[3], 1), 0, 999).astype(jnp.int32),
        "skip_weight": normal_values(splits[4], (2 * D, D), (2 * D) ** -0.5, 0.125, ((0, 8),)),
        "cond_weight": normal_values(splits[5], (D, 2 * D), D ** -0.5, 0.1875, ((0, 8),)),
        "qkv_weight": normal_values(splits[6], (D, 3 * D), D ** -0.5, 0.1875, ((0, 8),)),
        "out_weight": normal_values(splits[7], (D, D), (D // 64) ** -0.5, 1.5, ((0, 8),)),
        "up_weight": normal_values(splits[8], (D, FF), D ** -0.5, 0.1875, ((0, 8),)),
        "down_weight": normal_values(splits[9], (FF, D), FF ** -0.5, 0.09375, ((0, 8),)),
        "cotangent": normal_values(splits[10], (FRAMES, D), 1.0, 6.0, ((0, 32),)),
    }


@jax.custom_vjp
def low(v):
    return lax.optimization_barrier(v.astype(jnp.bfloat16)).astype(jnp.float32)

@jax.custom_vjp
def low_back(v):
    return v

def low_keep(v):
    return (low(v), None)

def low_pass(kept, grad):
    return (grad,)

def back_keep(v):
    return (v, None)

def back_low(kept, grad):
    return (low(grad),)
low.defvjp(low_keep, low_pass)
low_back.defvjp(back_keep, back_low)
PRECISE = lax.Precision.HIGHEST
EPS = 1e-06

def matmul(left, right):
    return jnp.dot(left, right, precision=PRECISE)

def embed_steps(time_steps):
    half_width = D // 2
    freqs = jnp.exp(-math.log(10000.0) * jnp.arange(half_width, dtype=jnp.float32) / half_width)
    angles = time_steps[:, None] * freqs[None, :]
    return jnp.concatenate([jnp.sin(angles), jnp.cos(angles)], axis=1)

def rotate(vectors, positions):
    half_size = HEAD // 2
    inverse = jnp.exp(-math.log(10000.0) * jnp.arange(half_size, dtype=jnp.float32) / half_size)
    angles = positions[:, None] * inverse[None, :]
    cosine = jnp.cos(angles)[:, None, :]
    sine = jnp.sin(angles)[:, None, :]
    split = vectors.reshape(vectors.shape[0], HEADS, HEAD)
    first_half = split[..., :half_size]
    second_half = split[..., half_size:]
    turned = jnp.concatenate([first_half * cosine - second_half * sine, first_half * sine + second_half * cosine], axis=-1)
    return turned.reshape(vectors.shape[0], D)

def scale_norm(hidden, cond_part):
    return hidden * lax.rsqrt(lax.optimization_barrier(jnp.mean(hidden * hidden, axis=1, keepdims=True)) + EPS) * (1.0 + cond_part)

def attention(queries, keys, values, owners):
    qblock = math.gcd(GROUP, 512)
    number = GROUP // qblock
    score_scale = HEAD ** (-0.5)
    keys_h = keys.reshape(GROUP, HEADS, HEAD)
    values_h = values.reshape(GROUP, HEADS, HEAD)
    q_blocks = queries.reshape(number, qblock, HEADS, HEAD)
    owner_blocks = owners.reshape(number, qblock)

    def one_block(pair):
        q_blk, blk_owner = pair
        raw = jnp.einsum('qhd,khd->qhk', q_blk, keys_h, precision=PRECISE)
        raw = low_back(raw)
        same_utt = (blk_owner[:, None] == owners[None, :])[:, None, :]
        scores = jnp.where(same_utt, raw * score_scale, -1e+30)
        probs = low(jax.nn.softmax(scores, axis=-1))
        return jnp.einsum('qhk,khd->qhd', probs, values_h, precision=PRECISE)
    result = lax.map(jax.checkpoint(one_block), (q_blocks, owner_blocks))
    return result.reshape(GROUP, D)

def block_forward(inputs, skipped, params, time_steps, owners, positions):
    skip_w, cond_w, qkv_w, out_w, up_w, down_w = params
    h_zero = low_back(matmul(jnp.concatenate([inputs, skipped], axis=1), skip_w))
    emb = low(embed_steps(time_steps))
    cond = low_back(matmul(emb, cond_w))
    normed = low(scale_norm(h_zero, cond[:, :D]))
    qkv = low_back(matmul(normed, qkv_w))
    queries = low(rotate(qkv[:, :D], positions))
    keys = low(rotate(qkv[:, D:2 * D], positions))
    values = low(qkv[:, 2 * D:])
    attended = low(low_back(attention(queries, keys, values, owners)))
    h_one = h_zero + low_back(matmul(attended, out_w))
    normed_two = low(scale_norm(h_one, cond[:, D:]))
    pre = low_back(matmul(normed_two, up_w))
    act = low(jax.nn.gelu(pre, approximate=False))
    return h_one + low_back(matmul(act, down_w))

def reference(hidden_in, skips, lengths, times, skip_weight, cond_weight, qkv_weight, out_weight, up_weight, down_weight, cotangent):
    params = tuple((array.astype(jnp.float32) for array in (skip_weight, cond_weight, qkv_weight, out_weight, up_weight, down_weight)))
    frames = jnp.arange(GROUP, dtype=jnp.int32)
    totals = tuple((jnp.zeros(array.shape, jnp.float32) for array in params))
    outputs, in_grads, skip_grads = ([], [], [])
    for group_idx in range(N_GRP):
        row_slice = slice(group_idx * GROUP, (group_idx + 1) * GROUP)
        utt_lengths = lengths[group_idx].astype(jnp.int32)
        utt_ends = jnp.cumsum(utt_lengths).astype(jnp.int32)
        starts = (utt_ends - utt_lengths).astype(jnp.int32)
        owners = lax.optimization_barrier(jnp.sum((frames[:, None] >= utt_ends[None, :]).astype(jnp.int32), axis=1)).astype(jnp.int32)
        onehot = owners[:, None] == jnp.arange(UTT, dtype=jnp.int32)[None, :]
        positions = (frames - lax.optimization_barrier(jnp.sum(jnp.where(onehot, starts[None, :], 0), axis=1))).astype(jnp.float32)
        time_steps = lax.optimization_barrier(jnp.sum(jnp.where(onehot, times[group_idx].astype(jnp.int32)[None, :], 0), axis=1)).astype(jnp.float32)

        def forward(inputs, skipped, *weights_in):
            return block_forward(inputs, skipped, weights_in, time_steps, owners, positions)
        result, pullback = jax.vjp(forward, hidden_in[row_slice].astype(jnp.float32), skips[row_slice].astype(jnp.float32), *params)
        gradients = pullback(cotangent[row_slice].astype(jnp.float32))
        outputs.append(result.astype(jnp.bfloat16))
        in_grads.append(gradients[0].astype(jnp.bfloat16))
        skip_grads.append(gradients[1].astype(jnp.bfloat16))
        totals = tuple((total + grad for total, grad in zip(totals, gradients[2:])))
    return (jnp.concatenate(outputs, axis=0), jnp.concatenate(in_grads, axis=0), jnp.concatenate(skip_grads, axis=0), totals[0], totals[1], totals[2], totals[3], totals[4], totals[5])
```

```python
import math

import jax
import jax.numpy as jnp
from jax import lax
from jax.experimental import pallas as pl
from jax.experimental.pallas import tpu as pltpu
from jax.sharding import PartitionSpec as P

HEADS = 16


EPS = 1e-06


def contract(left, right, left_dim, right_dim):
    return lax.dot_general(
        left, right, (((left_dim,), (right_dim,)), ((), ())), preferred_element_type=jnp.float32
    )


def matmul(left, right):
    return jnp.dot(left, right, preferred_element_type=jnp.float32)


def owner_of(frames, utt_ends):
    return jnp.sum((frames[:, None] >= utt_ends[None, :]).astype(jnp.int32), axis=1)


def same_owner(query_owner, key_owner):
    return (query_owner[:, None] == key_owner[None, :])[:, None, :]


def embed_steps(time_steps, model_width):
    half_width = model_width // 2
    freqs = jnp.exp(-math.log(10000.0) * jnp.arange(half_width, dtype=jnp.float32) / half_width)
    angles = time_steps[:, None] * freqs[None, :]
    return jnp.concatenate([jnp.sin(angles), jnp.cos(angles)], axis=1)


def rotate(vectors, positions, head_count, direction):
    tok_rows, model_width = vectors.shape
    head_size = model_width // head_count
    half_size = head_size // 2
    inverse = jnp.exp(-math.log(10000.0) * jnp.arange(half_size, dtype=jnp.float32) / half_size)
    angles = positions[:, None] * inverse[None, :]
    cosine = jnp.cos(angles)[:, None, :]
    sine = direction * jnp.sin(angles)[:, None, :]
    split = vectors.reshape(tok_rows, head_count, head_size)
    first_half = split[..., :half_size]
    second_half = split[..., half_size:]
    turned = jnp.concatenate(
        [first_half * cosine - second_half * sine, first_half * sine + second_half * cosine],
        axis=-1,
    )
    return turned.reshape(tok_rows, model_width)


def scale_norm(hidden, cond_part):
    return (
        hidden
        * lax.rsqrt(jnp.mean(hidden * hidden, axis=1, keepdims=True) + EPS)
        * (1.0 + cond_part)
    )


def over_blocks(update, running, arrays, first_row, block_cap):
    row_count = arrays[0].shape[0]
    block_size = math.gcd(row_count, block_cap)
    number = row_count // block_size
    if number == 1:
        return update(running, arrays, first_row)
    stacked = tuple((array.reshape((number, block_size) + array.shape[1:]) for array in arrays))
    offsets = first_row + block_size * jnp.arange(number, dtype=jnp.int32)

    def over_scan_step(inner, scan_in):
        return (update(inner, scan_in[0], scan_in[1]), None)

    result, unused = lax.scan(over_scan_step, running, (stacked, offsets))
    return result


def grad_terms(
    q_heads, do_heads, log_total, row_delta, key_heads, value_heads, same_utt, score_scale
):
    scores = (
        jnp.einsum("qhd,khd->qhk", q_heads, key_heads, preferred_element_type=jnp.float32)
        * score_scale
    )
    probs = jnp.where(same_utt, jnp.exp(scores - log_total[..., None]), 0.0)
    d_probs = jnp.einsum("qhd,khd->qhk", do_heads, value_heads, preferred_element_type=jnp.float32)
    d_scores = (probs * (d_probs - row_delta[..., None]) * score_scale).astype(jnp.bfloat16)
    return (probs.astype(jnp.bfloat16), d_scores)


def scatter_first(after, grad):
    return lax.optimization_barrier(
        (after, lax.psum_scatter(grad, "seq", scatter_dimension=0, tiled=True))
    )


def plain_body(
    hidden_in,
    skips,
    lengths,
    times,
    skip_weight,
    cond_weight,
    qkv_weight,
    out_weight,
    up_weight,
    down_weight,
    cotangent,
):
    tok_rows, model_width = hidden_in.shape
    head_count = HEADS
    head_size = model_width // head_count
    score_scale = head_size ** (-0.5)
    first_frame = lax.axis_index("seq") * tok_rows
    utt_lengths = lengths[0]
    utt_ends = jnp.cumsum(utt_lengths)
    starts = utt_ends - utt_lengths
    frames = first_frame + jnp.arange(tok_rows, dtype=jnp.int32)
    query_owner = owner_of(frames, utt_ends)
    onehot = query_owner[:, None] == jnp.arange(utt_lengths.shape[0], dtype=jnp.int32)[None, :]
    positions = (frames - jnp.sum(jnp.where(onehot, starts[None, :], 0), axis=1)).astype(
        jnp.float32
    )
    time_steps = jnp.sum(jnp.where(onehot, times[0][None, :], 0), axis=1).astype(jnp.float32)
    gathered = (
        lax.all_gather(skip_weight, "seq", axis=0, tiled=True),
        lax.all_gather(cond_weight, "seq", axis=0, tiled=True),
        lax.all_gather(qkv_weight, "seq", axis=0, tiled=True),
        lax.all_gather(out_weight, "seq", axis=0, tiled=True),
        lax.all_gather(up_weight, "seq", axis=0, tiled=True),
        lax.all_gather(down_weight, "seq", axis=0, tiled=True),
    )
    w_skip, w_cond, w_qkv, w_out, w_up, w_down = gathered
    h_zero = matmul(hidden_in, w_skip[:model_width]) + matmul(skips, w_skip[model_width:])
    emb = embed_steps(time_steps, model_width).astype(jnp.bfloat16)
    cond = matmul(emb, w_cond)
    cond_attn = cond[:, :model_width]
    cond_ffn = cond[:, model_width:]
    normed = scale_norm(h_zero, cond_attn).astype(jnp.bfloat16)
    qkv = matmul(normed, w_qkv)
    queries = rotate(qkv[:, :model_width], positions, head_count, 1.0).astype(jnp.bfloat16)
    keys = rotate(qkv[:, model_width : 2 * model_width], positions, head_count, 1.0).astype(
        jnp.bfloat16
    )
    values = qkv[:, 2 * model_width :].astype(jnp.bfloat16)
    q_heads = queries.reshape(tok_rows, head_count, head_size)

    def forward_step(running, blocks, first_row):
        weighted, run_max, run_sum = running
        key_heads = blocks[0].reshape(-1, head_count, head_size)
        value_heads = blocks[1].reshape(-1, head_count, head_size)
        key_owner = owner_of(first_row + jnp.arange(key_heads.shape[0], dtype=jnp.int32), utt_ends)
        same_utt = same_owner(query_owner, key_owner)
        scores = (
            jnp.einsum("qhd,khd->qhk", q_heads, key_heads, preferred_element_type=jnp.float32)
            * score_scale
        )
        new_max = jnp.maximum(run_max, jnp.max(jnp.where(same_utt, scores, -1e30), axis=-1))
        weights_b = jnp.where(same_utt, jnp.exp(scores - new_max[..., None]), 0.0)
        factor = jnp.exp(run_max - new_max)
        run_sum = run_sum * factor + jnp.sum(weights_b, axis=-1)
        weighted = weighted * factor[..., None] + jnp.einsum(
            "qhk,khd->qhd",
            weights_b.astype(jnp.bfloat16),
            value_heads,
            preferred_element_type=jnp.float32,
        )
        return (weighted, new_max, run_sum)

    start_state = (
        jnp.zeros((tok_rows, head_count, head_size), jnp.float32),
        jnp.full((tok_rows, head_count), -1e30, jnp.float32),
        jnp.zeros((tok_rows, head_count), jnp.float32),
    )
    weighted, run_max, run_sum = over_blocks(
        forward_step,
        start_state,
        (
            lax.all_gather(keys, "seq", axis=0, tiled=True),
            lax.all_gather(values, "seq", axis=0, tiled=True),
        ),
        jnp.int32(0),
        1024,
    )
    attended_full = (weighted / run_sum[..., None]).reshape(tok_rows, model_width)
    log_total = run_max + jnp.log(run_sum)
    attended = attended_full.astype(jnp.bfloat16)
    h_one = h_zero + matmul(attended, w_out)
    normed_two = scale_norm(h_one, cond_ffn).astype(jnp.bfloat16)
    pre = matmul(normed_two, w_up)
    act = jax.nn.gelu(pre, approximate=False).astype(jnp.bfloat16)
    block_out = (h_one + matmul(act, w_down)).astype(jnp.bfloat16)
    regathered = (
        lax.all_gather(skip_weight, "seq", axis=0, tiled=True),
        lax.all_gather(cond_weight, "seq", axis=0, tiled=True),
        lax.all_gather(qkv_weight, "seq", axis=0, tiled=True),
        lax.all_gather(out_weight, "seq", axis=0, tiled=True),
        lax.all_gather(up_weight, "seq", axis=0, tiled=True),
        lax.all_gather(down_weight, "seq", axis=0, tiled=True),
    )
    w_skip, w_cond, w_qkv, w_out, w_up, w_down = regathered
    d_act = contract(cotangent, w_down, 1, 1)
    d_act, shard_down = scatter_first(d_act, contract(act, cotangent, 0, 0))
    unused, gelu_back = jax.vjp(lambda inner: jax.nn.gelu(inner, approximate=False), pre)
    d_pre = gelu_back(d_act)[0].astype(jnp.bfloat16)
    d_pre, shard_up = scatter_first(d_pre, contract(normed_two, d_pre, 0, 0))
    d_normed_two = contract(d_pre, w_up, 1, 1)
    unused, norm_back_two = jax.vjp(scale_norm, h_one, cond_ffn)
    d_h_norm, d_cond_ffn = norm_back_two(d_normed_two)
    d_h_one = cotangent.astype(jnp.float32) + d_h_norm
    d_h_low = d_h_one.astype(jnp.bfloat16)
    d_h_low, shard_out = scatter_first(d_h_low, contract(attended, d_h_low, 0, 0))
    d_attended = contract(d_h_low, w_out, 1, 1).astype(jnp.bfloat16)
    row_delta = jnp.sum(
        (d_attended.astype(jnp.float32) * attended_full).reshape(tok_rows, head_count, head_size),
        axis=-1,
    )
    do_heads = d_attended.reshape(tok_rows, head_count, head_size)
    keys_all, values_all = (
        lax.all_gather(keys, "seq", axis=0, tiled=True),
        lax.all_gather(values, "seq", axis=0, tiled=True),
    )
    key_total = keys_all.shape[0]
    block_size = math.gcd(key_total, 1024)
    number = key_total // block_size

    def body_scan_step(d_query, scan_in):
        key_block, value_block, offset = scan_in
        key_heads = key_block.reshape(block_size, head_count, head_size)
        value_heads = value_block.reshape(block_size, head_count, head_size)
        key_owner = owner_of(offset + jnp.arange(block_size, dtype=jnp.int32), utt_ends)
        probs_low, d_scores = grad_terms(
            q_heads,
            do_heads,
            log_total,
            row_delta,
            key_heads,
            value_heads,
            same_owner(query_owner, key_owner),
            score_scale,
        )
        d_query = d_query + jnp.einsum(
            "qhk,khd->qhd", d_scores, key_heads, preferred_element_type=jnp.float32
        )
        d_key = jnp.einsum(
            "qhk,qhd->khd", d_scores, q_heads, preferred_element_type=jnp.float32
        ).reshape(block_size, model_width)
        d_value = jnp.einsum(
            "qhk,qhd->khd", probs_low, do_heads, preferred_element_type=jnp.float32
        ).reshape(block_size, model_width)
        return (d_query, (d_key, d_value))

    d_query, terms = lax.scan(
        body_scan_step,
        jnp.zeros((tok_rows, head_count, head_size), jnp.float32),
        (
            keys_all.reshape(number, block_size, model_width),
            values_all.reshape(number, block_size, model_width),
            block_size * jnp.arange(number, dtype=jnp.int32),
        ),
    )
    value_terms, d_key = scatter_first(terms[1], terms[0].reshape(key_total, model_width))
    d_value = lax.psum_scatter(
        value_terms.reshape(key_total, model_width), "seq", scatter_dimension=0, tiled=True
    )
    d_qkv = jnp.concatenate(
        [
            rotate(d_query.reshape(tok_rows, model_width), positions, head_count, -1.0),
            rotate(d_key, positions, head_count, -1.0),
            d_value,
        ],
        axis=1,
    ).astype(jnp.bfloat16)
    d_qkv, shard_qkv = scatter_first(d_qkv, contract(normed, d_qkv, 0, 0))
    d_normed = contract(d_qkv, w_qkv, 1, 1)
    unused, norm_back_one = jax.vjp(scale_norm, h_zero, cond_attn)
    d_h_first, d_cond_attn = norm_back_one(d_normed)
    d_h_zero = (d_h_one + d_h_first).astype(jnp.bfloat16)
    d_cond = jnp.concatenate([d_cond_attn, d_cond_ffn], axis=1).astype(jnp.bfloat16)
    d_cond, shard_cond = scatter_first(d_cond, contract(emb, d_cond, 0, 0))
    grad_skip_w = jnp.concatenate(
        [contract(hidden_in, d_h_zero, 0, 0), contract(skips, d_h_zero, 0, 0)], axis=0
    )
    in_grad = contract(d_h_zero, w_skip[:model_width], 1, 1).astype(jnp.bfloat16)
    skip_grad = contract(d_h_zero, w_skip[model_width:], 1, 1).astype(jnp.bfloat16)
    shards = (
        lax.psum_scatter(grad_skip_w, "seq", scatter_dimension=0, tiled=True),
        shard_cond,
        shard_qkv,
        shard_out,
        shard_up,
        shard_down,
    )
    summed = (
        lax.psum(shards[0].astype(jnp.bfloat16), "grp").astype(jnp.float32),
        lax.psum(shards[1].astype(jnp.bfloat16), "grp").astype(jnp.float32),
        lax.psum(shards[2].astype(jnp.bfloat16), "grp").astype(jnp.float32),
        lax.psum(shards[3].astype(jnp.bfloat16), "grp").astype(jnp.float32),
        lax.psum(shards[4].astype(jnp.bfloat16), "grp").astype(jnp.float32),
        lax.psum(shards[5].astype(jnp.bfloat16), "grp").astype(jnp.float32),
    )
    return (
        block_out,
        in_grad,
        skip_grad,
        summed[0],
        summed[1],
        summed[2],
        summed[3],
        summed[4],
        summed[5],
    )


ORDER = (0, 2, 1, 3)
BF16 = jnp.bfloat16
F32 = jnp.float32
ANY = pl.BlockSpec(memory_space=pl.ANY)
VMEM = pl.BlockSpec(memory_space=pltpu.VMEM)
SMEM = pl.BlockSpec(memory_space=pltpu.SMEM)


def swapped(axis, mask, size):
    return [(index, index ^ mask) for index in range(size)]


def from_seq(array, mask):
    return lax.ppermute(array, "seq", swapped("seq", mask, 8))


def from_grp(array, mask):
    return lax.ppermute(array, "grp", swapped("grp", mask, 4))


def run_copies(pairs, sems):
    copies = [pltpu.make_async_copy(src, dst, sems.at[i]) for i, (src, dst) in enumerate(pairs)]
    for copy in copies:
        copy.start()
    for copy in copies:
        copy.wait()


def call(kernel, out_shapes, in_specs, scratch, args, flops=0, vmem_mib=48):
    moved = sum(a.size * a.dtype.itemsize for a in args)
    moved += sum(o.size * o.dtype.itemsize for o in out_shapes)
    return pl.pallas_call(
        kernel,
        out_shape=tuple(out_shapes),
        in_specs=in_specs,
        out_specs=(VMEM,) * len(out_shapes),
        scratch_shapes=scratch,
        compiler_params=pltpu.CompilerParams(vmem_limit_bytes=vmem_mib * 1024 * 1024),
        cost_estimate=pl.CostEstimate(flops=flops, bytes_accessed=moved, transcendentals=0),
    )(*args)


def sds(shape, dtype):
    return jax.ShapeDtypeStruct(shape, dtype)


def aligned(index, size):
    return pl.ds(pl.multiple_of(index * size, size), size)


def nt(left, right):
    return lax.dot_general(left, right, (((1,), (1,)), ((), ())), preferred_element_type=F32)


def tn(left, right):
    return lax.dot_general(left, right, (((0,), (0,)), ((), ())), preferred_element_type=F32)


def nn(left, right):
    return jnp.dot(left, right, preferred_element_type=F32)


def slot_rows(ids, pieces, dst, rows, lanes=None):
    out = []
    for r, piece in enumerate(pieces):
        src = piece if lanes is None else piece.at[:, pl.ds(*lanes)]
        out.append((src, dst.at[aligned(ids[0] ^ r, rows), :]))
    return out


def h_zero_kernel(ids, *refs):
    inputs, weights = refs[:4], refs[4:12]
    out, held, wide, sems = refs[12:]
    tok = inputs[0].shape[0]
    pairs = [(x, held.at[pl.ds(f * tok, tok), :]) for f, x in enumerate(inputs)]
    run_copies(pairs + slot_rows(ids, weights, wide, weights[0].shape[0]), sems)
    out[...] = nn(held[...], wide[...]).astype(BF16)


def qkv_kernel(ids, *refs):
    pieces, scale, weights = refs[:4], refs[4], refs[5:13]
    normed_out, hidden_out, packed, held, wide, sems = refs[13:]
    tok = packed.shape[1]
    cols = pieces[0].shape[1]
    pairs = []
    for q in range(4):
        for f in range(4):
            pairs.append(
                (
                    pieces[q].at[pl.ds(ORDER[ORDER[f] ^ q] * tok, tok), :],
                    held.at[pl.ds(f * tok, tok), aligned(ids[1] ^ q, cols)],
                )
            )
    run_copies(pairs + slot_rows(ids, weights, wide, weights[0].shape[0]), sems)
    for f in range(4):
        rows = pl.ds(f * tok, tok)
        hidden = held[rows, :].astype(F32)
        inverse = lax.rsqrt(jnp.mean(hidden * hidden, axis=1, keepdims=True) + EPS)
        normed = (hidden * inverse * scale[rows, :]).astype(BF16)
        normed_out[rows, :] = normed
        if f < 2:
            hidden_out[rows, :] = held[rows, :]
        qkv = nn(normed, wide[...]).astype(BF16)
        group = ids[1] ^ ORDER[f]
        for pair in range(2):
            for part in range(3):
                packed[2 * group + pair, :, pl.ds(part * 128, 128)] = qkv[
                    :, (2 * part + pair) * 128 : (2 * part + pair + 1) * 128
                ]


def turn(vectors, cosine, sine):
    lane = lax.broadcasted_iota(jnp.int32, vectors.shape, 1)
    first = (lane & 63) < 32
    other = jnp.where(first, pltpu.roll(vectors, 96, 1), pltpu.roll(vectors, 32, 1))
    return vectors * cosine + other * sine


CHUNK = 256


def rotated(qkv, cosine, sine):
    total = qkv.shape[0] * qkv.shape[1]
    queries = qkv[:, :, 0:128].reshape(total, 128).astype(F32)
    keys = qkv[:, :, 128:256].reshape(total, 128).astype(F32)
    low_q = (turn(queries, cosine[...], sine[...])).astype(BF16) * jnp.asarray(0.125, BF16)
    low_k = turn(keys, cosine[...], sine[...]).astype(BF16)
    return low_q, low_k


def attend_kernel(qkv, cosine, sine, owner_col, owner_row, out, log_out):
    total = owner_col.shape[0]
    tok = qkv.shape[1]
    queries, keys = rotated(qkv, cosine, sine)
    values = qkv[:, :, 256:384].reshape(total, 128)
    for chunk in range(total // CHUNK):
        rows = slice(chunk * CHUNK, (chunk + 1) * CHUNK)
        same = owner_col[...] == owner_row[:, rows]
        both = []
        for head in range(2):
            lanes = slice(64 * head, 64 * head + 64)
            scores = jnp.where(same, nt(keys[:, lanes], queries[rows, lanes]), -1e30)
            top = jnp.max(scores, axis=0, keepdims=True)
            weights = jnp.exp(scores - top)
            total_w = jnp.sum(weights, axis=0, keepdims=True)
            log_out[head : head + 1, rows] = top + jnp.log(total_w)
            mixed = tn(values[:, lanes], weights.astype(BF16)) * (1.0 / total_w)
            both.append(mixed.T)
        joined = jnp.concatenate(both, axis=1).astype(BF16)
        for block in range(CHUNK // tok):
            out[chunk * (CHUNK // tok) + block] = joined[block * tok : (block + 1) * tok]


def attend_back_kernel(
    qkv, d_att, cosine, sine, owner_col, owner_row, log_total, out, d_keys, d_values
):
    total = owner_col.shape[0]
    tok = qkv.shape[1]
    queries, keys = rotated(qkv, cosine, sine)
    values = qkv[:, :, 256:384].reshape(total, 128)
    back = d_att[...].reshape(total, 128)
    keys_t = [keys[:, 64 * head : 64 * head + 64].astype(F32).T.astype(BF16) for head in range(2)]
    for chunk in range(total // CHUNK):
        rows = slice(chunk * CHUNK, (chunk + 1) * CHUNK)
        same = owner_col[...] == owner_row[:, rows]
        d_queries, k_terms, v_terms = [], [], []
        for head in range(2):
            lanes = slice(64 * head, 64 * head + 64)
            scores = nt(keys[:, lanes], queries[rows, lanes])
            probs = jnp.where(same, jnp.exp(scores - log_total[head : head + 1, rows]), 0.0)
            d_probs = nt(values[:, lanes], back[rows, lanes])
            delta = jnp.sum(probs * d_probs, axis=0, keepdims=True)
            d_scores = (probs * (d_probs - delta)).astype(BF16)
            v_terms.append(nn(probs.astype(BF16), back[rows, lanes]))
            k_terms.append(nn(d_scores, queries[rows, lanes]))
            d_queries.append(nn(keys_t[head], d_scores).T * 0.125)
        k_new = jnp.concatenate(k_terms, axis=1)
        v_new = jnp.concatenate(v_terms, axis=1)
        if chunk == 0:
            d_keys[...] = k_new
            d_values[...] = v_new
        else:
            d_keys[...] += k_new
            d_values[...] += v_new
        d_q = jnp.concatenate(d_queries, axis=1)
        d_q = turn(d_q, cosine[rows, :], -sine[rows, :]).astype(BF16)
        for block in range(CHUNK // tok):
            out[chunk * (CHUNK // tok) + block, :, 0:128] = d_q[block * tok : (block + 1) * tok]
    d_k = turn(d_keys[...], cosine[...], -sine[...]).astype(BF16)
    out[:, :, 128:256] = d_k.reshape(total // tok, tok, 128)
    out[:, :, 256:384] = d_values[...].astype(BF16).reshape(total // tok, tok, 128)


def attended_pairs(ids, blocks, dst, tok, parts):
    pairs = []
    for f in range(4):
        for pair in range(2):
            for part in range(parts):
                pairs.append(
                    (
                        blocks.at[2 * (ids[1] ^ ORDER[f]) + pair, :, pl.ds(part * 128, 128)],
                        dst.at[pl.ds(f * tok, tok), pl.ds((2 * part + pair) * 128, 128)],
                    )
                )
    return pairs


def out_rows(ids, weight, dst):
    return [
        (weight.at[aligned(ids[1], 128), :], dst.at[pl.ds(0, 128), :]),
        (weight.at[aligned(ids[1] + 4, 128), :], dst.at[pl.ds(128, 128), :]),
    ]


def project_kernel(ids, blocks, weight, keep, send, attended, wide, sems):
    tok = blocks.shape[1]
    run_copies(attended_pairs(ids, blocks, attended, tok, 1) + out_rows(ids, weight, wide), sems)
    keep[...] = nn(attended[0 : 2 * tok, :], wide[...])
    send[...] = nn(attended[2 * tok :, :], wide[...]).astype(BF16)


def residual_kernel(hidden, part, other, scale, h_one_out, normed_out):
    tok = hidden.shape[0] // 2
    for f in range(2):
        rows, swap = pl.ds(f * tok, tok), pl.ds((1 - f) * tok, tok)
        h_one = hidden[rows, :].astype(F32) + part[rows, :].astype(F32) + other[swap, :].astype(F32)
        inverse = lax.rsqrt(jnp.mean(h_one * h_one, axis=1, keepdims=True) + EPS)
        h_one_out[rows, :] = h_one
        normed_out[rows, :] = (h_one * inverse * scale[rows, :]).astype(BF16)


def gelu_parts(pre):
    half = 0.5 * (1.0 + lax.erf(pre * (2.0**-0.5)))
    slope = half + pre * jnp.exp(-0.5 * pre * pre) * ((2.0 * math.pi) ** -0.5)
    return pre * half, slope


def feed_kernel(ids, *refs):
    normed, normed_c, cot = refs[0], refs[1], refs[2:6]
    weights = refs[6:14]
    act_out, d_pre_out, keep, send, up, down, held, cots, sems = refs[14:]
    tok = cot[0].shape[0]
    rows = weights[0].shape[0]
    hidden = up.shape[1]
    pairs = [(normed, held.at[pl.ds(0, 2 * tok), :]), (normed_c, held.at[pl.ds(2 * tok, 2 * tok), :])]
    pairs += [(g, cots.at[pl.ds(f * tok, tok), :]) for f, g in enumerate(cot)]
    pairs += slot_rows(ids, weights, up, rows, (0, hidden))
    pairs += slot_rows(ids, weights, down, rows, (hidden, down.shape[1]))
    run_copies(pairs, sems)
    for f in range(4):
        block = pl.ds(f * tok, tok)
        pre = nn(held[block, :], up[...])
        act, slope = gelu_parts(pre)
        act_out[block, :] = act.astype(BF16)
        d_pre = (nt(cots[block, :], down[...]) * slope).astype(BF16)
        d_pre_out[block, :] = d_pre
        d_normed = nt(d_pre, up[...])
        if f < 2:
            keep[block, :] = d_normed
        else:
            send[pl.ds((f - 2) * tok, tok), :] = d_normed.astype(BF16)


def feed_grad_kernel(ids, normed, normed_c, c0, c1, c2, c3, act, d_pre, even, odd, held, cots, sems):
    tok = c0.shape[0]
    pairs = [(normed, held.at[pl.ds(0, 2 * tok), :]), (normed_c, held.at[pl.ds(2 * tok, 2 * tok), :])]
    pairs += [(g, cots.at[pl.ds(f * tok, tok), :]) for f, g in enumerate((c0, c1, c2, c3))]
    run_copies(pairs, sems)
    cols = act.shape[1]
    for r in range(8):
        block = aligned(ids[0] ^ r, 128)
        target = (even, odd)[r % 2]
        target[r // 2, :, 0:cols] = tn(held[:, block], d_pre[...]).astype(BF16)
        target[r // 2, :, cols:] = tn(act[:, block], cots[...]).astype(BF16)


def feed_out_kernel(ids, act, *refs):
    weights = refs[:8]
    keep, send, down, sems = refs[8:]
    half = keep.shape[0]
    width = down.shape[1]
    run_copies(slot_rows(ids, weights, down, weights[0].shape[0], (act.shape[1], width)), sems)
    keep[...] = nn(act[0:half, :], down[...])
    send[...] = nn(act[half:, :], down[...]).astype(BF16)


def norm_back(hidden, scale, d_normed):
    inverse = lax.rsqrt(jnp.mean(hidden * hidden, axis=1, keepdims=True) + EPS)
    y = hidden * inverse
    d_y = d_normed * scale
    d_hidden = inverse * (d_y - y * jnp.mean(d_y * y, axis=1, keepdims=True))
    return d_hidden, d_normed * y


def norm_back_kernel(hidden, scale, part, other, base, base_y, utt, low_out, sums_out):
    tok = hidden.shape[0] // 2
    for f in range(2):
        rows, swap = pl.ds(f * tok, tok), pl.ds((1 - f) * tok, tok)
        d_normed = part[rows, :].astype(F32) + other[swap, :].astype(F32)
        d_hidden, d_scale = norm_back(hidden[rows, :].astype(F32), scale[rows, :], d_normed)
        added = (base, base_y)[f][...].astype(F32) + d_hidden
        low_out[rows, :] = added.astype(low_out.dtype)
        if f == 0:
            sums_out[...] = nn(utt[...], d_scale.astype(BF16))


def d_attended_kernel(ids, d_h, d_h_c, weight, packed, wide, sems):
    tok = packed.shape[1]
    run_copies(out_rows(ids, weight, wide), sems)
    for f in range(4):
        rows = pl.ds((f % 2) * tok, tok)
        part = nt((d_h, d_h_c)[f // 2][rows, :], wide[...]).astype(BF16)
        group = ids[1] ^ ORDER[f]
        for pair in range(2):
            packed[2 * group + pair] = part[:, pair * 128 : (pair + 1) * 128]


def qkv_back_kernel(ids, blocks, *refs):
    weights = refs[:8]
    keep, send, joined, wide, sems = refs[8:]
    tok = blocks.shape[1]
    pairs = attended_pairs(ids, blocks, joined, tok, 3)
    run_copies(pairs + slot_rows(ids, weights, wide, weights[0].shape[0]), sems)
    half = keep.shape[0]
    keep[...] = nt(joined[0:half, :], wide[...])
    send[...] = nt(joined[half:, :], wide[...]).astype(BF16)


def qkv_grad_kernel(ids, normed, joined, d_h, d_h_c, a0, a1, a2, a3, even, odd, attended, sems):
    tok = a0.shape[0] // 4
    half = d_h.shape[0]
    pairs = []
    for q, piece in enumerate((a0, a1, a2, a3)):
        for f in range(4):
            for pair in range(2):
                pairs.append(
                    (
                        piece.at[pl.ds(ORDER[ORDER[f] ^ q] * tok, tok), pl.ds(pair * 128, 128)],
                        attended.at[pl.ds(f * tok, tok), aligned((ids[1] ^ q) + 4 * pair, 128)],
                    )
                )
    run_copies(pairs, sems)
    cols = joined.shape[1]
    mine = aligned(ids[1], 256)
    for r in range(8):
        block = aligned(ids[0] ^ r, 128)
        target = (even, odd)[r % 2]
        target[r // 2, :, 0:cols] = tn(normed[:, block], joined[...]).astype(BF16)
        target[r // 2, :, cols:] = (
            tn(attended[0:half, block], d_h[:, mine]) + tn(attended[half:, block], d_h_c[:, mine])
        ).astype(BF16)


def skip_back_kernel(ids, *refs):
    d_h, d_h_c, inputs, weights = refs[0], refs[1], refs[2:6], refs[6:14]
    even, odd, keep, send, held, wide, sems = refs[14:]
    tok = inputs[0].shape[0]
    pairs = [(x, held.at[pl.ds(f * tok, tok), :]) for f, x in enumerate(inputs)]
    run_copies(pairs + slot_rows(ids, weights, wide, weights[0].shape[0]), sems)
    mine = aligned(ids[1], 256)
    near, far = d_h[:, mine], d_h_c[:, mine]
    half = 2 * tok
    for r in range(8):
        block = aligned(ids[0] ^ r, 256)
        target = (even, odd)[r % 2]
        target[r // 2] = (tn(held[0:half, block], near) + tn(held[half:, block], far)).astype(BF16)
    keep[...] = nt(near, wide[...])
    send[...] = nt(far, wide[...]).astype(BF16)


def spread_kernel(ids, *refs):
    qkv_o, out_o, up_o, down_o, skip_o = refs[12:]
    for q in range(4):
        part = ids[1] ^ q
        qkv_out, feed, skip = refs[q], refs[4 + q], refs[8 + q]
        for block in range(6):
            qkv_o[:, aligned(4 * block + part, 128)] = qkv_out[:, pl.ds(block * 128, 128)].astype(F32)
        out_o[:, aligned(part, 256)] = qkv_out[:, pl.ds(768, 256)].astype(F32)
        for block in range(8):
            up_o[:, aligned(4 * block + part, 128)] = feed[:, pl.ds(block * 128, 128)].astype(F32)
        down_o[aligned(part, 128), :] = feed[:, pl.ds(1024, 1024)].astype(F32)
        skip_o[:, aligned(part, 256)] = skip[...].astype(F32)


def gather_slots(piece):
    near = [piece] + [from_seq(piece, 2 * k) for k in range(1, 4)]
    out = []
    for array in near:
        out += [array, from_seq(array, 1)]
    return out


def gather_groups(piece):
    along_y = from_grp(piece, 2)
    return [piece, along_y, from_grp(piece, 1), from_grp(along_y, 1)]


def scatter_slots(even, odd):
    arrived = from_seq(odd, 1)
    parts = [
        (even[k].astype(F32) + arrived[k].astype(F32)).astype(BF16) for k in range(4)
    ]
    total = parts[0].astype(F32)
    for k in range(1, 4):
        total = total + from_seq(parts[k], 2 * k).astype(F32)
    return total.astype(BF16)


def halves_sum(keep, send):
    return (keep + from_grp(send, 1).astype(F32)).astype(BF16)


def exchange(array, cols):
    return lax.all_to_all(array, "seq", 0, 0, tiled=True)


def tp_body(
    hidden_in, skips, lengths, times, skip_weight, cond_weight, qkv_weight, out_weight,
    up_weight, down_weight, cotangent,
):
    tok, width = hidden_in.shape
    ff = up_weight.shape[1]
    frames = 8 * tok
    slot = lax.axis_index("seq")
    part = lax.axis_index("grp")
    ids = jnp.stack([slot, part]).astype(jnp.int32)
    sem = pltpu.SemaphoreType.DMA

    def columns(weight, blocks, size):
        rows = weight.shape[0]
        split = weight.reshape(rows, blocks, 4, size)
        return lax.dynamic_index_in_dim(split, part, 2, keepdims=False).reshape(rows, blocks * size)

    w_skip = gather_slots(columns(skip_weight, 1, 256))
    inputs_own = jnp.concatenate([hidden_in, skips], axis=1)
    x_y = from_grp(inputs_own, 2)
    inputs = [inputs_own, x_y, from_grp(inputs_own, 1), from_grp(x_y, 1)]

    half_width = width // 2
    freqs = jnp.exp(-math.log(10000.0) * jnp.arange(half_width, dtype=F32) / half_width)
    angles = times[0].astype(F32)[:, None] * freqs[None, :]
    emb = jnp.concatenate([jnp.sin(angles), jnp.cos(angles)], axis=1).astype(BF16)
    rows_here = cond_weight.shape[0]
    emb_here = lax.dynamic_slice_in_dim(emb, slot * rows_here, rows_here, 1)
    utts = emb.shape[0]
    cond_part = matmul(emb_here, cond_weight)
    note = jnp.zeros((1, 2 * width), F32).at[0, :utts].set(lengths[0].astype(F32))
    told = lax.all_gather(jnp.concatenate([cond_part, note], axis=0), ("grp", "seq"), axis=0)
    told = told.reshape(4, 8, utts + 1, 2 * width)
    cond_all = jnp.sum(told[:, :, :utts], axis=1)
    lengths_all = told[:, 0, utts, :utts].astype(jnp.int32)
    ends_all = jnp.cumsum(lengths_all, axis=1)

    frame_here = slot * tok + jnp.arange(tok, dtype=jnp.int32)

    def scale_rows(f, cond_cols):
        group = part ^ ORDER[f]
        ends = lax.dynamic_index_in_dim(ends_all, group, 0, keepdims=False)
        owner = owner_of(frame_here, ends)
        rows = lax.dynamic_index_in_dim(cond_all, group, 0, keepdims=False)[:, cond_cols]
        onehot = owner[:, None] == jnp.arange(utts, dtype=jnp.int32)[None, :]
        picked = 1.0 + jnp.dot(onehot.astype(F32), rows, precision=lax.Precision.HIGHEST)
        return picked, onehot

    attn_cols, ffn_cols = slice(0, width), slice(width, 2 * width)
    scaled = [scale_rows(f, attn_cols) for f in range(4)]
    scale_attn = jnp.concatenate([pair[0] for pair in scaled], axis=0)
    scale_ffn = jnp.concatenate([scale_rows(f, ffn_cols)[0] for f in range(2)], axis=0)
    utt_rows = scaled[0][1].astype(BF16).T

    my_ends = lax.dynamic_index_in_dim(ends_all, slot // 2, 0, keepdims=False)
    my_lengths = lax.dynamic_index_in_dim(lengths_all, slot // 2, 0, keepdims=False)
    all_frames = jnp.arange(frames, dtype=jnp.int32)
    owner_all = owner_of(all_frames, my_ends)
    own_hot = owner_all[:, None] == jnp.arange(utts, dtype=jnp.int32)[None, :]
    begins = jnp.sum(jnp.where(own_hot, (my_ends - my_lengths)[None, :], 0), axis=1)
    positions = (all_frames - begins).astype(F32)
    inverse = jnp.exp(-math.log(10000.0) * jnp.arange(32, dtype=F32) / 32)
    turn_angles = positions[:, None] * inverse[None, :]
    cos_half, sin_half = jnp.cos(turn_angles), jnp.sin(turn_angles)
    cosine = jnp.concatenate([cos_half] * 4, axis=1)
    sine = jnp.concatenate([-sin_half, sin_half] * 2, axis=1)
    owner_col, owner_row = owner_all[:, None], owner_all[None, :]

    w_qkv = gather_slots(columns(qkv_weight, 6, 128))
    out_rows_all = lax.all_gather(out_weight, "seq", axis=0, tiled=True)
    w_feed = gather_slots(
        jnp.concatenate(
            [columns(up_weight, 8, 128), lax.dynamic_slice_in_dim(down_weight, part * 128, 128, 0)],
            axis=1,
        )
    )
    cots = gather_groups(cotangent)

    (h_cols,) = call(
        h_zero_kernel,
        [sds((4 * tok, 256), BF16)],
        [SMEM] + [ANY] * 12,
        [pltpu.VMEM((4 * tok, 2 * width), BF16), pltpu.VMEM((2 * width, 256), BF16), sem((12,))],
        [ids] + inputs + w_skip,
        flops=2 * 4 * tok * 2 * width * 256,
    )
    h_pieces = gather_groups(h_cols)
    h_pieces = [h_pieces[0], h_pieces[2], h_pieces[1], h_pieces[3]]
    normed, h_zero, packed = call(
        qkv_kernel,
        [sds((4 * tok, width), BF16), sds((2 * tok, width), BF16), sds((8, tok, 384), BF16)],
        [SMEM] + [ANY] * 4 + [VMEM] + [ANY] * 8,
        [pltpu.VMEM((4 * tok, width), BF16), pltpu.VMEM((width, 768), BF16), sem((24,))],
        [ids] + h_pieces + [scale_attn] + w_qkv,
        flops=2 * 4 * tok * width * 768,
    )
    qkv = exchange(packed, 384)
    mixed, log_total = call(
        attend_kernel,
        [sds((8, tok, 128), BF16), sds((2, frames), F32)],
        [VMEM] * 5,
        [],
        [qkv, cosine, sine, owner_col, owner_row],
        flops=2 * 2 * 2 * frames * frames * 64 * 2,
    )
    attended_blocks = exchange(mixed, 128)
    keep, send, attended = call(
        project_kernel,
        [sds((2 * tok, width), F32), sds((2 * tok, width), BF16), sds((4 * tok, 256), BF16)],
        [SMEM, ANY, ANY],
        [pltpu.VMEM((256, width), BF16), sem((10,))],
        [ids, attended_blocks, out_rows_all],
        flops=2 * 4 * tok * width * 256,
    )
    h_part = halves_sum(keep, send)
    h_one, normed_two = call(
        residual_kernel,
        [sds((2 * tok, width), F32), sds((2 * tok, width), BF16)],
        [VMEM] * 4,
        [],
        [h_zero, h_part, from_grp(h_part, 2), scale_ffn],
    )
    normed_two_c = from_grp(normed_two, 1)
    quarter = ff // 4
    feed_scratch = [
        pltpu.VMEM((width, quarter), BF16),
        pltpu.VMEM((quarter, width), BF16),
        pltpu.VMEM((4 * tok, width), BF16),
        pltpu.VMEM((4 * tok, width), BF16),
        sem((22,)),
    ]
    act, d_pre, keep, send = call(
        feed_kernel,
        [
            sds((4 * tok, quarter), BF16),
            sds((4 * tok, quarter), BF16),
            sds((2 * tok, width), F32),
            sds((2 * tok, width), BF16),
        ],
        [SMEM] + [ANY] * 14,
        feed_scratch,
        [ids, normed_two, normed_two_c] + cots + w_feed,
        flops=3 * 2 * 4 * tok * width * quarter,
    )

    d_part = halves_sum(keep, send)
    d_h_one, sums_ffn = call(
        norm_back_kernel,
        [sds((2 * tok, width), BF16), sds((utts, width), F32)],
        [VMEM] * 7,
        [],
        [h_one, scale_ffn, d_part, from_grp(d_part, 2), cots[0], cots[1], utt_rows],
    )
    d_h_one_c = from_grp(d_h_one, 1)
    (d_att_packed,) = call(
        d_attended_kernel,
        [sds((8, tok, 128), BF16)],
        [SMEM, VMEM, VMEM, ANY],
        [pltpu.VMEM((256, width), BF16), sem((2,))],
        [ids, d_h_one, d_h_one_c, out_rows_all],
        flops=2 * 4 * tok * width * 256,
    )
    d_att = exchange(d_att_packed, 128)

    out_keep, out_send = call(
        feed_out_kernel,
        [sds((2 * tok, width), F32), sds((2 * tok, width), BF16)],
        [SMEM, VMEM] + [ANY] * 8,
        [pltpu.VMEM((quarter, width), BF16), sem((8,))],
        [ids, act] + w_feed,
        flops=2 * 4 * tok * width * quarter,
    )
    out_part = halves_sum(out_keep, out_send)
    block_out = (
        h_one[:tok] + out_part[:tok].astype(F32) + from_grp(out_part[tok:], 2).astype(F32)
    ).astype(BF16)
    feed_even, feed_odd = call(
        feed_grad_kernel,
        [sds((4, 128, 2 * width), BF16)] * 2,
        [SMEM] + [ANY] * 6 + [VMEM] * 2,
        feed_scratch[2:4] + [sem((6,))],
        [ids, normed_two, normed_two_c] + cots + [act, d_pre],
        flops=2 * 2 * 4 * tok * width * quarter,
    )
    feed_grads = gather_groups(scatter_slots(feed_even, feed_odd))
    att_pieces = gather_groups(attended)

    (d_packed,) = call(
        attend_back_kernel,
        [sds((8, tok, 384), BF16)],
        [VMEM] * 7,
        [pltpu.VMEM((frames, 128), F32), pltpu.VMEM((frames, 128), F32)],
        [qkv, d_att, cosine, sine, owner_col, owner_row, log_total],
        flops=5 * 2 * 2 * frames * frames * 64 * 2,
    )
    d_qkv_blocks = exchange(d_packed, 384)
    keep, send, d_qkv = call(
        qkv_back_kernel,
        [sds((2 * tok, width), F32), sds((2 * tok, width), BF16), sds((4 * tok, 768), BF16)],
        [SMEM] + [ANY] * 9,
        [pltpu.VMEM((width, 768), BF16), sem((32,))],
        [ids, d_qkv_blocks] + w_qkv,
        flops=2 * 4 * tok * width * 768,
    )
    d_part = halves_sum(keep, send)
    d_h_zero, sums_attn = call(
        norm_back_kernel,
        [sds((2 * tok, width), BF16), sds((utts, width), F32)],
        [VMEM] * 7,
        [],
        [h_zero, scale_attn[: 2 * tok], d_part, from_grp(d_part, 2), d_h_one[:tok], d_h_one[tok:], utt_rows],
    )
    qkv_even, qkv_odd = call(
        qkv_grad_kernel,
        [sds((4, 128, 1024), BF16)] * 2,
        [SMEM] + [VMEM] * 4 + [ANY] * 4,
        [pltpu.VMEM((4 * tok, width), BF16), sem((32,))],
        [ids, normed, d_qkv, d_h_one, d_h_one_c, att_pieces[0], att_pieces[2], att_pieces[1], att_pieces[3]],
        flops=2 * 4 * tok * width * 1024,
    )
    d_h_zero_c = from_grp(d_h_zero, 1)
    skip_even, skip_odd, in_keep, in_send = call(
        skip_back_kernel,
        [sds((4, 256, 256), BF16)] * 2 + [sds((2 * tok, 2 * width), F32), sds((2 * tok, 2 * width), BF16)],
        [SMEM, VMEM, VMEM] + [ANY] * 12,
        [pltpu.VMEM((4 * tok, 2 * width), BF16), pltpu.VMEM((2 * width, 256), BF16), sem((12,))],
        [ids, d_h_zero, d_h_zero_c] + inputs + w_skip,
        flops=2 * 2 * 4 * tok * 2 * width * 256,
    )
    skip_grads = gather_groups(scatter_slots(skip_even, skip_odd))
    qkv_grads = gather_groups(scatter_slots(qkv_even, qkv_odd))
    in_part = halves_sum(in_keep, in_send)
    in_both = (in_part[:tok].astype(F32) + from_grp(in_part[tok:], 2).astype(F32)).astype(BF16)

    emb_sums = jnp.concatenate([sums_attn, sums_ffn], axis=1)
    sums_all = lax.all_gather(emb_sums, ("grp", "seq"), axis=0).reshape(4, 8, utts, 2 * width)
    sums_all = jnp.sum(sums_all, axis=1)
    emb_all = lax.all_gather(emb_here, "grp", axis=0)
    cond_grad = contract(
        emb_all.reshape(4 * utts, rows_here), sums_all.reshape(4 * utts, 2 * width).astype(BF16), 0, 0
    )

    def by_mask(pieces):
        return [pieces[0], pieces[2], pieces[1], pieces[3]]

    qkv_grad, out_grad, up_grad, down_grad, skip_grad_w = call(
        spread_kernel,
        [
            sds((128, 3 * width), F32),
            sds((128, width), F32),
            sds((128, ff), F32),
            sds((ff // 8, width), F32),
            sds((256, width), F32),
        ],
        [SMEM] + [VMEM] * 12,
        [],
        [ids] + by_mask(qkv_grads) + by_mask(feed_grads) + by_mask(skip_grads),
    )
    return (
        block_out, in_both[:, :width], in_both[:, width:], skip_grad_w, cond_grad, qkv_grad,
        out_grad, up_grad, down_grad,
    )


def solution(mesh):
    placed = (
        P(("grp", "seq"), None),
        P(("grp", "seq"), None),
        P("grp", None),
        P("grp", None),
        P("seq", None),
        P("seq", None),
        P("seq", None),
        P("seq", None),
        P("seq", None),
        P("seq", None),
        P(("grp", "seq"), None),
    )
    body = tp_body if (mesh.shape["grp"], mesh.shape["seq"]) == (4, 8) else plain_body
    return jax.shard_map(
        body,
        mesh=mesh,
        in_specs=placed,
        out_specs=(
            P(("grp", "seq"), None),
            P(("grp", "seq"), None),
            P(("grp", "seq"), None),
            P("seq", None),
            P("seq", None),
            P("seq", None),
            P("seq", None),
            P("seq", None),
            P("seq", None),
        ),
        check_vma=False,
    )
```

```python
import functools
import math

import jax
import jax.numpy as jnp
from jax import lax
from jax.experimental import pallas as pl
from jax.experimental.pallas import tpu as pltpu
from jax.sharding import PartitionSpec as P

HEADS = 16


EPS = 1e-06


def contract(left, right, left_dim, right_dim):
    return lax.dot_general(
        left, right, (((left_dim,), (right_dim,)), ((), ())), preferred_element_type=jnp.float32
    )


def matmul(left, right):
    return jnp.dot(left, right, preferred_element_type=jnp.float32)


def owner_of(frames, utt_ends):
    return jnp.sum((frames[:, None] >= utt_ends[None, :]).astype(jnp.int32), axis=1)


def same_owner(query_owner, key_owner):
    return (query_owner[:, None] == key_owner[None, :])[:, None, :]


def embed_steps(time_steps, model_width):
    half_width = model_width // 2
    freqs = jnp.exp(-math.log(10000.0) * jnp.arange(half_width, dtype=jnp.float32) / half_width)
    angles = time_steps[:, None] * freqs[None, :]
    return jnp.concatenate([jnp.sin(angles), jnp.cos(angles)], axis=1)


def rotate(vectors, positions, head_count, direction):
    tok_rows, model_width = vectors.shape
    head_size = model_width // head_count
    half_size = head_size // 2
    inverse = jnp.exp(-math.log(10000.0) * jnp.arange(half_size, dtype=jnp.float32) / half_size)
    angles = positions[:, None] * inverse[None, :]
    cosine = jnp.cos(angles)[:, None, :]
    sine = direction * jnp.sin(angles)[:, None, :]
    split = vectors.reshape(tok_rows, head_count, head_size)
    first_half = split[..., :half_size]
    second_half = split[..., half_size:]
    turned = jnp.concatenate(
        [first_half * cosine - second_half * sine, first_half * sine + second_half * cosine],
        axis=-1,
    )
    return turned.reshape(tok_rows, model_width)


def scale_norm(hidden, cond_part):
    return (
        hidden
        * lax.rsqrt(jnp.mean(hidden * hidden, axis=1, keepdims=True) + EPS)
        * (1.0 + cond_part)
    )


def over_blocks(update, running, arrays, first_row, block_cap):
    row_count = arrays[0].shape[0]
    block_size = math.gcd(row_count, block_cap)
    number = row_count // block_size
    if number == 1:
        return update(running, arrays, first_row)
    stacked = tuple((array.reshape((number, block_size) + array.shape[1:]) for array in arrays))
    offsets = first_row + block_size * jnp.arange(number, dtype=jnp.int32)

    def over_scan_step(inner, scan_in):
        return (update(inner, scan_in[0], scan_in[1]), None)

    result, unused = lax.scan(over_scan_step, running, (stacked, offsets))
    return result


def grad_terms(
    q_heads, do_heads, log_total, row_delta, key_heads, value_heads, same_utt, score_scale
):
    scores = (
        jnp.einsum("qhd,khd->qhk", q_heads, key_heads, preferred_element_type=jnp.float32)
        * score_scale
    )
    probs = jnp.where(same_utt, jnp.exp(scores - log_total[..., None]), 0.0)
    d_probs = jnp.einsum("qhd,khd->qhk", do_heads, value_heads, preferred_element_type=jnp.float32)
    d_scores = (probs * (d_probs - row_delta[..., None]) * score_scale).astype(jnp.bfloat16)
    return (probs.astype(jnp.bfloat16), d_scores)


def scatter_first(after, grad):
    return lax.optimization_barrier(
        (after, lax.psum_scatter(grad, "seq", scatter_dimension=0, tiled=True))
    )


def plain_body(
    hidden_in,
    skips,
    lengths,
    times,
    skip_weight,
    cond_weight,
    qkv_weight,
    out_weight,
    up_weight,
    down_weight,
    cotangent,
):
    tok_rows, model_width = hidden_in.shape
    head_count = HEADS
    head_size = model_width // head_count
    score_scale = head_size ** (-0.5)
    first_frame = lax.axis_index("seq") * tok_rows
    utt_lengths = lengths[0]
    utt_ends = jnp.cumsum(utt_lengths)
    starts = utt_ends - utt_lengths
    frames = first_frame + jnp.arange(tok_rows, dtype=jnp.int32)
    query_owner = owner_of(frames, utt_ends)
    onehot = query_owner[:, None] == jnp.arange(utt_lengths.shape[0], dtype=jnp.int32)[None, :]
    positions = (frames - jnp.sum(jnp.where(onehot, starts[None, :], 0), axis=1)).astype(
        jnp.float32
    )
    time_steps = jnp.sum(jnp.where(onehot, times[0][None, :], 0), axis=1).astype(jnp.float32)
    gathered = (
        lax.all_gather(skip_weight, "seq", axis=0, tiled=True),
        lax.all_gather(cond_weight, "seq", axis=0, tiled=True),
        lax.all_gather(qkv_weight, "seq", axis=0, tiled=True),
        lax.all_gather(out_weight, "seq", axis=0, tiled=True),
        lax.all_gather(up_weight, "seq", axis=0, tiled=True),
        lax.all_gather(down_weight, "seq", axis=0, tiled=True),
    )
    w_skip, w_cond, w_qkv, w_out, w_up, w_down = gathered
    h_zero = matmul(hidden_in, w_skip[:model_width]) + matmul(skips, w_skip[model_width:])
    emb = embed_steps(time_steps, model_width).astype(jnp.bfloat16)
    cond = matmul(emb, w_cond)
    cond_attn = cond[:, :model_width]
    cond_ffn = cond[:, model_width:]
    normed = scale_norm(h_zero, cond_attn).astype(jnp.bfloat16)
    qkv = matmul(normed, w_qkv)
    queries = rotate(qkv[:, :model_width], positions, head_count, 1.0).astype(jnp.bfloat16)
    keys = rotate(qkv[:, model_width : 2 * model_width], positions, head_count, 1.0).astype(
        jnp.bfloat16
    )
    values = qkv[:, 2 * model_width :].astype(jnp.bfloat16)
    q_heads = queries.reshape(tok_rows, head_count, head_size)

    def forward_step(running, blocks, first_row):
        weighted, run_max, run_sum = running
        key_heads = blocks[0].reshape(-1, head_count, head_size)
        value_heads = blocks[1].reshape(-1, head_count, head_size)
        key_owner = owner_of(first_row + jnp.arange(key_heads.shape[0], dtype=jnp.int32), utt_ends)
        same_utt = same_owner(query_owner, key_owner)
        scores = (
            jnp.einsum("qhd,khd->qhk", q_heads, key_heads, preferred_element_type=jnp.float32)
            * score_scale
        )
        new_max = jnp.maximum(run_max, jnp.max(jnp.where(same_utt, scores, -1e30), axis=-1))
        weights_b = jnp.where(same_utt, jnp.exp(scores - new_max[..., None]), 0.0)
        factor = jnp.exp(run_max - new_max)
        run_sum = run_sum * factor + jnp.sum(weights_b, axis=-1)
        weighted = weighted * factor[..., None] + jnp.einsum(
            "qhk,khd->qhd",
            weights_b.astype(jnp.bfloat16),
            value_heads,
            preferred_element_type=jnp.float32,
        )
        return (weighted, new_max, run_sum)

    start_state = (
        jnp.zeros((tok_rows, head_count, head_size), jnp.float32),
        jnp.full((tok_rows, head_count), -1e30, jnp.float32),
        jnp.zeros((tok_rows, head_count), jnp.float32),
    )
    weighted, run_max, run_sum = over_blocks(
        forward_step,
        start_state,
        (
            lax.all_gather(keys, "seq", axis=0, tiled=True),
            lax.all_gather(values, "seq", axis=0, tiled=True),
        ),
        jnp.int32(0),
        1024,
    )
    attended_full = (weighted / run_sum[..., None]).reshape(tok_rows, model_width)
    log_total = run_max + jnp.log(run_sum)
    attended = attended_full.astype(jnp.bfloat16)
    h_one = h_zero + matmul(attended, w_out)
    normed_two = scale_norm(h_one, cond_ffn).astype(jnp.bfloat16)
    pre = matmul(normed_two, w_up)
    act = jax.nn.gelu(pre, approximate=False).astype(jnp.bfloat16)
    block_out = (h_one + matmul(act, w_down)).astype(jnp.bfloat16)
    regathered = (
        lax.all_gather(skip_weight, "seq", axis=0, tiled=True),
        lax.all_gather(cond_weight, "seq", axis=0, tiled=True),
        lax.all_gather(qkv_weight, "seq", axis=0, tiled=True),
        lax.all_gather(out_weight, "seq", axis=0, tiled=True),
        lax.all_gather(up_weight, "seq", axis=0, tiled=True),
        lax.all_gather(down_weight, "seq", axis=0, tiled=True),
    )
    w_skip, w_cond, w_qkv, w_out, w_up, w_down = regathered
    d_act = contract(cotangent, w_down, 1, 1)
    d_act, shard_down = scatter_first(d_act, contract(act, cotangent, 0, 0))
    unused, gelu_back = jax.vjp(lambda inner: jax.nn.gelu(inner, approximate=False), pre)
    d_pre = gelu_back(d_act)[0].astype(jnp.bfloat16)
    d_pre, shard_up = scatter_first(d_pre, contract(normed_two, d_pre, 0, 0))
    d_normed_two = contract(d_pre, w_up, 1, 1)
    unused, norm_back_two = jax.vjp(scale_norm, h_one, cond_ffn)
    d_h_norm, d_cond_ffn = norm_back_two(d_normed_two)
    d_h_one = cotangent.astype(jnp.float32) + d_h_norm
    d_h_low = d_h_one.astype(jnp.bfloat16)
    d_h_low, shard_out = scatter_first(d_h_low, contract(attended, d_h_low, 0, 0))
    d_attended = contract(d_h_low, w_out, 1, 1).astype(jnp.bfloat16)
    row_delta = jnp.sum(
        (d_attended.astype(jnp.float32) * attended_full).reshape(tok_rows, head_count, head_size),
        axis=-1,
    )
    do_heads = d_attended.reshape(tok_rows, head_count, head_size)
    keys_all, values_all = (
        lax.all_gather(keys, "seq", axis=0, tiled=True),
        lax.all_gather(values, "seq", axis=0, tiled=True),
    )
    key_total = keys_all.shape[0]
    block_size = math.gcd(key_total, 1024)
    number = key_total // block_size

    def body_scan_step(d_query, scan_in):
        key_block, value_block, offset = scan_in
        key_heads = key_block.reshape(block_size, head_count, head_size)
        value_heads = value_block.reshape(block_size, head_count, head_size)
        key_owner = owner_of(offset + jnp.arange(block_size, dtype=jnp.int32), utt_ends)
        probs_low, d_scores = grad_terms(
            q_heads,
            do_heads,
            log_total,
            row_delta,
            key_heads,
            value_heads,
            same_owner(query_owner, key_owner),
            score_scale,
        )
        d_query = d_query + jnp.einsum(
            "qhk,khd->qhd", d_scores, key_heads, preferred_element_type=jnp.float32
        )
        d_key = jnp.einsum(
            "qhk,qhd->khd", d_scores, q_heads, preferred_element_type=jnp.float32
        ).reshape(block_size, model_width)
        d_value = jnp.einsum(
            "qhk,qhd->khd", probs_low, do_heads, preferred_element_type=jnp.float32
        ).reshape(block_size, model_width)
        return (d_query, (d_key, d_value))

    d_query, terms = lax.scan(
        body_scan_step,
        jnp.zeros((tok_rows, head_count, head_size), jnp.float32),
        (
            keys_all.reshape(number, block_size, model_width),
            values_all.reshape(number, block_size, model_width),
            block_size * jnp.arange(number, dtype=jnp.int32),
        ),
    )
    value_terms, d_key = scatter_first(terms[1], terms[0].reshape(key_total, model_width))
    d_value = lax.psum_scatter(
        value_terms.reshape(key_total, model_width), "seq", scatter_dimension=0, tiled=True
    )
    d_qkv = jnp.concatenate(
        [
            rotate(d_query.reshape(tok_rows, model_width), positions, head_count, -1.0),
            rotate(d_key, positions, head_count, -1.0),
            d_value,
        ],
        axis=1,
    ).astype(jnp.bfloat16)
    d_qkv, shard_qkv = scatter_first(d_qkv, contract(normed, d_qkv, 0, 0))
    d_normed = contract(d_qkv, w_qkv, 1, 1)
    unused, norm_back_one = jax.vjp(scale_norm, h_zero, cond_attn)
    d_h_first, d_cond_attn = norm_back_one(d_normed)
    d_h_zero = (d_h_one + d_h_first).astype(jnp.bfloat16)
    d_cond = jnp.concatenate([d_cond_attn, d_cond_ffn], axis=1).astype(jnp.bfloat16)
    d_cond, shard_cond = scatter_first(d_cond, contract(emb, d_cond, 0, 0))
    grad_skip_w = jnp.concatenate(
        [contract(hidden_in, d_h_zero, 0, 0), contract(skips, d_h_zero, 0, 0)], axis=0
    )
    in_grad = contract(d_h_zero, w_skip[:model_width], 1, 1).astype(jnp.bfloat16)
    skip_grad = contract(d_h_zero, w_skip[model_width:], 1, 1).astype(jnp.bfloat16)
    shards = (
        lax.psum_scatter(grad_skip_w, "seq", scatter_dimension=0, tiled=True),
        shard_cond,
        shard_qkv,
        shard_out,
        shard_up,
        shard_down,
    )
    summed = (
        lax.psum(shards[0].astype(jnp.bfloat16), "grp").astype(jnp.float32),
        lax.psum(shards[1].astype(jnp.bfloat16), "grp").astype(jnp.float32),
        lax.psum(shards[2].astype(jnp.bfloat16), "grp").astype(jnp.float32),
        lax.psum(shards[3].astype(jnp.bfloat16), "grp").astype(jnp.float32),
        lax.psum(shards[4].astype(jnp.bfloat16), "grp").astype(jnp.float32),
        lax.psum(shards[5].astype(jnp.bfloat16), "grp").astype(jnp.float32),
    )
    return (
        block_out,
        in_grad,
        skip_grad,
        summed[0],
        summed[1],
        summed[2],
        summed[3],
        summed[4],
        summed[5],
    )


ORDER = (0, 2, 1, 3)
BF16 = jnp.bfloat16
VMEM_MIB = 63
F32 = jnp.float32
ANY = pl.BlockSpec(memory_space=pl.ANY)
VMEM = pl.BlockSpec(memory_space=pltpu.VMEM)
HBM = pl.BlockSpec(memory_space=pltpu.HBM)
SMEM = pl.BlockSpec(memory_space=pltpu.SMEM)


def swapped(axis, mask, size):
    return [(index, index ^ mask) for index in range(size)]


def from_seq(array, mask):
    return lax.ppermute(array, "seq", swapped("seq", mask, 8))


def from_grp(array, mask):
    return lax.ppermute(array, "grp", swapped("grp", mask, 4))


def run_copies(pairs, sems):
    copies = [pltpu.make_async_copy(src, dst, sems.at[i]) for i, (src, dst) in enumerate(pairs)]
    for copy in copies:
        copy.start()
    for copy in copies:
        copy.wait()


def call(kernel, out_shapes, in_specs, scratch, args, deps=(), out_spec=VMEM, cost_us=0.0):
    moved = sum(a.size * a.dtype.itemsize for a in args)
    moved += sum(o.size * o.dtype.itemsize for o in out_shapes)
    given, extra = len(args), len(deps)

    def with_deps(*refs):
        kernel(*refs[:given], *refs[given + extra :])

    return pl.pallas_call(
        with_deps,
        out_shape=tuple(out_shapes),
        in_specs=list(in_specs) + [ANY] * extra,
        out_specs=(out_spec,) * len(out_shapes),
        scratch_shapes=scratch,
        compiler_params=pltpu.CompilerParams(vmem_limit_bytes=VMEM_MIB * 1024 * 1024),
        cost_estimate=pl.CostEstimate(
            flops=int(cost_us * 1.15e9), bytes_accessed=0, transcendentals=0
        ),
    )(*args, *deps)


def sds(shape, dtype):
    return jax.ShapeDtypeStruct(shape, dtype)


def aligned(index, size):
    return pl.ds(pl.multiple_of(index * size, size), size)


def nt(left, right):
    return lax.dot_general(left, right, (((1,), (1,)), ((), ())), preferred_element_type=F32)


def tn(left, right):
    return lax.dot_general(left, right, (((0,), (0,)), ((), ())), preferred_element_type=F32)


def nn(left, right):
    return jnp.dot(left, right, preferred_element_type=F32)


def frame_blocks(ids, blocks, dst):
    tok = blocks.shape[1]
    return [(blocks.at[ids[1] ^ ORDER[f]], dst.at[pl.ds(f * tok, tok), :]) for f in range(4)]


def h_zero_kernel(ids, inputs, near, far, notes, out, whole, held, wide, shares, sems):
    rows = wide.shape[0] // 8
    frames = held.shape[0]
    pairs = frame_blocks(ids, inputs, held)
    for r in range(8):
        piece = (near, far)[r % 2].at[pl.ds((r // 2) * rows, rows), :]
        pairs.append((piece, wide.at[aligned(ids[0] ^ r, rows), :]))
    for k, pieces in enumerate((near, far)):
        pairs.append((pieces.at[pl.ds(4 * rows, 64), :], shares.at[k]))
    run_copies(pairs, sems)
    out[0:frames, :] = nn(held[...], wide[...]).astype(BF16)
    out[frames : frames + 64, :] = (shares[0].astype(F32) + shares[1].astype(F32)).astype(BF16)
    out[frames + 64 :, :] = notes[...]
    whole[...] = wide[...]


def qkv_kernel(ids, *refs):
    pieces, weight = refs[:4], refs[4]
    normed_out, hidden_out, packed, told, held, raw, sems = refs[5:]
    tok = packed.shape[1]
    cols = pieces[0].shape[1]
    pairs = [(pieces[ORDER[f]].at[pl.ds(4 * tok, 80), :], raw.at[f]) for f in range(4)]
    for q in range(4):
        for f in range(4):
            pairs.append(
                (
                    pieces[q].at[pl.ds(ORDER[ORDER[f] ^ q] * tok, tok), :],
                    held.at[pl.ds(f * tok, tok), aligned(ids[1] ^ q, cols)],
                )
            )
    run_copies(pairs, sems)
    for f in range(4):
        rows = raw[f].astype(F32)
        told[f, 0:8, :] = unpacked_rows(rows[0:64])
        counts = jnp.concatenate(
            [32.0 * rows[64:65] + rows[65:66], 32.0 * rows[66:67] + rows[67:68], jnp.zeros((6, cols), F32)], axis=0
        )
        told[f, 8:16, :] = jnp.concatenate([counts, jnp.zeros((8, told.shape[2] - cols), F32)], axis=1)
    for f in range(4):
        rows = pl.ds(f * tok, tok)
        hidden = held[rows, :].astype(F32)
        inverse = lax.rsqrt(jnp.mean(hidden * hidden, axis=1, keepdims=True) + EPS)
        normed = (hidden * inverse * scale_of(ids, told.at[f], tok, 0, hidden.shape[1])).astype(BF16)
        normed_out[rows, :] = normed
        if f < 2:
            hidden_out[rows, :] = held[rows, :]
        qkv = nn(normed, weight[...]).astype(BF16)
        group = ids[1] ^ ORDER[f]
        for pair in range(2):
            for part in range(3):
                packed[2 * group + pair, :, pl.ds(part * 128, 128)] = qkv[
                    :, (2 * part + pair) * 128 : (2 * part + pair + 1) * 128
                ]


def turn(vectors, cosine, sine):
    lane = lax.broadcasted_iota(jnp.int32, vectors.shape, 1)
    first = (lane & 63) < 32
    other = jnp.where(first, pltpu.roll(vectors, 96, 1), pltpu.roll(vectors, 32, 1))
    return vectors * cosine + other * sine


CHUNK = 256


def rotated(qkv, cosine, sine):
    total = qkv.shape[0] * qkv.shape[1]
    queries = qkv[:, :, 0:128].reshape(total, 128).astype(F32)
    keys = qkv[:, :, 128:256].reshape(total, 128).astype(F32)
    low_q = (turn(queries, cosine[...], sine[...])).astype(BF16) * jnp.asarray(0.125, BF16)
    low_k = turn(keys, cosine[...], sine[...]).astype(BF16)
    return low_q, low_k


def owners_of(ids, told, total):
    utts = told.shape[1] // 2
    group = ids[1] ^ (ids[0] >> 1)
    lens = jnp.zeros((2 * utts, utts), F32)
    for f in range(4):
        lens = lens + jnp.where(group == ORDER[f], told[f, :, 0:utts], 0.0)
    _, end, _, end_col = utt_bounds(lens, utts)
    down = lax.broadcasted_iota(jnp.int32, (total, utts), 0).astype(F32)
    across = lax.broadcasted_iota(jnp.int32, (utts, total), 1).astype(F32)
    col = jnp.sum(jnp.where(down >= end, 1.0, 0.0), axis=1, keepdims=True)
    row = jnp.sum(jnp.where(across >= end_col, 1.0, 0.0), axis=0, keepdims=True)
    return col, row


def attend_kernel(ids, qkv, cosine, sine, told, out, log_out, owner_row):
    total = cosine.shape[0]
    owner_col, owner_row[...] = owners_of(ids, told, total)
    tok = qkv.shape[1]
    queries, keys = rotated(qkv, cosine, sine)
    values = qkv[:, :, 256:384].reshape(total, 128)
    for chunk in range(total // CHUNK):
        rows = slice(chunk * CHUNK, (chunk + 1) * CHUNK)
        same = owner_col == owner_row[:, rows]
        both = []
        for head in range(2):
            lanes = slice(64 * head, 64 * head + 64)
            scores = jnp.where(same, nt(keys[:, lanes], queries[rows, lanes]), -1e30)
            top = jnp.max(scores, axis=0, keepdims=True)
            weights = jnp.exp(scores - top)
            total_w = jnp.sum(weights, axis=0, keepdims=True)
            log_out[head : head + 1, rows] = top + jnp.log(total_w)
            mixed = tn(values[:, lanes], weights.astype(BF16)) * (1.0 / total_w)
            both.append(mixed.T)
        joined = jnp.concatenate(both, axis=1).astype(BF16)
        for block in range(CHUNK // tok):
            out[chunk * (CHUNK // tok) + block] = joined[block * tok : (block + 1) * tok]


def attend_back_kernel(
    ids, qkv, d_att, cosine, sine, log_total, told, out, d_keys, d_values, owner_row
):
    total = cosine.shape[0]
    owner_col, owner_row[...] = owners_of(ids, told, total)
    tok = qkv.shape[1]
    queries, keys = rotated(qkv, cosine, sine)
    values = qkv[:, :, 256:384].reshape(total, 128)
    back = d_att[...].reshape(total, 128)
    keys_t = [keys[:, 64 * head : 64 * head + 64].astype(F32).T.astype(BF16) for head in range(2)]
    for chunk in range(total // CHUNK):
        rows = slice(chunk * CHUNK, (chunk + 1) * CHUNK)
        same = owner_col == owner_row[:, rows]
        d_queries, k_terms, v_terms = [], [], []
        for head in range(2):
            lanes = slice(64 * head, 64 * head + 64)
            scores = nt(keys[:, lanes], queries[rows, lanes])
            probs = jnp.where(same, jnp.exp(scores - log_total[head : head + 1, rows]), 0.0)
            d_probs = nt(values[:, lanes], back[rows, lanes])
            delta = jnp.sum(probs * d_probs, axis=0, keepdims=True)
            d_scores = (probs * (d_probs - delta)).astype(BF16)
            v_terms.append(nn(probs.astype(BF16), back[rows, lanes]))
            k_terms.append(nn(d_scores, queries[rows, lanes]))
            d_queries.append(nn(keys_t[head], d_scores).T * 0.125)
        k_new = jnp.concatenate(k_terms, axis=1)
        v_new = jnp.concatenate(v_terms, axis=1)
        if chunk == 0:
            d_keys[...] = k_new
            d_values[...] = v_new
        else:
            d_keys[...] += k_new
            d_values[...] += v_new
        d_q = jnp.concatenate(d_queries, axis=1)
        d_q = turn(d_q, cosine[rows, :], -sine[rows, :]).astype(BF16)
        for block in range(CHUNK // tok):
            out[chunk * (CHUNK // tok) + block, :, 0:128] = d_q[block * tok : (block + 1) * tok]
    d_k = turn(d_keys[...], cosine[...], -sine[...]).astype(BF16)
    out[:, :, 128:256] = d_k.reshape(total // tok, tok, 128)
    out[:, :, 256:384] = d_values[...].astype(BF16).reshape(total // tok, tok, 128)


def attended_pairs(ids, blocks, dst, tok, parts):
    pairs = []
    for f in range(4):
        for pair in range(2):
            for part in range(parts):
                pairs.append(
                    (
                        blocks.at[2 * (ids[1] ^ ORDER[f]) + pair, :, pl.ds(part * 128, 128)],
                        dst.at[pl.ds(f * tok, tok), pl.ds((2 * part + pair) * 128, 128)],
                    )
                )
    return pairs


def packed_rows(wide):
    return jnp.concatenate([wide[:, k : k + 256] for k in range(0, wide.shape[1], 256)], axis=0)


def unpacked_rows(rows):
    return jnp.concatenate([rows[k : k + 8] for k in range(0, rows.shape[0], 8)], axis=1)


def cut_skip_kernel(ids, weight, emb, cond_weight, piece):
    rows = weight.shape[0]
    piece[0:rows, :] = weight[:, aligned(ids[1], piece.shape[1])]
    piece[rows:, :] = packed_rows(nn(emb[...], cond_weight[...])).astype(BF16)


def gather_kernel(p0, p1, p2, p3, out):
    rows = (out.shape[0] - 64) // 4
    total = jnp.zeros((64, out.shape[1]), F32)
    for k, piece in enumerate((p0, p1, p2, p3)):
        out[k * rows : (k + 1) * rows, :] = piece[0:rows, :]
        total = total + piece[rows:, :].astype(F32)
    out[4 * rows :, :] = total.astype(BF16)


def join_kernel(left, right, joined):
    width = left.shape[1]
    for k in range(joined.shape[0]):
        joined[k, :, 0:width] = left[...]
        joined[k, :, width:] = right[...]


def near_kernel(even, odd, *outs):
    for k, out in enumerate(outs):
        out[...] = (even[k].astype(F32) + odd[k].astype(F32)).astype(BF16)


def add_kernel(left, right, out, held, sem):
    held[...] = (left[...].astype(F32) + right[...].astype(F32)).astype(out.dtype)
    copy = pltpu.make_async_copy(held, out, sem)
    copy.start()
    copy.wait()


def add_twice_kernel(left, right, out, again):
    total = (left[...].astype(F32) + right[...].astype(F32)).astype(out.dtype)
    out[...] = total
    again[...] = total


def add_three_kernel(first, second, third, out):
    total = first[...].astype(F32) + second[...].astype(F32) + third[...].astype(F32)
    out[...] = total.astype(out.dtype)


def pick_kernel(ids, own, near, far, farther, out):
    z, y = ids[0] >> 1, ids[1] >> 1
    rows = own.shape[0]
    low = z >> 1
    source = (z & 1) == y
    first, second = aligned(low, rows), aligned(1 - low, rows)

    @pl.when(source)
    def _():
        out[first, :] = own[...]
        out[second, :] = far[...]

    @pl.when(jnp.logical_not(source))
    def _():
        out[first, :] = near[...]
        out[second, :] = farther[...]


def copy_kernel(source, out):
    out[...] = source[...]


def stack_kernel(*refs):
    out = refs[-1]
    for k, ref in enumerate(refs[:-1]):
        out[k] = ref[...]


def cut_qkv_kernel(ids, qkv, piece):
    for block in range(piece.shape[1] // 128):
        piece[:, pl.ds(block * 128, 128)] = qkv[:, aligned(4 * block + ids[1], 128)]


def cut_feed_kernel(ids, up, down, piece, sem):
    fetch = pltpu.make_async_copy(down.at[aligned(ids[1], 128), :], piece.at[:, up.shape[1] // 4 :], sem)
    fetch.start()
    for block in range(up.shape[1] // 512):
        piece[:, pl.ds(block * 128, 128)] = up[:, aligned(4 * block + ids[1], 128)]
    fetch.wait()


def utt_bounds(told, utts):
    row = lax.broadcasted_iota(jnp.int32, (utts, utts), 0)
    col = lax.broadcasted_iota(jnp.int32, (utts, utts), 1)
    lens = told[utts : utts + 1, 0:utts]
    spread = jnp.broadcast_to(lens, (utts, utts))
    lens_col = jnp.sum(jnp.where(row == col, spread, 0.0), axis=1, keepdims=True)
    ends = jnp.sum(jnp.where(row <= col, lens_col, 0.0), axis=0, keepdims=True)
    ends_col = jnp.sum(jnp.where(col <= row, spread, 0.0), axis=1, keepdims=True)
    return ends - lens, ends, ends_col - lens_col, ends_col


def scale_of(ids, told, tok, first_col, width):
    utts = told.shape[0] // 2
    begin, end, _, _ = utt_bounds(told, utts)
    frame = (ids[0] * tok + lax.broadcasted_iota(jnp.int32, (tok, utts), 0)).astype(F32)
    onehot = jnp.where((frame >= begin) & (frame < end), 1.0, 0.0).astype(BF16)
    cond = told[0:utts, first_col : first_col + width]
    high = cond.astype(BF16)
    rest = cond - high.astype(F32)
    low = rest.astype(BF16)
    return 1.0 + (nn(onehot, high) + nn(onehot, low))


def utt_picks(ids, told, tok):
    utts = told.shape[0] // 2
    _, _, begin, end = utt_bounds(told, utts)
    frame = (ids[0] * tok + lax.broadcasted_iota(jnp.int32, (utts, tok), 1)).astype(F32)
    return jnp.where((frame >= begin) & (frame < end), 1.0, 0.0).astype(BF16)


def project_kernel(ids, blocks, picked, over, keep, send, attended, weight, sems):
    tok = blocks.shape[1]
    mine = (ids[0] & 1) == (ids[1] & 1)

    @pl.when(mine)
    def _():
        run_copies([(picked, weight)], sems.at[pl.ds(8, 1)])

    @pl.when(jnp.logical_not(mine))
    def _():
        run_copies([(over, weight)], sems.at[pl.ds(8, 1)])

    run_copies(attended_pairs(ids, blocks, attended, tok, 1), sems)
    keep[...] = nn(attended[0 : 2 * tok, :], weight[...])
    send[...] = nn(attended[2 * tok :, :], weight[...]).astype(BF16)


def residual_kernel(ids, hidden, part, other, told, h_one_out, normed_out):
    tok = hidden.shape[0] // 2
    for f in range(2):
        rows, swap = pl.ds(f * tok, tok), pl.ds((1 - f) * tok, tok)
        h_one = hidden[rows, :].astype(F32) + part[rows, :].astype(F32) + other[swap, :].astype(F32)
        inverse = lax.rsqrt(jnp.mean(h_one * h_one, axis=1, keepdims=True) + EPS)
        h_one_out[rows, :] = h_one
        scale = scale_of(ids, told.at[f], tok, h_one.shape[1], h_one.shape[1])
        normed_out[rows, :] = (h_one * inverse * scale).astype(BF16)


def gelu_parts(pre):
    size = jnp.abs(pre)
    decay = jnp.exp(-0.5 * pre * pre)
    t = 1.0 / (1.0 + (0.3275911 * 2.0**-0.5) * size)
    series = t * (0.254829592 + t * (-0.284496736 + t * (1.421413741 + t * (-1.453152027 + t * 1.061405429))))
    tail = 0.5 * series * decay
    half = jnp.where(pre < 0.0, tail, 1.0 - tail)
    return pre * half, half + pre * decay * ((2.0 * math.pi) ** -0.5)


def feed_kernel(ids, *refs):
    normed, normed_c, cots, weight = refs[0], refs[1], refs[2:6], refs[6]
    act_out, d_pre_out, keep, send = refs[7:]
    tok = cots[0].shape[0]
    hidden = act_out.shape[1]
    for f in range(4):
        block = pl.ds(f * tok, tok)
        rows = pl.ds((f % 2) * tok, tok)
        pre = nn((normed, normed_c)[f // 2][rows, :], weight[:, 0:hidden])
        act, slope = gelu_parts(pre)
        act_out[block, :] = act.astype(BF16)
        d_pre = (nt(cots[f][...], weight[:, hidden:]) * slope).astype(BF16)
        d_pre_out[block, :] = d_pre
        d_normed = nt(d_pre, weight[:, 0:hidden])
        if f < 2:
            keep[block, :] = d_normed
        else:
            send[rows, :] = d_normed.astype(BF16)


def feed_grad_kernel(normed, normed_c, c0, c1, c2, c3, act, d_pre, out, held, cots, sems):
    tok = c0.shape[0]
    pairs = [(normed, held.at[pl.ds(0, 2 * tok), :]), (normed_c, held.at[pl.ds(2 * tok, 2 * tok), :])]
    pairs += [(cot, cots.at[pl.ds(f * tok, tok), :]) for f, cot in enumerate((c0, c1, c2, c3))]
    run_copies(pairs, sems)
    cols = act.shape[1]
    for r in range(8):
        block = pl.ds(r * 128, 128)
        out[block, 0:cols] = tn(held[:, block], d_pre[...]).astype(BF16)
        out[block, cols:] = tn(act[:, block], cots[...]).astype(BF16)


def feed_out_kernel(act, weight, keep, send):
    half = keep.shape[0]
    hidden = act.shape[1]
    keep[...] = nn(act[0:half, :], weight[:, hidden:])
    send[...] = nn(act[half:, :], weight[:, hidden:]).astype(BF16)


def norm_back(hidden, scale, d_normed):
    inverse = lax.rsqrt(jnp.mean(hidden * hidden, axis=1, keepdims=True) + EPS)
    y = hidden * inverse
    d_y = d_normed * scale
    d_hidden = inverse * (d_y - y * jnp.mean(d_y * y, axis=1, keepdims=True))
    return d_hidden, d_normed * y


def norm_back_kernel(first_col, ids, hidden, part, other, base, base_y, told, low_out, sums_out):
    tok = hidden.shape[0] // 2
    width = hidden.shape[1]
    for f in range(2):
        rows, swap = pl.ds(f * tok, tok), pl.ds((1 - f) * tok, tok)
        d_normed = part[rows, :].astype(F32) + other[swap, :].astype(F32)
        scale = scale_of(ids, told.at[f], tok, first_col, width)
        d_hidden, d_scale = norm_back(hidden[rows, :].astype(F32), scale, d_normed)
        added = (base, base_y)[f][...].astype(F32) + d_hidden
        low_out[rows, :] = added.astype(low_out.dtype)
        if f == 0:
            sums_out[...] = nn(utt_picks(ids, told.at[0], tok), d_scale.astype(BF16))


def d_attended_kernel(ids, d_h, d_h_c, weight, packed):
    tok = packed.shape[1]
    for f in range(4):
        rows = pl.ds((f % 2) * tok, tok)
        part = nt((d_h, d_h_c)[f // 2][rows, :], weight[...]).astype(BF16)
        group = ids[1] ^ ORDER[f]
        for pair in range(2):
            packed[2 * group + pair] = part[:, pair * 128 : (pair + 1) * 128]


def qkv_back_kernel(ids, blocks, weight, keep, send, joined, sems):
    tok = blocks.shape[1]
    run_copies(attended_pairs(ids, blocks, joined, tok, 3), sems)
    half = keep.shape[0]
    send[...] = nt(joined[half:, :], weight[...]).astype(BF16)
    keep[...] = nt(joined[0:half, :], weight[...])


def qkv_grad_kernel(ids, normed, joined, d_h, d_h_c, a0, a2, a1, a3, even, odd, attended, sems):
    tok = a0.shape[0] // 4
    half = d_h.shape[0]
    pairs = []
    for q, piece in enumerate((a0, a1, a2, a3)):
        for f in range(4):
            for pair in range(2):
                pairs.append(
                    (
                        piece.at[pl.ds(ORDER[ORDER[f] ^ q] * tok, tok), pl.ds(pair * 128, 128)],
                        attended.at[pl.ds(f * tok, tok), aligned((ids[1] ^ q) + 4 * pair, 128)],
                    )
                )
    run_copies(pairs, sems)
    cols = joined.shape[1]
    mine = aligned(ids[1], 256)
    for r in (1, 3, 5, 7, 0, 2, 4, 6):
        block = aligned(ids[0] ^ r, 128)
        target = (even, odd)[r % 2]
        target[r // 2, :, 0:cols] = tn(normed[:, block], joined[...]).astype(BF16)
        target[r // 2, :, cols:] = (
            tn(attended[0:half, block], d_h[:, mine]) + tn(attended[half:, block], d_h_c[:, mine])
        ).astype(BF16)


def skip_back_kernel(ids, d_h, d_h_c, inputs, sums_attn, sums_ffn, even, odd, sums, held, sems):
    tok = inputs.shape[1]
    run_copies(frame_blocks(ids, inputs, held), sems)
    mine = aligned(ids[1], 256)
    near, far = d_h[:, mine], d_h_c[:, mine]
    half = 2 * tok
    for r in (1, 3, 5, 7, 0, 2, 4, 6):
        block = aligned(ids[0] ^ r, 256)
        grad = (tn(held[0:half, block], near) + tn(held[half:, block], far)).astype(BF16)
        if r % 2:
            odd[(r // 2) * 256 : (r // 2) * 256 + 256, :] = grad
        else:
            even[r // 2] = grad
    low = packed_rows(jnp.concatenate([sums_attn[...], sums_ffn[...]], axis=1)).astype(BF16)
    odd[1024:, :] = low
    sums[...] = low


def skip_near_kernel(even, sums, arrived, *outs):
    both = (sums[...].astype(F32) + arrived[1024:, :].astype(F32)).astype(BF16)
    for k, out in enumerate(outs):
        out[0:256, :] = (even[k].astype(F32) + arrived[k * 256 : (k + 1) * 256, :].astype(F32)).astype(BF16)
        out[256:, :] = both


def in_back_kernel(ids, d_h, near, far, in_out, skip_out):
    tok, width = in_out.shape
    total = jnp.zeros((tok, 2 * width), F32)
    for q in range(4):
        weight = (near, far)[q % 2].at[q // 2]
        total = total + nt(d_h[0:tok, aligned(ids[1] ^ q, 256)], weight[...])
    in_out[...] = total[:, 0:width].astype(BF16)
    skip_out[...] = total[:, width:].astype(BF16)


def spread_feed_kernel(ids, near, far, up_o, down_o):
    hidden = near.shape[2] - down_o.shape[1]
    for q in range(4):
        part = ids[1] ^ q
        feed = (near, far)[q % 2].at[q // 2]
        for block in range(hidden // 128):
            up_o[:, aligned(4 * block + part, 128)] = feed[:, pl.ds(block * 128, 128)].astype(F32)
        down_o[aligned(part, 128), :] = feed[:, hidden:].astype(F32)


def last_kernel(p0, p1, p2, p3, q0, q1, q2, q3, out):
    qkv = q0[...].astype(F32) + q1[...].astype(F32) + q2[...].astype(F32) + q3[...].astype(F32)
    skip = p0[...].astype(F32) + p1[...].astype(F32) + p2[...].astype(F32) + p3[...].astype(F32)
    out[:, 0:1024] = qkv.astype(BF16)
    out[:, 1024:1280] = skip[0:128].astype(BF16)
    out[:, 1280:1536] = skip[128:256].astype(BF16)
    out[0:64, 1536:1792] = skip[256:].astype(BF16)
    out[64:, 1536:1792] = jnp.zeros((64, 256), BF16)


def spread_kernel(ids, g0, g1, g2, g3, emb, qkv_o, out_o, skip_o, cond_o):
    rows = qkv_o.shape[0]
    utts = emb.shape[0] // 4
    for q in range(4):
        part = ids[1] ^ q
        piece = (g0, g2, g1, g3)[q]
        for block in range(6):
            qkv_o[:, aligned(4 * block + part, 128)] = piece[0:rows, pl.ds(block * 128, 128)].astype(F32)
        out_o[:, aligned(part, 256)] = piece[0:rows, pl.ds(768, 256)].astype(F32)
        skip_o[0:rows, aligned(part, 256)] = piece[0:rows, pl.ds(1024, 256)].astype(F32)
        skip_o[rows:, aligned(part, 256)] = piece[0:rows, pl.ds(1280, 256)].astype(F32)
    total = jnp.zeros(cond_o.shape, F32)
    for f in range(4):
        sums = unpacked_rows((g0, g1, g2, g3)[f][0:64, 1536:1792].astype(F32)).astype(BF16)
        total = total + tn(emb[f * utts : (f + 1) * utts, :], sums)
    cond_o[...] = total


def stack(arrays, deps=()):
    shape = (len(arrays),) + arrays[0].shape
    return call(stack_kernel, [sds(shape, arrays[0].dtype)], [VMEM] * len(arrays), [], list(arrays), deps=deps)[0]


def around(piece):
    return [piece, from_grp(piece, 2), from_grp(piece, 1), from_grp(piece, 3)]


def gather_groups(piece):
    along_y = from_grp(piece, 2)
    return [piece, along_y, from_grp(piece, 1), from_grp(along_y, 1)]


def gather_pairs(piece, deps=()):
    near = stack([piece, from_grp(piece, 2)], deps)
    return near, from_grp(near, 1)


def scatter_near(even, odd, deps):
    arrived = from_seq(odd, 1)
    return call(near_kernel, [sds(even.shape[1:], BF16)] * 4, [VMEM] * 2, [], [even, arrived], deps=deps)


def by_mask(pieces):
    return [pieces[0], pieces[2], pieces[1], pieces[3]]


def halves_sum(keep, send):
    kept, sent = call(
        add_twice_kernel, [sds(keep.shape, BF16)] * 2, [VMEM] * 2, [], [keep, from_grp(send, 1)]
    )
    return kept, from_grp(sent, 2)


def add_two(left, right, deps=()):
    return call(
        add_kernel,
        [sds(left.shape, BF16)],
        [VMEM] * 2,
        [pltpu.VMEM(left.shape, BF16), pltpu.SemaphoreType.DMA],
        [left, right],
        deps=deps,
        out_spec=HBM,
    )[0]


def exchange(array, cols):
    return lax.all_to_all(array, "seq", 0, 0, tiled=True)


def out_moves(mask, keep):
    pairs = []
    for t in range(4):
        for slot in range(8):
            if keep(slot, t):
                pairs.append((t * 8 + slot, t * 8 + (slot ^ mask)))
    return pairs


def out_along_z(piece):
    def holds(slot, t):
        return (slot & 1) == (t & 1) and ((slot >> 1) & 1) == (t >> 1)

    return [lax.ppermute(piece, ("grp", "seq"), out_moves(2 * k, holds)) for k in range(1, 4)]


def out_along_x(rows):
    return lax.ppermute(rows, ("grp", "seq"), out_moves(1, lambda slot, t: (slot & 1) == (t & 1)))


def tp_body(
    hidden_in, skips, lengths, times, skip_weight, cond_weight, qkv_weight, out_weight,
    up_weight, down_weight, cotangent,
):
    tok, width = hidden_in.shape
    ff = up_weight.shape[1]
    frames = 8 * tok
    slot = lax.axis_index("seq")
    part = lax.axis_index("grp")
    ids = jnp.stack([slot, part]).astype(jnp.int32)
    sem = pltpu.SemaphoreType.DMA

    half_width = width // 2
    rows_here = cond_weight.shape[0]
    utts = times.shape[1]

    def embed_here(time_rows):
        column = (slot * rows_here + jnp.arange(rows_here, dtype=jnp.int32)) % half_width
        freqs = jnp.exp(-math.log(10000.0) * column.astype(F32) / half_width)
        angles = time_rows[:, None] * freqs[None, :]
        return jnp.where(slot * rows_here < half_width, jnp.sin(angles), jnp.cos(angles)).astype(BF16)

    skip_rows = skip_weight.shape[0]
    (skip_piece,) = call(
        cut_skip_kernel,
        [sds((skip_rows + 64, 256), BF16)],
        [SMEM] + [VMEM] * 3,
        [],
        [ids, skip_weight, embed_here(times[0].astype(F32)), cond_weight],
    )
    (skip_same,) = call(
        gather_kernel,
        [sds((4 * skip_rows + 64, 256), BF16)],
        [VMEM] * 4,
        [],
        [skip_piece] + [from_seq(skip_piece, 2 * k) for k in range(1, 4)],
    )
    skip_other = from_seq(skip_same, 1)
    (joined,) = call(
        join_kernel, [sds((4, tok, 2 * width), BF16)], [VMEM] * 2, [], [hidden_in, skips], deps=[skip_piece]
    )
    inputs = lax.all_to_all(joined, "grp", 0, 0, tiled=True)
    (qkv_piece,) = call(cut_qkv_kernel, [sds((128, 768), BF16)], [SMEM, VMEM], [], [ids, qkv_weight], deps=[joined])
    w_qkv = lax.all_gather(qkv_piece, "seq", axis=0, tiled=True)
    (feed_piece,) = call(
        cut_feed_kernel,
        [sds((128, ff // 4 + width), BF16)],
        [SMEM, VMEM, ANY],
        [sem],
        [ids, up_weight, down_weight],
        deps=[qkv_piece],
    )
    w_feed = lax.all_gather(feed_piece, "seq", axis=0, tiled=True)

    counts = jnp.stack([lengths[0] >> 5, lengths[0] & 31, times[0] >> 5, times[0] & 31])
    notes = jnp.zeros((16, 256), BF16).at[0:4, 0:utts].set(counts.astype(BF16))

    (out_piece,) = call(copy_kernel, [sds(out_weight.shape, BF16)], [VMEM], [], [out_weight], deps=[skip_same])
    out_came = out_along_z(out_piece)

    inverse = jnp.exp(-math.log(10000.0) * jnp.arange(32, dtype=F32) / 32)
    turn_angles = jnp.arange(frames, dtype=F32)[:, None] * inverse[None, :]
    cos_half, sin_half = jnp.cos(turn_angles), jnp.sin(turn_angles)
    cosine = jnp.concatenate([cos_half] * 4, axis=1)
    sine = jnp.concatenate([-sin_half, sin_half] * 2, axis=1)

    h_cols, w_skip = call(
        h_zero_kernel,
        [sds((4 * tok + 80, 256), BF16), sds((2 * width, 256), BF16)],
        [SMEM] + [ANY] * 3 + [VMEM],
        [
            pltpu.VMEM((4 * tok, 2 * width), BF16),
            pltpu.VMEM((2 * width, 256), BF16),
            pltpu.VMEM((2, 64, 256), BF16),
            sem((14,)),
        ],
        [ids, inputs, skip_same, skip_other, notes],
        deps=out_came,
        cost_us=100.0,
    )
    h_pieces = gather_groups(h_cols)
    h_pieces = [h_pieces[0], h_pieces[2], h_pieces[1], h_pieces[3]]
    normed, h_zero, packed, told = call(
        qkv_kernel,
        [
            sds((4 * tok, width), BF16),
            sds((2 * tok, width), BF16),
            sds((8, tok, 384), BF16),
            sds((4, 2 * utts, 2 * width), F32),
        ],
        [SMEM] + [ANY] * 4 + [VMEM],
        [pltpu.VMEM((4 * tok, width), BF16), pltpu.VMEM((4, 80, 256), BF16), sem((20,))],
        [ids] + h_pieces + [w_qkv],
    )
    emb_all = embed_here(told[:, utts + 1, :utts].reshape(4 * utts))
    qkv = exchange(packed, 384)
    (out_picked,) = call(
        pick_kernel, [sds((2 * tok, width), BF16)], [SMEM] + [VMEM] * 4, [], [ids, out_piece] + out_came
    )
    out_over = out_along_x(out_picked)
    (w_skip,) = call(copy_kernel, [sds(w_skip.shape, BF16)], [VMEM], [], [w_skip], deps=[packed])
    skip_y = from_grp(w_skip, 2)
    mixed, log_total = call(
        attend_kernel,
        [sds((8, tok, 128), BF16), sds((2, frames), F32)],
        [SMEM] + [VMEM] * 4,
        [pltpu.VMEM((1, frames), F32)],
        [ids, qkv, cosine, sine, told],
        deps=[emb_all, out_over, skip_y],
    )
    attended_blocks = exchange(mixed, 128)
    (cot_piece,) = call(
        copy_kernel, [sds((tok, width), BF16)], [VMEM], [], [cotangent], deps=[mixed]
    )
    cots = around(cot_piece)
    keep, send, attended, w_out = call(
        project_kernel,
        [
            sds((2 * tok, width), F32),
            sds((2 * tok, width), BF16),
            sds((4 * tok, 256), BF16),
            sds((2 * tok, width), BF16),
        ],
        [SMEM, ANY, ANY, ANY],
        [sem((9,))],
        [ids, attended_blocks, out_picked, out_over],
        deps=cots[1:],
    )
    h_part, h_part_y = halves_sum(keep, send)
    skip_near = stack([w_skip, skip_y], [h_part])
    skip_far = from_grp(skip_near, 1)
    h_one, normed_two = call(
        residual_kernel,
        [sds((2 * tok, width), F32), sds((2 * tok, width), BF16)],
        [SMEM] + [VMEM] * 4,
        [],
        [ids, h_zero, h_part, h_part_y, told],
        deps=[skip_near],
    )
    normed_two_c = from_grp(normed_two, 1)
    quarter = ff // 4
    act, d_pre, keep, send = call(
        feed_kernel,
        [
            sds((4 * tok, quarter), BF16),
            sds((4 * tok, quarter), BF16),
            sds((2 * tok, width), F32),
            sds((2 * tok, width), BF16),
        ],
        [SMEM] + [VMEM] * 7,
        [],
        [ids, normed_two, normed_two_c, *cots, w_feed],
    )

    d_part, d_part_y = halves_sum(keep, send)
    (feed_terms,) = call(
        feed_grad_kernel,
        [sds((width, quarter + width), BF16)],
        [ANY] * 6 + [VMEM] * 2,
        [pltpu.VMEM((4 * tok, width), BF16), pltpu.VMEM((4 * tok, width), BF16), sem((6,))],
        [normed_two, normed_two_c, *cots, act, d_pre],
        deps=[d_part],
    )
    out_keep, out_send = call(
        feed_out_kernel,
        [sds((2 * tok, width), F32), sds((2 * tok, width), BF16)],
        [VMEM, VMEM],
        [],
        [act, w_feed],
        deps=[feed_terms],
    )
    d_h_one, sums_ffn = call(
        functools.partial(norm_back_kernel, width),
        [sds((2 * tok, width), BF16), sds((utts, width), F32)],
        [SMEM] + [VMEM] * 6,
        [],
        [ids, h_one, d_part, d_part_y, cots[0], cots[1], told],
        deps=[out_send],
        cost_us=100.0,
    )
    d_h_one_c = from_grp(d_h_one, 1)
    (d_att_packed,) = call(
        d_attended_kernel,
        [sds((8, tok, 128), BF16)],
        [SMEM, VMEM, VMEM, VMEM],
        [],
        [ids, d_h_one, d_h_one_c, w_out],
    )
    d_att = exchange(d_att_packed, 128)

    out_part = add_two(out_keep, from_grp(out_send, 1), [d_att_packed])
    feed_own = lax.psum_scatter(feed_terms, "seq", scatter_dimension=0, tiled=True)
    att_pieces = around(attended)
    (d_packed,) = call(
        attend_back_kernel,
        [sds((8, tok, 384), BF16)],
        [SMEM] + [VMEM] * 6,
        [pltpu.VMEM((frames, 128), F32), pltpu.VMEM((frames, 128), F32), pltpu.VMEM((1, frames), F32)],
        [ids, qkv, d_att, cosine, sine, log_total, told],
        deps=[out_part] + att_pieces[1:],
    )
    d_qkv_blocks = exchange(d_packed, 384)
    (block_out,) = call(
        add_three_kernel,
        [sds((tok, width), BF16)],
        [VMEM] * 3,
        [],
        [h_one[:tok], out_part[:tok], from_grp(out_part[tok:], 2)],
        deps=[d_packed],
    )
    keep, send, d_qkv = call(
        qkv_back_kernel,
        [sds((2 * tok, width), F32), sds((2 * tok, width), BF16), sds((4 * tok, 768), BF16)],
        [SMEM, ANY, VMEM],
        [sem((24,))],
        [ids, d_qkv_blocks, w_qkv],
        deps=[block_out],
    )
    d_part, d_part_y = halves_sum(keep, send)
    qkv_even, qkv_odd = call(
        qkv_grad_kernel,
        [sds((4, 128, 1024), BF16)] * 2,
        [SMEM] + [VMEM] * 4 + [ANY] * 4,
        [pltpu.VMEM((4 * tok, width), BF16), sem((32,))],
        [ids, normed, d_qkv, d_h_one, d_h_one_c] + att_pieces,
        deps=[d_part],
    )
    d_h_zero, sums_attn = call(
        functools.partial(norm_back_kernel, 0),
        [sds((2 * tok, width), BF16), sds((utts, width), F32)],
        [SMEM] + [VMEM] * 6,
        [],
        [ids, h_zero, d_part, d_part_y, d_h_one[:tok], d_h_one[tok:], told],
        deps=[qkv_odd],
    )
    d_h_zero_c = from_grp(d_h_zero, 1)
    skip_even, skip_odd, skip_sums = call(
        skip_back_kernel,
        [sds((4, 256, 256), BF16), sds((1024 + 64, 256), BF16), sds((64, 256), BF16)],
        [SMEM, VMEM, VMEM, ANY, VMEM, VMEM],
        [pltpu.VMEM((4 * tok, 2 * width), BF16), sem((4,))],
        [ids, d_h_zero, d_h_zero_c, inputs, sums_attn, sums_ffn],
    )
    qkv_near = scatter_near(qkv_even, qkv_odd, [skip_odd])
    qkv_came = [from_seq(qkv_near[k], 2 * k) for k in range(1, 4)]
    last_near = call(
        skip_near_kernel,
        [sds((256 + 64, 256), BF16)] * 4,
        [VMEM] * 3,
        [],
        [skip_even, skip_sums, from_seq(skip_odd, 1)],
        deps=[qkv_near[0]],
    )
    last_came = [from_seq(last_near[k], 2 * k) for k in range(1, 4)]
    in_grad, skip_grad = call(
        in_back_kernel,
        [sds((tok, width), BF16)] * 2,
        [SMEM] + [VMEM] * 3,
        [],
        [ids, d_h_zero, skip_near, skip_far],
        deps=qkv_came + [last_near[0]],
    )
    (last_own,) = call(
        last_kernel,
        [sds((128, 1792), BF16)],
        [VMEM] * 8,
        [],
        [last_near[0]] + last_came + [qkv_near[0]] + qkv_came,
        deps=[in_grad],
    )
    last_all = gather_groups(last_own)
    feed_near, feed_far = gather_pairs(feed_own, [last_own])
    up_grad, down_grad = call(
        spread_feed_kernel,
        [sds((128, ff), F32), sds((ff // 8, width), F32)],
        [SMEM] + [VMEM] * 2,
        [],
        [ids, feed_near, feed_far],
    )
    qkv_grad, out_grad, skip_grad_w, cond_grad = call(
        spread_kernel,
        [
            sds((128, 3 * width), F32),
            sds((128, width), F32),
            sds((256, width), F32),
            sds((rows_here, 2 * width), F32),
        ],
        [SMEM] + [VMEM] * 5,
        [],
        [ids] + last_all + [emb_all],
        deps=[up_grad],
    )
    return (
        block_out, in_grad, skip_grad, skip_grad_w, cond_grad, qkv_grad,
        out_grad, up_grad, down_grad,
    )


def solution(mesh):
    placed = (
        P(("grp", "seq"), None),
        P(("grp", "seq"), None),
        P("grp", None),
        P("grp", None),
        P("seq", None),
        P("seq", None),
        P("seq", None),
        P("seq", None),
        P("seq", None),
        P("seq", None),
        P(("grp", "seq"), None),
    )
    body = tp_body if (mesh.shape["grp"], mesh.shape["seq"]) == (4, 8) else plain_body
    return jax.shard_map(
        body,
        mesh=mesh,
        in_specs=placed,
        out_specs=(
            P(("grp", "seq"), None),
            P(("grp", "seq"), None),
            P(("grp", "seq"), None),
            P("seq", None),
            P("seq", None),
            P("seq", None),
            P("seq", None),
            P("seq", None),
            P("seq", None),
        ),
        check_vma=False,
    )
```

```python
import functools
import math

import jax
import jax.numpy as jnp
from jax import lax
from jax.experimental import pallas as pl
from jax.experimental.pallas import tpu as pltpu
from jax.sharding import PartitionSpec as P

HEADS = 16


EPS = 1e-06


def contract(left, right, left_dim, right_dim):
    return lax.dot_general(
        left, right, (((left_dim,), (right_dim,)), ((), ())), preferred_element_type=jnp.float32
    )


def matmul(left, right):
    return jnp.dot(left, right, preferred_element_type=jnp.float32)


def owner_of(frames, utt_ends):
    return jnp.sum((frames[:, None] >= utt_ends[None, :]).astype(jnp.int32), axis=1)


def same_owner(query_owner, key_owner):
    return (query_owner[:, None] == key_owner[None, :])[:, None, :]


def embed_steps(time_steps, model_width):
    half_width = model_width // 2
    freqs = jnp.exp(-math.log(10000.0) * jnp.arange(half_width, dtype=jnp.float32) / half_width)
    angles = time_steps[:, None] * freqs[None, :]
    return jnp.concatenate([jnp.sin(angles), jnp.cos(angles)], axis=1)


def rotate(vectors, positions, head_count, direction):
    tok_rows, model_width = vectors.shape
    head_size = model_width // head_count
    half_size = head_size // 2
    inverse = jnp.exp(-math.log(10000.0) * jnp.arange(half_size, dtype=jnp.float32) / half_size)
    angles = positions[:, None] * inverse[None, :]
    cosine = jnp.cos(angles)[:, None, :]
    sine = direction * jnp.sin(angles)[:, None, :]
    split = vectors.reshape(tok_rows, head_count, head_size)
    first_half = split[..., :half_size]
    second_half = split[..., half_size:]
    turned = jnp.concatenate(
        [first_half * cosine - second_half * sine, first_half * sine + second_half * cosine],
        axis=-1,
    )
    return turned.reshape(tok_rows, model_width)


def scale_norm(hidden, cond_part):
    return (
        hidden
        * lax.rsqrt(jnp.mean(hidden * hidden, axis=1, keepdims=True) + EPS)
        * (1.0 + cond_part)
    )


def over_blocks(update, running, arrays, first_row, block_cap):
    row_count = arrays[0].shape[0]
    block_size = math.gcd(row_count, block_cap)
    number = row_count // block_size
    if number == 1:
        return update(running, arrays, first_row)
    stacked = tuple((array.reshape((number, block_size) + array.shape[1:]) for array in arrays))
    offsets = first_row + block_size * jnp.arange(number, dtype=jnp.int32)

    def over_scan_step(inner, scan_in):
        return (update(inner, scan_in[0], scan_in[1]), None)

    result, unused = lax.scan(over_scan_step, running, (stacked, offsets))
    return result


def grad_terms(
    q_heads, do_heads, log_total, row_delta, key_heads, value_heads, same_utt, score_scale
):
    scores = (
        jnp.einsum("qhd,khd->qhk", q_heads, key_heads, preferred_element_type=jnp.float32)
        * score_scale
    )
    probs = jnp.where(same_utt, jnp.exp(scores - log_total[..., None]), 0.0)
    d_probs = jnp.einsum("qhd,khd->qhk", do_heads, value_heads, preferred_element_type=jnp.float32)
    d_scores = (probs * (d_probs - row_delta[..., None]) * score_scale).astype(jnp.bfloat16)
    return (probs.astype(jnp.bfloat16), d_scores)


def scatter_first(after, grad):
    return lax.optimization_barrier(
        (after, lax.psum_scatter(grad, "seq", scatter_dimension=0, tiled=True))
    )


def plain_body(
    hidden_in,
    skips,
    lengths,
    times,
    skip_weight,
    cond_weight,
    qkv_weight,
    out_weight,
    up_weight,
    down_weight,
    cotangent,
):
    tok_rows, model_width = hidden_in.shape
    head_count = HEADS
    head_size = model_width // head_count
    score_scale = head_size ** (-0.5)
    first_frame = lax.axis_index("seq") * tok_rows
    utt_lengths = lengths[0]
    utt_ends = jnp.cumsum(utt_lengths)
    starts = utt_ends - utt_lengths
    frames = first_frame + jnp.arange(tok_rows, dtype=jnp.int32)
    query_owner = owner_of(frames, utt_ends)
    onehot = query_owner[:, None] == jnp.arange(utt_lengths.shape[0], dtype=jnp.int32)[None, :]
    positions = (frames - jnp.sum(jnp.where(onehot, starts[None, :], 0), axis=1)).astype(
        jnp.float32
    )
    time_steps = jnp.sum(jnp.where(onehot, times[0][None, :], 0), axis=1).astype(jnp.float32)
    gathered = (
        lax.all_gather(skip_weight, "seq", axis=0, tiled=True),
        lax.all_gather(cond_weight, "seq", axis=0, tiled=True),
        lax.all_gather(qkv_weight, "seq", axis=0, tiled=True),
        lax.all_gather(out_weight, "seq", axis=0, tiled=True),
        lax.all_gather(up_weight, "seq", axis=0, tiled=True),
        lax.all_gather(down_weight, "seq", axis=0, tiled=True),
    )
    w_skip, w_cond, w_qkv, w_out, w_up, w_down = gathered
    h_zero = matmul(hidden_in, w_skip[:model_width]) + matmul(skips, w_skip[model_width:])
    emb = embed_steps(time_steps, model_width).astype(jnp.bfloat16)
    cond = matmul(emb, w_cond)
    cond_attn = cond[:, :model_width]
    cond_ffn = cond[:, model_width:]
    normed = scale_norm(h_zero, cond_attn).astype(jnp.bfloat16)
    qkv = matmul(normed, w_qkv)
    queries = rotate(qkv[:, :model_width], positions, head_count, 1.0).astype(jnp.bfloat16)
    keys = rotate(qkv[:, model_width : 2 * model_width], positions, head_count, 1.0).astype(
        jnp.bfloat16
    )
    values = qkv[:, 2 * model_width :].astype(jnp.bfloat16)
    q_heads = queries.reshape(tok_rows, head_count, head_size)

    def forward_step(running, blocks, first_row):
        weighted, run_max, run_sum = running
        key_heads = blocks[0].reshape(-1, head_count, head_size)
        value_heads = blocks[1].reshape(-1, head_count, head_size)
        key_owner = owner_of(first_row + jnp.arange(key_heads.shape[0], dtype=jnp.int32), utt_ends)
        same_utt = same_owner(query_owner, key_owner)
        scores = (
            jnp.einsum("qhd,khd->qhk", q_heads, key_heads, preferred_element_type=jnp.float32)
            * score_scale
        )
        new_max = jnp.maximum(run_max, jnp.max(jnp.where(same_utt, scores, -1e30), axis=-1))
        weights_b = jnp.where(same_utt, jnp.exp(scores - new_max[..., None]), 0.0)
        factor = jnp.exp(run_max - new_max)
        run_sum = run_sum * factor + jnp.sum(weights_b, axis=-1)
        weighted = weighted * factor[..., None] + jnp.einsum(
            "qhk,khd->qhd",
            weights_b.astype(jnp.bfloat16),
            value_heads,
            preferred_element_type=jnp.float32,
        )
        return (weighted, new_max, run_sum)

    start_state = (
        jnp.zeros((tok_rows, head_count, head_size), jnp.float32),
        jnp.full((tok_rows, head_count), -1e30, jnp.float32),
        jnp.zeros((tok_rows, head_count), jnp.float32),
    )
    weighted, run_max, run_sum = over_blocks(
        forward_step,
        start_state,
        (
            lax.all_gather(keys, "seq", axis=0, tiled=True),
            lax.all_gather(values, "seq", axis=0, tiled=True),
        ),
        jnp.int32(0),
        1024,
    )
    attended_full = (weighted / run_sum[..., None]).reshape(tok_rows, model_width)
    log_total = run_max + jnp.log(run_sum)
    attended = attended_full.astype(jnp.bfloat16)
    h_one = h_zero + matmul(attended, w_out)
    normed_two = scale_norm(h_one, cond_ffn).astype(jnp.bfloat16)
    pre = matmul(normed_two, w_up)
    act = jax.nn.gelu(pre, approximate=False).astype(jnp.bfloat16)
    block_out = (h_one + matmul(act, w_down)).astype(jnp.bfloat16)
    regathered = (
        lax.all_gather(skip_weight, "seq", axis=0, tiled=True),
        lax.all_gather(cond_weight, "seq", axis=0, tiled=True),
        lax.all_gather(qkv_weight, "seq", axis=0, tiled=True),
        lax.all_gather(out_weight, "seq", axis=0, tiled=True),
        lax.all_gather(up_weight, "seq", axis=0, tiled=True),
        lax.all_gather(down_weight, "seq", axis=0, tiled=True),
    )
    w_skip, w_cond, w_qkv, w_out, w_up, w_down = regathered
    d_act = contract(cotangent, w_down, 1, 1)
    d_act, shard_down = scatter_first(d_act, contract(act, cotangent, 0, 0))
    unused, gelu_back = jax.vjp(lambda inner: jax.nn.gelu(inner, approximate=False), pre)
    d_pre = gelu_back(d_act)[0].astype(jnp.bfloat16)
    d_pre, shard_up = scatter_first(d_pre, contract(normed_two, d_pre, 0, 0))
    d_normed_two = contract(d_pre, w_up, 1, 1)
    unused, norm_back_two = jax.vjp(scale_norm, h_one, cond_ffn)
    d_h_norm, d_cond_ffn = norm_back_two(d_normed_two)
    d_h_one = cotangent.astype(jnp.float32) + d_h_norm
    d_h_low = d_h_one.astype(jnp.bfloat16)
    d_h_low, shard_out = scatter_first(d_h_low, contract(attended, d_h_low, 0, 0))
    d_attended = contract(d_h_low, w_out, 1, 1).astype(jnp.bfloat16)
    row_delta = jnp.sum(
        (d_attended.astype(jnp.float32) * attended_full).reshape(tok_rows, head_count, head_size),
        axis=-1,
    )
    do_heads = d_attended.reshape(tok_rows, head_count, head_size)
    keys_all, values_all = (
        lax.all_gather(keys, "seq", axis=0, tiled=True),
        lax.all_gather(values, "seq", axis=0, tiled=True),
    )
    key_total = keys_all.shape[0]
    block_size = math.gcd(key_total, 1024)
    number = key_total // block_size

    def body_scan_step(d_query, scan_in):
        key_block, value_block, offset = scan_in
        key_heads = key_block.reshape(block_size, head_count, head_size)
        value_heads = value_block.reshape(block_size, head_count, head_size)
        key_owner = owner_of(offset + jnp.arange(block_size, dtype=jnp.int32), utt_ends)
        probs_low, d_scores = grad_terms(
            q_heads,
            do_heads,
            log_total,
            row_delta,
            key_heads,
            value_heads,
            same_owner(query_owner, key_owner),
            score_scale,
        )
        d_query = d_query + jnp.einsum(
            "qhk,khd->qhd", d_scores, key_heads, preferred_element_type=jnp.float32
        )
        d_key = jnp.einsum(
            "qhk,qhd->khd", d_scores, q_heads, preferred_element_type=jnp.float32
        ).reshape(block_size, model_width)
        d_value = jnp.einsum(
            "qhk,qhd->khd", probs_low, do_heads, preferred_element_type=jnp.float32
        ).reshape(block_size, model_width)
        return (d_query, (d_key, d_value))

    d_query, terms = lax.scan(
        body_scan_step,
        jnp.zeros((tok_rows, head_count, head_size), jnp.float32),
        (
            keys_all.reshape(number, block_size, model_width),
            values_all.reshape(number, block_size, model_width),
            block_size * jnp.arange(number, dtype=jnp.int32),
        ),
    )
    value_terms, d_key = scatter_first(terms[1], terms[0].reshape(key_total, model_width))
    d_value = lax.psum_scatter(
        value_terms.reshape(key_total, model_width), "seq", scatter_dimension=0, tiled=True
    )
    d_qkv = jnp.concatenate(
        [
            rotate(d_query.reshape(tok_rows, model_width), positions, head_count, -1.0),
            rotate(d_key, positions, head_count, -1.0),
            d_value,
        ],
        axis=1,
    ).astype(jnp.bfloat16)
    d_qkv, shard_qkv = scatter_first(d_qkv, contract(normed, d_qkv, 0, 0))
    d_normed = contract(d_qkv, w_qkv, 1, 1)
    unused, norm_back_one = jax.vjp(scale_norm, h_zero, cond_attn)
    d_h_first, d_cond_attn = norm_back_one(d_normed)
    d_h_zero = (d_h_one + d_h_first).astype(jnp.bfloat16)
    d_cond = jnp.concatenate([d_cond_attn, d_cond_ffn], axis=1).astype(jnp.bfloat16)
    d_cond, shard_cond = scatter_first(d_cond, contract(emb, d_cond, 0, 0))
    grad_skip_w = jnp.concatenate(
        [contract(hidden_in, d_h_zero, 0, 0), contract(skips, d_h_zero, 0, 0)], axis=0
    )
    in_grad = contract(d_h_zero, w_skip[:model_width], 1, 1).astype(jnp.bfloat16)
    skip_grad = contract(d_h_zero, w_skip[model_width:], 1, 1).astype(jnp.bfloat16)
    shards = (
        lax.psum_scatter(grad_skip_w, "seq", scatter_dimension=0, tiled=True),
        shard_cond,
        shard_qkv,
        shard_out,
        shard_up,
        shard_down,
    )
    summed = (
        lax.psum(shards[0].astype(jnp.bfloat16), "grp").astype(jnp.float32),
        lax.psum(shards[1].astype(jnp.bfloat16), "grp").astype(jnp.float32),
        lax.psum(shards[2].astype(jnp.bfloat16), "grp").astype(jnp.float32),
        lax.psum(shards[3].astype(jnp.bfloat16), "grp").astype(jnp.float32),
        lax.psum(shards[4].astype(jnp.bfloat16), "grp").astype(jnp.float32),
        lax.psum(shards[5].astype(jnp.bfloat16), "grp").astype(jnp.float32),
    )
    return (
        block_out,
        in_grad,
        skip_grad,
        summed[0],
        summed[1],
        summed[2],
        summed[3],
        summed[4],
        summed[5],
    )


ORDER = (0, 2, 1, 3)
BF16 = jnp.bfloat16
VMEM_MIB = 44
F32 = jnp.float32
ANY = pl.BlockSpec(memory_space=pl.ANY)
VMEM = pl.BlockSpec(memory_space=pltpu.VMEM)
HBM = pl.BlockSpec(memory_space=pltpu.HBM)
SMEM = pl.BlockSpec(memory_space=pltpu.SMEM)


def swapped(axis, mask, size):
    return [(index, index ^ mask) for index in range(size)]


def from_seq(array, mask):
    return lax.ppermute(array, "seq", swapped("seq", mask, 8))


def from_grp(array, mask):
    return lax.ppermute(array, "grp", swapped("grp", mask, 4))


def run_copies(pairs, sems):
    copies = [pltpu.make_async_copy(src, dst, sems.at[i]) for i, (src, dst) in enumerate(pairs)]
    for copy in copies:
        copy.start()
    for copy in copies:
        copy.wait()


def call(kernel, out_shapes, in_specs, scratch, args, deps=(), out_spec=VMEM, cost_us=0.0):
    moved = sum(a.size * a.dtype.itemsize for a in args)
    moved += sum(o.size * o.dtype.itemsize for o in out_shapes)
    given, extra = len(args), len(deps)

    def with_deps(*refs):
        kernel(*refs[:given], *refs[given + extra :])

    return pl.pallas_call(
        with_deps,
        out_shape=tuple(out_shapes),
        in_specs=list(in_specs) + [ANY] * extra,
        out_specs=(out_spec,) * len(out_shapes),
        scratch_shapes=scratch,
        compiler_params=pltpu.CompilerParams(vmem_limit_bytes=VMEM_MIB * 1024 * 1024),
        cost_estimate=pl.CostEstimate(
            flops=int(cost_us * 1.15e9), bytes_accessed=0, transcendentals=0
        ),
    )(*args, *deps)


def sds(shape, dtype):
    return jax.ShapeDtypeStruct(shape, dtype)


MARK = sds((8, 128), F32)


def aligned(index, size):
    return pl.ds(pl.multiple_of(index * size, size), size)


def nt(left, right):
    return lax.dot_general(left, right, (((1,), (1,)), ((), ())), preferred_element_type=F32)


def tn(left, right):
    return lax.dot_general(left, right, (((0,), (0,)), ((), ())), preferred_element_type=F32)


def nn(left, right):
    return jnp.dot(left, right, preferred_element_type=F32)


def frame_blocks(ids, blocks, dst):
    tok = blocks.shape[1]
    return [(blocks.at[ids[1] ^ ORDER[f]], dst.at[pl.ds(f * tok, tok), :]) for f in range(4)]


def h_zero_kernel(ids, inputs, near, far, notes, out, whole, held, wide, shares, sems):
    rows = wide.shape[0] // 8
    frames = held.shape[0]
    pairs = frame_blocks(ids, inputs, held)
    for r in range(8):
        piece = (near, far)[r % 2].at[pl.ds((r // 2) * rows, rows), :]
        pairs.append((piece, wide.at[aligned(ids[0] ^ r, rows), :]))
    for k, pieces in enumerate((near, far)):
        pairs.append((pieces.at[pl.ds(4 * rows, 64), :], shares.at[k]))
    run_copies(pairs, sems)
    out[0:frames, :] = nn(held[...], wide[...]).astype(BF16)
    out[frames : frames + 64, :] = (shares[0].astype(F32) + shares[1].astype(F32)).astype(BF16)
    out[frames + 64 :, :] = notes[...]
    whole[...] = wide[...]


def qkv_kernel(ids, *refs):
    pieces, weight = refs[:4], refs[4]
    normed_out, hidden_out, packed, told, held, raw, sems = refs[5:]
    tok = packed.shape[1]
    cols = pieces[0].shape[1]
    pairs = [(pieces[ORDER[f]].at[pl.ds(4 * tok, 80), :], raw.at[f]) for f in range(4)]
    for q in range(4):
        for f in range(4):
            pairs.append(
                (
                    pieces[q].at[pl.ds(ORDER[ORDER[f] ^ q] * tok, tok), :],
                    held.at[pl.ds(f * tok, tok), aligned(ids[1] ^ q, cols)],
                )
            )
    run_copies(pairs, sems)
    for f in range(4):
        rows = raw[f].astype(F32)
        told[f, 0:8, :] = unpacked_rows(rows[0:64])
        counts = jnp.concatenate(
            [32.0 * rows[64:65] + rows[65:66], 32.0 * rows[66:67] + rows[67:68], jnp.zeros((6, cols), F32)], axis=0
        )
        told[f, 8:16, :] = jnp.concatenate([counts, jnp.zeros((8, told.shape[2] - cols), F32)], axis=1)
    for f in range(4):
        rows = pl.ds(f * tok, tok)
        hidden = held[rows, :].astype(F32)
        inverse = lax.rsqrt(jnp.mean(hidden * hidden, axis=1, keepdims=True) + EPS)
        normed = (hidden * inverse * scale_of(ids, told.at[f], tok, 0, hidden.shape[1])).astype(BF16)
        normed_out[rows, :] = normed
        if f < 2:
            hidden_out[rows, :] = held[rows, :]
        qkv = nn(normed, weight[...]).astype(BF16)
        group = ids[1] ^ ORDER[f]
        for pair in range(2):
            for part in range(3):
                packed[2 * group + pair, :, pl.ds(part * 128, 128)] = qkv[
                    :, (2 * part + pair) * 128 : (2 * part + pair + 1) * 128
                ]


def turn(vectors, cosine, sine):
    lane = lax.broadcasted_iota(jnp.int32, vectors.shape, 1)
    first = (lane & 63) < 32
    other = jnp.where(first, pltpu.roll(vectors, 96, 1), pltpu.roll(vectors, 32, 1))
    return vectors * cosine + other * sine


CHUNK = 256


def rotated(qkv, cosine, sine):
    total = qkv.shape[0] * qkv.shape[1]
    queries = qkv[:, :, 0:128].reshape(total, 128).astype(F32)
    keys = qkv[:, :, 128:256].reshape(total, 128).astype(F32)
    low_q = (turn(queries, cosine[...], sine[...])).astype(BF16) * jnp.asarray(0.125, BF16)
    low_k = turn(keys, cosine[...], sine[...]).astype(BF16)
    return low_q, low_k


def owners_of(ids, told, total):
    utts = told.shape[1] // 2
    group = ids[1] ^ (ids[0] >> 1)
    lens = jnp.zeros((2 * utts, utts), F32)
    for f in range(4):
        lens = lens + jnp.where(group == ORDER[f], told[f, :, 0:utts], 0.0)
    _, end, _, end_col = utt_bounds(lens, utts)
    down = lax.broadcasted_iota(jnp.int32, (total, utts), 0).astype(F32)
    across = lax.broadcasted_iota(jnp.int32, (utts, total), 1).astype(F32)
    col = jnp.sum(jnp.where(down >= end, 1.0, 0.0), axis=1, keepdims=True)
    row = jnp.sum(jnp.where(across >= end_col, 1.0, 0.0), axis=0, keepdims=True)
    return col, row


def attend_kernel(ids, qkv, turns, told, out, log_out, owner_row):
    total = turns.shape[0]
    cosine, sine = turns.at[:, 0:128], turns.at[:, 128:256]
    owner_col, owner_row[...] = owners_of(ids, told, total)
    tok = qkv.shape[1]
    queries, keys = rotated(qkv, cosine, sine)
    values = qkv[:, :, 256:384].reshape(total, 128)
    for chunk in range(total // CHUNK):
        rows = slice(chunk * CHUNK, (chunk + 1) * CHUNK)
        same = owner_col == owner_row[:, rows]
        both = []
        for head in range(2):
            lanes = slice(64 * head, 64 * head + 64)
            scores = jnp.where(same, nt(keys[:, lanes], queries[rows, lanes]), -1e30)
            top = jnp.max(scores, axis=0, keepdims=True)
            weights = jnp.exp(scores - top)
            total_w = jnp.sum(weights, axis=0, keepdims=True)
            log_out[head : head + 1, rows] = top + jnp.log(total_w)
            mixed = tn(values[:, lanes], weights.astype(BF16)) * (1.0 / total_w)
            both.append(mixed.T)
        joined = jnp.concatenate(both, axis=1).astype(BF16)
        for block in range(CHUNK // tok):
            out[chunk * (CHUNK // tok) + block] = joined[block * tok : (block + 1) * tok]


def attend_back_kernel(
    ids, qkv, d_att, turns, log_total, told, out, d_keys, d_values, owner_row
):
    total = turns.shape[0]
    cosine, sine = turns.at[:, 0:128], turns.at[:, 128:256]
    owner_col, owner_row[...] = owners_of(ids, told, total)
    tok = qkv.shape[1]
    queries, keys = rotated(qkv, cosine, sine)
    values = qkv[:, :, 256:384].reshape(total, 128)
    back = d_att[...].reshape(total, 128)
    keys_t = [keys[:, 64 * head : 64 * head + 64].astype(F32).T.astype(BF16) for head in range(2)]
    for chunk in range(total // CHUNK):
        rows = slice(chunk * CHUNK, (chunk + 1) * CHUNK)
        same = owner_col == owner_row[:, rows]
        d_queries, k_terms, v_terms = [], [], []
        for head in range(2):
            lanes = slice(64 * head, 64 * head + 64)
            scores = nt(keys[:, lanes], queries[rows, lanes])
            probs = jnp.where(same, jnp.exp(scores - log_total[head : head + 1, rows]), 0.0)
            d_probs = nt(values[:, lanes], back[rows, lanes])
            delta = jnp.sum(probs * d_probs, axis=0, keepdims=True)
            d_scores = (probs * (d_probs - delta)).astype(BF16)
            v_terms.append(nn(probs.astype(BF16), back[rows, lanes]))
            k_terms.append(nn(d_scores, queries[rows, lanes]))
            d_queries.append(nn(keys_t[head], d_scores).T * 0.125)
        k_new = jnp.concatenate(k_terms, axis=1)
        v_new = jnp.concatenate(v_terms, axis=1)
        if chunk == 0:
            d_keys[...] = k_new
            d_values[...] = v_new
        else:
            d_keys[...] += k_new
            d_values[...] += v_new
        d_q = jnp.concatenate(d_queries, axis=1)
        d_q = turn(d_q, cosine[rows, :], -sine[rows, :]).astype(BF16)
        for block in range(CHUNK // tok):
            out[chunk * (CHUNK // tok) + block, :, 0:128] = d_q[block * tok : (block + 1) * tok]
    d_k = turn(d_keys[...], cosine[...], -sine[...]).astype(BF16)
    out[:, :, 128:256] = d_k.reshape(total // tok, tok, 128)
    out[:, :, 256:384] = d_values[...].astype(BF16).reshape(total // tok, tok, 128)


def attended_pairs(ids, blocks, dst, tok, parts):
    pairs = []
    for f in range(4):
        for pair in range(2):
            for part in range(parts):
                pairs.append(
                    (
                        blocks.at[2 * (ids[1] ^ ORDER[f]) + pair, :, pl.ds(part * 128, 128)],
                        dst.at[pl.ds(f * tok, tok), pl.ds((2 * part + pair) * 128, 128)],
                    )
                )
    return pairs


def packed_rows(wide):
    return jnp.concatenate([wide[:, k : k + 256] for k in range(0, wide.shape[1], 256)], axis=0)


def unpacked_rows(rows):
    return jnp.concatenate([rows[k : k + 8] for k in range(0, rows.shape[0], 8)], axis=1)


def cut_skip_kernel(ids, weight, emb, cond_weight, piece):
    rows = weight.shape[0]
    piece[0:rows, :] = weight[:, aligned(ids[1], piece.shape[1])]
    piece[rows:, :] = packed_rows(nn(emb[...], cond_weight[...])).astype(BF16)


def gather_kernel(p0, p1, p2, p3, out):
    rows = (out.shape[0] - 64) // 4
    total = jnp.zeros((64, out.shape[1]), F32)
    for k, piece in enumerate((p0, p1, p2, p3)):
        out[k * rows : (k + 1) * rows, :] = piece[0:rows, :]
        total = total + piece[rows:, :].astype(F32)
    out[4 * rows :, :] = total.astype(BF16)


def join_kernel(left, right, joined):
    width = left.shape[1]
    for k in range(joined.shape[0]):
        joined[k, :, 0:width] = left[...]
        joined[k, :, width:] = right[...]


def near_kernel(even, odd, *outs):
    for k, out in enumerate(outs):
        out[...] = (even[k].astype(F32) + odd[k].astype(F32)).astype(BF16)


def add_kernel(left, right, out, mark):
    out[...] = (left[...].astype(F32) + right[...].astype(F32)).astype(out.dtype)
    mark[...] = jnp.zeros_like(mark)


def add_twice_kernel(left, right, out, again):
    total = (left[...].astype(F32) + right[...].astype(F32)).astype(out.dtype)
    out[...] = total
    again[...] = total


def add_three_kernel(first, second, third, out):
    total = first[...].astype(F32) + second[...].astype(F32) + third[...].astype(F32)
    out[...] = total.astype(out.dtype)


def choose_kernel(ids, own, other, out, mark):
    mine = (ids[0] & 1) == (ids[1] & 1)

    @pl.when(mine)
    def _():
        out[...] = own[...]

    @pl.when(jnp.logical_not(mine))
    def _():
        out[...] = other[...]

    mark[...] = jnp.zeros_like(mark)


def pick_kernel(ids, own, near, far, farther, out):
    z, y = ids[0] >> 1, ids[1] >> 1
    rows = own.shape[0]
    low = z >> 1
    source = (z & 1) == y
    first, second = aligned(low, rows), aligned(1 - low, rows)

    @pl.when(source)
    def _():
        out[first, :] = own[...]
        out[second, :] = far[...]

    @pl.when(jnp.logical_not(source))
    def _():
        out[first, :] = near[...]
        out[second, :] = farther[...]


def copy_kernel(source, out):
    out[...] = source[...]


def stack_kernel(*refs):
    out, mark = refs[-2:]
    for k, ref in enumerate(refs[:-2]):
        out[k] = ref[...]
    mark[...] = jnp.zeros_like(mark)


def cut_qkv_kernel(ids, qkv, piece):
    for block in range(piece.shape[1] // 128):
        piece[:, pl.ds(block * 128, 128)] = qkv[:, aligned(4 * block + ids[1], 128)]


def cut_feed_kernel(ids, up, down, piece, sem):
    fetch = pltpu.make_async_copy(down.at[aligned(ids[1], 128), :], piece.at[:, up.shape[1] // 4 :], sem)
    fetch.start()
    for block in range(up.shape[1] // 512):
        piece[:, pl.ds(block * 128, 128)] = up[:, aligned(4 * block + ids[1], 128)]
    fetch.wait()


def utt_bounds(told, utts):
    row = lax.broadcasted_iota(jnp.int32, (utts, utts), 0)
    col = lax.broadcasted_iota(jnp.int32, (utts, utts), 1)
    lens = told[utts : utts + 1, 0:utts]
    spread = jnp.broadcast_to(lens, (utts, utts))
    lens_col = jnp.sum(jnp.where(row == col, spread, 0.0), axis=1, keepdims=True)
    ends = jnp.sum(jnp.where(row <= col, lens_col, 0.0), axis=0, keepdims=True)
    ends_col = jnp.sum(jnp.where(col <= row, spread, 0.0), axis=1, keepdims=True)
    return ends - lens, ends, ends_col - lens_col, ends_col


def scale_of(ids, told, tok, first_col, width):
    utts = told.shape[0] // 2
    begin, end, _, _ = utt_bounds(told, utts)
    frame = (ids[0] * tok + lax.broadcasted_iota(jnp.int32, (tok, utts), 0)).astype(F32)
    onehot = jnp.where((frame >= begin) & (frame < end), 1.0, 0.0).astype(BF16)
    cond = told[0:utts, first_col : first_col + width]
    high = cond.astype(BF16)
    rest = cond - high.astype(F32)
    low = rest.astype(BF16)
    return 1.0 + (nn(onehot, high) + nn(onehot, low))


def utt_picks(ids, told, tok):
    utts = told.shape[0] // 2
    _, _, begin, end = utt_bounds(told, utts)
    frame = (ids[0] * tok + lax.broadcasted_iota(jnp.int32, (utts, tok), 1)).astype(F32)
    return jnp.where((frame >= begin) & (frame < end), 1.0, 0.0).astype(BF16)


def project_kernel(ids, blocks, weight, keep, send, attended, sems):
    tok = blocks.shape[1]
    run_copies(attended_pairs(ids, blocks, attended, tok, 1), sems)
    send[...] = nn(attended[2 * tok :, :], weight[...]).astype(BF16)
    keep[...] = nn(attended[0 : 2 * tok, :], weight[...])


def residual_kernel(ids, hidden, part, other, told, h_one_out, normed_out):
    tok = hidden.shape[0] // 2
    for f in range(2):
        rows, swap = pl.ds(f * tok, tok), pl.ds((1 - f) * tok, tok)
        h_one = hidden[rows, :].astype(F32) + part[rows, :].astype(F32) + other[swap, :].astype(F32)
        inverse = lax.rsqrt(jnp.mean(h_one * h_one, axis=1, keepdims=True) + EPS)
        h_one_out[rows, :] = h_one
        scale = scale_of(ids, told.at[f], tok, h_one.shape[1], h_one.shape[1])
        normed_out[rows, :] = (h_one * inverse * scale).astype(BF16)


def gelu_parts(pre):
    size = jnp.abs(pre)
    decay = jnp.exp(-0.5 * pre * pre)
    t = 1.0 / (1.0 + (0.3275911 * 2.0**-0.5) * size)
    series = t * (0.254829592 + t * (-0.284496736 + t * (1.421413741 + t * (-1.453152027 + t * 1.061405429))))
    tail = 0.5 * series * decay
    half = jnp.where(pre < 0.0, tail, 1.0 - tail)
    return pre * half, half + pre * decay * ((2.0 * math.pi) ** -0.5)


def feed_kernel(ids, *refs):
    normed, normed_c, cots, weight = refs[:4]
    act_out, d_pre_out, keep, send = refs[4:]
    tok = cots.shape[1]
    hidden = act_out.shape[1]
    for f in range(4):
        block = pl.ds(f * tok, tok)
        rows = pl.ds((f % 2) * tok, tok)
        pre = nn((normed, normed_c)[f // 2][rows, :], weight[:, 0:hidden])
        act, slope = gelu_parts(pre)
        act_out[block, :] = act.astype(BF16)
        d_pre = (nt(cots[f], weight[:, hidden:]) * slope).astype(BF16)
        d_pre_out[block, :] = d_pre
        d_normed = nt(d_pre, weight[:, 0:hidden])
        if f < 2:
            keep[block, :] = d_normed
        else:
            send[rows, :] = d_normed.astype(BF16)


def feed_grad_kernel(normed, normed_c, cots, act, d_pre, out, held, sems):
    tok = cots.shape[1]
    run_copies([(normed, held.at[pl.ds(0, 2 * tok), :]), (normed_c, held.at[pl.ds(2 * tok, 2 * tok), :])], sems)
    cots_all = cots[...].reshape(4 * tok, cots.shape[2])
    cols = act.shape[1]
    for r in range(8):
        block = pl.ds(r * 128, 128)
        out[block, 0:cols] = tn(held[:, block], d_pre[...]).astype(BF16)
        out[block, cols:] = tn(act[:, block], cots_all).astype(BF16)


def feed_out_kernel(act, weight, keep, send):
    half = keep.shape[0]
    hidden = act.shape[1]
    keep[...] = nn(act[0:half, :], weight[:, hidden:])
    send[...] = nn(act[half:, :], weight[:, hidden:]).astype(BF16)


def norm_back(hidden, scale, d_normed):
    inverse = lax.rsqrt(jnp.mean(hidden * hidden, axis=1, keepdims=True) + EPS)
    y = hidden * inverse
    d_y = d_normed * scale
    d_hidden = inverse * (d_y - y * jnp.mean(d_y * y, axis=1, keepdims=True))
    return d_hidden, d_normed * y


def norm_back_kernel(first_col, ids, hidden, part, other, base, told, low_out, sums_out):
    tok = hidden.shape[0] // 2
    width = hidden.shape[1]
    for f in range(2):
        rows, swap = pl.ds(f * tok, tok), pl.ds((1 - f) * tok, tok)
        d_normed = part[rows, :].astype(F32) + other[swap, :].astype(F32)
        scale = scale_of(ids, told.at[f], tok, first_col, width)
        d_hidden, d_scale = norm_back(hidden[rows, :].astype(F32), scale, d_normed)
        added = base[f].astype(F32) + d_hidden
        low_out[rows, :] = added.astype(low_out.dtype)
        if f == 0:
            sums_out[...] = nn(utt_picks(ids, told.at[0], tok), d_scale.astype(BF16))


def d_attended_kernel(ids, d_h, d_h_c, weight, packed):
    tok = packed.shape[1]
    for f in range(4):
        rows = pl.ds((f % 2) * tok, tok)
        part = nt((d_h, d_h_c)[f // 2][rows, :], weight[...]).astype(BF16)
        group = ids[1] ^ ORDER[f]
        for pair in range(2):
            packed[2 * group + pair] = part[:, pair * 128 : (pair + 1) * 128]


def qkv_back_kernel(ids, blocks, weight, keep, send, joined, sems):
    tok = blocks.shape[1]
    run_copies(attended_pairs(ids, blocks, joined, tok, 3), sems)
    half = keep.shape[0]
    send[...] = nt(joined[half:, :], weight[...]).astype(BF16)
    keep[...] = nt(joined[0:half, :], weight[...])


def qkv_grad_kernel(ids, normed, joined, d_h, d_h_c, a0, a2, a1, a3, even, odd, attended, sems):
    tok = a0.shape[0] // 4
    half = d_h.shape[0]
    pairs = []
    for q, piece in enumerate((a0, a1, a2, a3)):
        for f in range(4):
            for pair in range(2):
                pairs.append(
                    (
                        piece.at[pl.ds(ORDER[ORDER[f] ^ q] * tok, tok), pl.ds(pair * 128, 128)],
                        attended.at[pl.ds(f * tok, tok), aligned((ids[1] ^ q) + 4 * pair, 128)],
                    )
                )
    run_copies(pairs, sems)
    cols = joined.shape[1]
    mine = aligned(ids[1], 256)
    for r in (1, 3, 5, 7, 0, 2, 4, 6):
        block = aligned(ids[0] ^ r, 128)
        target = (even, odd)[r % 2]
        target[r // 2, :, 0:cols] = tn(normed[:, block], joined[...]).astype(BF16)
        target[r // 2, :, cols:] = (
            tn(attended[0:half, block], d_h[:, mine]) + tn(attended[half:, block], d_h_c[:, mine])
        ).astype(BF16)


def skip_back_kernel(ids, d_h, d_h_c, inputs, sums_attn, sums_ffn, even, odd, sums, held, sems):
    tok = inputs.shape[1]
    run_copies(frame_blocks(ids, inputs, held), sems)
    mine = aligned(ids[1], 256)
    near, far = d_h[:, mine], d_h_c[:, mine]
    half = 2 * tok
    for r in (1, 3, 5, 7, 0, 2, 4, 6):
        block = aligned(ids[0] ^ r, 256)
        grad = (tn(held[0:half, block], near) + tn(held[half:, block], far)).astype(BF16)
        if r % 2:
            odd[(r // 2) * 256 : (r // 2) * 256 + 256, :] = grad
        else:
            even[r // 2] = grad
    low = packed_rows(jnp.concatenate([sums_attn[...], sums_ffn[...]], axis=1)).astype(BF16)
    odd[1024:, :] = low
    sums[...] = low


def skip_near_kernel(even, sums, arrived, *outs):
    both = (sums[...].astype(F32) + arrived[1024:, :].astype(F32)).astype(BF16)
    for k, out in enumerate(outs):
        out[0:256, :] = (even[k].astype(F32) + arrived[k * 256 : (k + 1) * 256, :].astype(F32)).astype(BF16)
        out[256:, :] = both


def in_back_kernel(ids, d_h, near, far, in_out, skip_out):
    tok, width = in_out.shape
    total = jnp.zeros((tok, 2 * width), F32)
    for q in range(4):
        weight = (near, far)[q % 2].at[q // 2]
        total = total + nt(d_h[0:tok, aligned(ids[1] ^ q, 256)], weight[...])
    in_out[...] = total[:, 0:width].astype(BF16)
    skip_out[...] = total[:, width:].astype(BF16)


def spread_feed_kernel(ids, near, far, up_o, down_o):
    hidden = near.shape[2] - down_o.shape[1]
    for q in range(4):
        part = ids[1] ^ q
        feed = (near, far)[q % 2].at[q // 2]
        for block in range(hidden // 128):
            up_o[:, aligned(4 * block + part, 128)] = feed[:, pl.ds(block * 128, 128)].astype(F32)
        down_o[aligned(part, 128), :] = feed[:, hidden:].astype(F32)


def last_kernel(p0, p1, p2, p3, q0, q1, q2, q3, out):
    qkv = q0[...].astype(F32) + q1[...].astype(F32) + q2[...].astype(F32) + q3[...].astype(F32)
    skip = p0[...].astype(F32) + p1[...].astype(F32) + p2[...].astype(F32) + p3[...].astype(F32)
    out[:, 0:1024] = qkv.astype(BF16)
    out[:, 1024:1280] = skip[0:128].astype(BF16)
    out[:, 1280:1536] = skip[128:256].astype(BF16)
    out[0:64, 1536:1792] = skip[256:].astype(BF16)
    out[64:, 1536:1792] = jnp.zeros((64, 256), BF16)


def spread_kernel(ids, g0, g1, g2, g3, emb, qkv_o, out_o, skip_o, cond_o):
    rows = qkv_o.shape[0]
    utts = emb.shape[0] // 4
    for q in range(4):
        part = ids[1] ^ q
        piece = (g0, g2, g1, g3)[q]
        for block in range(6):
            qkv_o[:, aligned(4 * block + part, 128)] = piece[0:rows, pl.ds(block * 128, 128)].astype(F32)
        out_o[:, aligned(part, 256)] = piece[0:rows, pl.ds(768, 256)].astype(F32)
        skip_o[0:rows, aligned(part, 256)] = piece[0:rows, pl.ds(1024, 256)].astype(F32)
        skip_o[rows:, aligned(part, 256)] = piece[0:rows, pl.ds(1280, 256)].astype(F32)
    total = jnp.zeros(cond_o.shape, F32)
    for f in range(4):
        sums = unpacked_rows((g0, g1, g2, g3)[f][0:64, 1536:1792].astype(F32)).astype(BF16)
        total = total + tn(emb[f * utts : (f + 1) * utts, :], sums)
    cond_o[...] = total


def stack(arrays, deps=()):
    shape = (len(arrays),) + arrays[0].shape
    return call(stack_kernel, [sds(shape, arrays[0].dtype), MARK], [VMEM] * len(arrays), [], list(arrays), deps=deps)


def around(piece):
    return [piece, from_grp(piece, 2), from_grp(piece, 1), from_grp(piece, 3)]


def gather_groups(piece):
    along_y = from_grp(piece, 2)
    return [piece, along_y, from_grp(piece, 1), from_grp(along_y, 1)]


def gather_pairs(piece, deps=()):
    near, _ = stack([piece, from_grp(piece, 2)], deps)
    return near, from_grp(near, 1)


def scatter_near(even, odd, deps):
    arrived = from_seq(odd, 1)
    return call(near_kernel, [sds(even.shape[1:], BF16)] * 4, [VMEM] * 2, [], [even, arrived], deps=deps)


def by_mask(pieces):
    return [pieces[0], pieces[2], pieces[1], pieces[3]]


def halves_sum(keep, send):
    kept, sent = call(
        add_twice_kernel, [sds(keep.shape, BF16)] * 2, [VMEM] * 2, [], [keep, from_grp(send, 1)]
    )
    return kept, from_grp(sent, 2)


def add_two(left, right, deps=()):
    return call(add_kernel, [sds(left.shape, BF16), MARK], [VMEM] * 2, [], [left, right], deps=deps)


def exchange(array, cols):
    return lax.all_to_all(array, "seq", 0, 0, tiled=True)


def out_moves(mask, keep):
    pairs = []
    for t in range(4):
        for slot in range(8):
            if keep(slot, t):
                pairs.append((t * 8 + slot, t * 8 + (slot ^ mask)))
    return pairs


def out_along_z(piece):
    def holds(slot, t):
        return (slot & 1) == (t & 1) and ((slot >> 1) & 1) == (t >> 1)

    return [lax.ppermute(piece, ("grp", "seq"), out_moves(2 * k, holds)) for k in range(1, 4)]


def out_along_x(rows):
    return lax.ppermute(rows, ("grp", "seq"), out_moves(1, lambda slot, t: (slot & 1) == (t & 1)))


def tp_body(
    hidden_in, skips, lengths, times, skip_weight, cond_weight, qkv_weight, out_weight,
    up_weight, down_weight, cotangent,
):
    tok, width = hidden_in.shape
    ff = up_weight.shape[1]
    frames = 8 * tok
    slot = lax.axis_index("seq")
    part = lax.axis_index("grp")
    ids = jnp.stack([slot, part]).astype(jnp.int32)
    sem = pltpu.SemaphoreType.DMA

    half_width = width // 2
    rows_here = cond_weight.shape[0]
    utts = times.shape[1]

    def embed_here(time_rows):
        column = (slot * rows_here + jnp.arange(rows_here, dtype=jnp.int32)) % half_width
        freqs = jnp.exp(-math.log(10000.0) * column.astype(F32) / half_width)
        angles = time_rows[:, None] * freqs[None, :]
        return jnp.where(slot * rows_here < half_width, jnp.sin(angles), jnp.cos(angles)).astype(BF16)

    skip_rows = skip_weight.shape[0]
    (skip_piece,) = call(
        cut_skip_kernel,
        [sds((skip_rows + 64, 256), BF16)],
        [SMEM] + [VMEM] * 3,
        [],
        [ids, skip_weight, embed_here(times[0].astype(F32)), cond_weight],
    )
    (qkv_piece,) = call(cut_qkv_kernel, [sds((128, 768), BF16)], [SMEM, VMEM], [], [ids, qkv_weight])
    (skip_same,) = call(
        gather_kernel,
        [sds((4 * skip_rows + 64, 256), BF16)],
        [VMEM] * 4,
        [],
        [skip_piece] + [from_seq(skip_piece, 2 * k) for k in range(1, 4)],
        deps=[qkv_piece],
    )
    skip_other = from_seq(skip_same, 1)
    (joined,) = call(
        join_kernel, [sds((4, tok, 2 * width), BF16)], [VMEM] * 2, [], [hidden_in, skips], deps=[skip_piece]
    )
    inputs = lax.all_to_all(joined, "grp", 0, 0, tiled=True)
    w_qkv = lax.all_gather(qkv_piece, "seq", axis=0, tiled=True)
    (feed_piece,) = call(
        cut_feed_kernel,
        [sds((128, ff // 4 + width), BF16)],
        [SMEM, VMEM, ANY],
        [sem],
        [ids, up_weight, down_weight],
        deps=[qkv_piece],
    )
    w_feed = lax.all_gather(feed_piece, "seq", axis=0, tiled=True)

    counts = jnp.stack([lengths[0] >> 5, lengths[0] & 31, times[0] >> 5, times[0] & 31])
    notes = jnp.zeros((16, 256), BF16).at[0:4, 0:utts].set(counts.astype(BF16))

    (out_piece,) = call(copy_kernel, [sds(out_weight.shape, BF16)], [VMEM], [], [out_weight], deps=[skip_same])
    out_came = out_along_z(out_piece)

    inverse = jnp.exp(-math.log(10000.0) * jnp.arange(32, dtype=F32) / 32)
    turn_angles = jnp.arange(frames, dtype=F32)[:, None] * inverse[None, :]
    cos_half, sin_half = jnp.cos(turn_angles), jnp.sin(turn_angles)
    turns = jnp.concatenate([cos_half] * 4 + [-sin_half, sin_half] * 2, axis=1)

    h_cols, w_skip = call(
        h_zero_kernel,
        [sds((4 * tok + 80, 256), BF16), sds((2 * width, 256), BF16)],
        [SMEM] + [ANY] * 3 + [VMEM],
        [
            pltpu.VMEM((4 * tok, 2 * width), BF16),
            pltpu.VMEM((2 * width, 256), BF16),
            pltpu.VMEM((2, 64, 256), BF16),
            sem((14,)),
        ],
        [ids, inputs, skip_same, skip_other, notes],
        deps=out_came,
        cost_us=100.0,
    )
    h_pieces = gather_groups(h_cols)
    h_pieces = [h_pieces[0], h_pieces[2], h_pieces[1], h_pieces[3]]
    normed, h_zero, packed, told = call(
        qkv_kernel,
        [
            sds((4 * tok, width), BF16),
            sds((2 * tok, width), BF16),
            sds((8, tok, 384), BF16),
            sds((4, 2 * utts, 2 * width), F32),
        ],
        [SMEM] + [ANY] * 4 + [VMEM],
        [pltpu.VMEM((4 * tok, width), BF16), pltpu.VMEM((4, 80, 256), BF16), sem((20,))],
        [ids] + h_pieces + [w_qkv],
    )
    emb_all = embed_here(told[:, utts + 1, :utts].reshape(4 * utts))
    qkv = exchange(packed, 384)
    (out_picked,) = call(
        pick_kernel, [sds((2 * tok, width), BF16)], [SMEM] + [VMEM] * 4, [], [ids, out_piece] + out_came
    )
    (w_skip,) = call(copy_kernel, [sds(w_skip.shape, BF16)], [VMEM], [], [w_skip], deps=[packed])
    skip_y = from_grp(w_skip, 2)
    w_out, out_mark = call(
        choose_kernel,
        [sds((2 * tok, width), BF16), MARK],
        [SMEM] + [VMEM] * 2,
        [],
        [ids, out_picked, out_along_x(out_picked)],
    )
    skip_near, skip_mark = stack([w_skip, skip_y], [packed])
    skip_far = from_grp(skip_near, 1)
    mixed, log_total = call(
        attend_kernel,
        [sds((8, tok, 128), BF16), sds((2, frames), F32)],
        [SMEM] + [VMEM] * 3,
        [pltpu.VMEM((1, frames), F32)],
        [ids, qkv, turns, told],
        deps=[out_mark, skip_mark],
    )
    attended_blocks = exchange(mixed, 128)
    (cot_piece,) = call(
        copy_kernel, [sds((tok, width), BF16)], [VMEM], [], [cotangent], deps=[mixed]
    )
    cots, cot_mark = stack(around(cot_piece))
    keep, send, attended = call(
        project_kernel,
        [
            sds((2 * tok, width), F32),
            sds((2 * tok, width), BF16),
            sds((4 * tok, 256), BF16),
        ],
        [SMEM, ANY, VMEM],
        [sem((8,))],
        [ids, attended_blocks, w_out],
        deps=[cot_mark],
    )
    h_part, h_part_y = halves_sum(keep, send)
    h_one, normed_two = call(
        residual_kernel,
        [sds((2 * tok, width), F32), sds((2 * tok, width), BF16)],
        [SMEM] + [VMEM] * 4,
        [],
        [ids, h_zero, h_part, h_part_y, told],
    )
    normed_two_c = from_grp(normed_two, 1)
    quarter = ff // 4
    act, d_pre, keep, send = call(
        feed_kernel,
        [
            sds((4 * tok, quarter), BF16),
            sds((4 * tok, quarter), BF16),
            sds((2 * tok, width), F32),
            sds((2 * tok, width), BF16),
        ],
        [SMEM] + [VMEM] * 4,
        [],
        [ids, normed_two, normed_two_c, cots, w_feed],
    )

    d_part, d_part_y = halves_sum(keep, send)
    (feed_terms,) = call(
        feed_grad_kernel,
        [sds((width, quarter + width), BF16)],
        [ANY] * 2 + [VMEM] * 3,
        [pltpu.VMEM((4 * tok, width), BF16), sem((2,))],
        [normed_two, normed_two_c, cots, act, d_pre],
        deps=[d_part],
    )
    out_keep, out_send = call(
        feed_out_kernel,
        [sds((2 * tok, width), F32), sds((2 * tok, width), BF16)],
        [VMEM, VMEM],
        [],
        [act, w_feed],
        deps=[feed_terms],
    )
    d_h_one, sums_ffn = call(
        functools.partial(norm_back_kernel, width),
        [sds((2 * tok, width), BF16), sds((utts, width), F32)],
        [SMEM] + [VMEM] * 5,
        [],
        [ids, h_one, d_part, d_part_y, cots, told],
        deps=[out_send],
        cost_us=100.0,
    )
    d_h_one_c = from_grp(d_h_one, 1)
    (d_att_packed,) = call(
        d_attended_kernel,
        [sds((8, tok, 128), BF16)],
        [SMEM, VMEM, VMEM, VMEM],
        [],
        [ids, d_h_one, d_h_one_c, w_out],
    )
    d_att = exchange(d_att_packed, 128)

    feed_own = lax.psum_scatter(feed_terms, "seq", scatter_dimension=0, tiled=True)
    att_pieces = around(attended)
    out_part, out_done = add_two(out_keep, from_grp(out_send, 1), att_pieces[1:])
    (d_packed,) = call(
        attend_back_kernel,
        [sds((8, tok, 384), BF16)],
        [SMEM] + [VMEM] * 5,
        [pltpu.VMEM((frames, 128), F32), pltpu.VMEM((frames, 128), F32), pltpu.VMEM((1, frames), F32)],
        [ids, qkv, d_att, turns, log_total, told],
        deps=[out_done],
    )
    d_qkv_blocks = exchange(d_packed, 384)
    (block_out,) = call(
        add_three_kernel,
        [sds((tok, width), BF16)],
        [VMEM] * 3,
        [],
        [h_one[:tok], out_part[:tok], from_grp(out_part[tok:], 2)],
        deps=[d_packed],
    )
    keep, send, d_qkv = call(
        qkv_back_kernel,
        [sds((2 * tok, width), F32), sds((2 * tok, width), BF16), sds((4 * tok, 768), BF16)],
        [SMEM, ANY, VMEM],
        [sem((24,))],
        [ids, d_qkv_blocks, w_qkv],
        deps=[block_out],
    )
    d_part, d_part_y = halves_sum(keep, send)
    qkv_even, qkv_odd = call(
        qkv_grad_kernel,
        [sds((4, 128, 1024), BF16)] * 2,
        [SMEM] + [VMEM] * 4 + [ANY] * 4,
        [pltpu.VMEM((4 * tok, width), BF16), sem((32,))],
        [ids, normed, d_qkv, d_h_one, d_h_one_c] + att_pieces,
        deps=[d_part],
    )
    d_h_zero, sums_attn = call(
        functools.partial(norm_back_kernel, 0),
        [sds((2 * tok, width), BF16), sds((utts, width), F32)],
        [SMEM] + [VMEM] * 5,
        [],
        [ids, h_zero, d_part, d_part_y, d_h_one.reshape(2, tok, width), told],
        deps=[qkv_odd],
    )
    d_h_zero_c = from_grp(d_h_zero, 1)
    skip_even, skip_odd, skip_sums = call(
        skip_back_kernel,
        [sds((4, 256, 256), BF16), sds((1024 + 64, 256), BF16), sds((64, 256), BF16)],
        [SMEM, VMEM, VMEM, ANY, VMEM, VMEM],
        [pltpu.VMEM((4 * tok, 2 * width), BF16), sem((4,))],
        [ids, d_h_zero, d_h_zero_c, inputs, sums_attn, sums_ffn],
    )
    qkv_near = scatter_near(qkv_even, qkv_odd, [skip_odd])
    qkv_came = [from_seq(qkv_near[k], 2 * k) for k in range(1, 4)]
    last_near = call(
        skip_near_kernel,
        [sds((256 + 64, 256), BF16)] * 4,
        [VMEM] * 3,
        [],
        [skip_even, skip_sums, from_seq(skip_odd, 1)],
        deps=[qkv_near[0]],
    )
    last_came = [from_seq(last_near[k], 2 * k) for k in range(1, 4)]
    in_grad, skip_grad = call(
        in_back_kernel,
        [sds((tok, width), BF16)] * 2,
        [SMEM] + [VMEM] * 3,
        [],
        [ids, d_h_zero, skip_near, skip_far],
        deps=qkv_came + [last_near[0]],
    )
    (last_own,) = call(
        last_kernel,
        [sds((128, 1792), BF16)],
        [VMEM] * 8,
        [],
        [last_near[0]] + last_came + [qkv_near[0]] + qkv_came,
        deps=[in_grad],
    )
    last_all = gather_groups(last_own)
    feed_near, feed_far = gather_pairs(feed_own, [last_own])
    up_grad, down_grad = call(
        spread_feed_kernel,
        [sds((128, ff), F32), sds((ff // 8, width), F32)],
        [SMEM] + [VMEM] * 2,
        [],
        [ids, feed_near, feed_far],
    )
    qkv_grad, out_grad, skip_grad_w, cond_grad = call(
        spread_kernel,
        [
            sds((128, 3 * width), F32),
            sds((128, width), F32),
            sds((256, width), F32),
            sds((rows_here, 2 * width), F32),
        ],
        [SMEM] + [VMEM] * 5,
        [],
        [ids] + last_all + [emb_all],
        deps=[up_grad],
    )
    return (
        block_out, in_grad, skip_grad, skip_grad_w, cond_grad, qkv_grad,
        out_grad, up_grad, down_grad,
    )


def solution(mesh):
    placed = (
        P(("grp", "seq"), None),
        P(("grp", "seq"), None),
        P("grp", None),
        P("grp", None),
        P("seq", None),
        P("seq", None),
        P("seq", None),
        P("seq", None),
        P("seq", None),
        P("seq", None),
        P(("grp", "seq"), None),
    )
    body = tp_body if (mesh.shape["grp"], mesh.shape["seq"]) == (4, 8) else plain_body
    return jax.shard_map(
        body,
        mesh=mesh,
        in_specs=placed,
        out_specs=(
            P(("grp", "seq"), None),
            P(("grp", "seq"), None),
            P(("grp", "seq"), None),
            P("seq", None),
            P("seq", None),
            P("seq", None),
            P("seq", None),
            P("seq", None),
            P("seq", None),
        ),
        check_vma=False,
    )
```

```python
import functools
import math

import jax
import jax.numpy as jnp
from jax import lax
from jax.experimental import pallas as pl
from jax.experimental.pallas import tpu as pltpu
from jax.sharding import PartitionSpec as P

HEADS = 16


EPS = 1e-06


def contract(left, right, left_dim, right_dim):
    return lax.dot_general(
        left, right, (((left_dim,), (right_dim,)), ((), ())), preferred_element_type=jnp.float32
    )


def matmul(left, right):
    return jnp.dot(left, right, preferred_element_type=jnp.float32)


def owner_of(frames, utt_ends):
    return jnp.sum((frames[:, None] >= utt_ends[None, :]).astype(jnp.int32), axis=1)


def same_owner(query_owner, key_owner):
    return (query_owner[:, None] == key_owner[None, :])[:, None, :]


def embed_steps(time_steps, model_width):
    half_width = model_width // 2
    freqs = jnp.exp(-math.log(10000.0) * jnp.arange(half_width, dtype=jnp.float32) / half_width)
    angles = time_steps[:, None] * freqs[None, :]
    return jnp.concatenate([jnp.sin(angles), jnp.cos(angles)], axis=1)


def rotate(vectors, positions, head_count, direction):
    tok_rows, model_width = vectors.shape
    head_size = model_width // head_count
    half_size = head_size // 2
    inverse = jnp.exp(-math.log(10000.0) * jnp.arange(half_size, dtype=jnp.float32) / half_size)
    angles = positions[:, None] * inverse[None, :]
    cosine = jnp.cos(angles)[:, None, :]
    sine = direction * jnp.sin(angles)[:, None, :]
    split = vectors.reshape(tok_rows, head_count, head_size)
    first_half = split[..., :half_size]
    second_half = split[..., half_size:]
    turned = jnp.concatenate(
        [first_half * cosine - second_half * sine, first_half * sine + second_half * cosine],
        axis=-1,
    )
    return turned.reshape(tok_rows, model_width)


def scale_norm(hidden, cond_part):
    return (
        hidden
        * lax.rsqrt(jnp.mean(hidden * hidden, axis=1, keepdims=True) + EPS)
        * (1.0 + cond_part)
    )


def over_blocks(update, running, arrays, first_row, block_cap):
    row_count = arrays[0].shape[0]
    block_size = math.gcd(row_count, block_cap)
    number = row_count // block_size
    if number == 1:
        return update(running, arrays, first_row)
    stacked = tuple((array.reshape((number, block_size) + array.shape[1:]) for array in arrays))
    offsets = first_row + block_size * jnp.arange(number, dtype=jnp.int32)

    def over_scan_step(inner, scan_in):
        return (update(inner, scan_in[0], scan_in[1]), None)

    result, unused = lax.scan(over_scan_step, running, (stacked, offsets))
    return result


def grad_terms(
    q_heads, do_heads, log_total, row_delta, key_heads, value_heads, same_utt, score_scale
):
    scores = (
        jnp.einsum("qhd,khd->qhk", q_heads, key_heads, preferred_element_type=jnp.float32)
        * score_scale
    )
    probs = jnp.where(same_utt, jnp.exp(scores - log_total[..., None]), 0.0)
    d_probs = jnp.einsum("qhd,khd->qhk", do_heads, value_heads, preferred_element_type=jnp.float32)
    d_scores = (probs * (d_probs - row_delta[..., None]) * score_scale).astype(jnp.bfloat16)
    return (probs.astype(jnp.bfloat16), d_scores)


def scatter_first(after, grad):
    return lax.optimization_barrier(
        (after, lax.psum_scatter(grad, "seq", scatter_dimension=0, tiled=True))
    )


def plain_body(
    hidden_in,
    skips,
    lengths,
    times,
    skip_weight,
    cond_weight,
    qkv_weight,
    out_weight,
    up_weight,
    down_weight,
    cotangent,
):
    tok_rows, model_width = hidden_in.shape
    head_count = HEADS
    head_size = model_width // head_count
    score_scale = head_size ** (-0.5)
    first_frame = lax.axis_index("seq") * tok_rows
    utt_lengths = lengths[0]
    utt_ends = jnp.cumsum(utt_lengths)
    starts = utt_ends - utt_lengths
    frames = first_frame + jnp.arange(tok_rows, dtype=jnp.int32)
    query_owner = owner_of(frames, utt_ends)
    onehot = query_owner[:, None] == jnp.arange(utt_lengths.shape[0], dtype=jnp.int32)[None, :]
    positions = (frames - jnp.sum(jnp.where(onehot, starts[None, :], 0), axis=1)).astype(
        jnp.float32
    )
    time_steps = jnp.sum(jnp.where(onehot, times[0][None, :], 0), axis=1).astype(jnp.float32)
    gathered = (
        lax.all_gather(skip_weight, "seq", axis=0, tiled=True),
        lax.all_gather(cond_weight, "seq", axis=0, tiled=True),
        lax.all_gather(qkv_weight, "seq", axis=0, tiled=True),
        lax.all_gather(out_weight, "seq", axis=0, tiled=True),
        lax.all_gather(up_weight, "seq", axis=0, tiled=True),
        lax.all_gather(down_weight, "seq", axis=0, tiled=True),
    )
    w_skip, w_cond, w_qkv, w_out, w_up, w_down = gathered
    h_zero = matmul(hidden_in, w_skip[:model_width]) + matmul(skips, w_skip[model_width:])
    emb = embed_steps(time_steps, model_width).astype(jnp.bfloat16)
    cond = matmul(emb, w_cond)
    cond_attn = cond[:, :model_width]
    cond_ffn = cond[:, model_width:]
    normed = scale_norm(h_zero, cond_attn).astype(jnp.bfloat16)
    qkv = matmul(normed, w_qkv)
    queries = rotate(qkv[:, :model_width], positions, head_count, 1.0).astype(jnp.bfloat16)
    keys = rotate(qkv[:, model_width : 2 * model_width], positions, head_count, 1.0).astype(
        jnp.bfloat16
    )
    values = qkv[:, 2 * model_width :].astype(jnp.bfloat16)
    q_heads = queries.reshape(tok_rows, head_count, head_size)

    def forward_step(running, blocks, first_row):
        weighted, run_max, run_sum = running
        key_heads = blocks[0].reshape(-1, head_count, head_size)
        value_heads = blocks[1].reshape(-1, head_count, head_size)
        key_owner = owner_of(first_row + jnp.arange(key_heads.shape[0], dtype=jnp.int32), utt_ends)
        same_utt = same_owner(query_owner, key_owner)
        scores = (
            jnp.einsum("qhd,khd->qhk", q_heads, key_heads, preferred_element_type=jnp.float32)
            * score_scale
        )
        new_max = jnp.maximum(run_max, jnp.max(jnp.where(same_utt, scores, -1e30), axis=-1))
        weights_b = jnp.where(same_utt, jnp.exp(scores - new_max[..., None]), 0.0)
        factor = jnp.exp(run_max - new_max)
        run_sum = run_sum * factor + jnp.sum(weights_b, axis=-1)
        weighted = weighted * factor[..., None] + jnp.einsum(
            "qhk,khd->qhd",
            weights_b.astype(jnp.bfloat16),
            value_heads,
            preferred_element_type=jnp.float32,
        )
        return (weighted, new_max, run_sum)

    start_state = (
        jnp.zeros((tok_rows, head_count, head_size), jnp.float32),
        jnp.full((tok_rows, head_count), -1e30, jnp.float32),
        jnp.zeros((tok_rows, head_count), jnp.float32),
    )
    weighted, run_max, run_sum = over_blocks(
        forward_step,
        start_state,
        (
            lax.all_gather(keys, "seq", axis=0, tiled=True),
            lax.all_gather(values, "seq", axis=0, tiled=True),
        ),
        jnp.int32(0),
        1024,
    )
    attended_full = (weighted / run_sum[..., None]).reshape(tok_rows, model_width)
    log_total = run_max + jnp.log(run_sum)
    attended = attended_full.astype(jnp.bfloat16)
    h_one = h_zero + matmul(attended, w_out)
    normed_two = scale_norm(h_one, cond_ffn).astype(jnp.bfloat16)
    pre = matmul(normed_two, w_up)
    act = jax.nn.gelu(pre, approximate=False).astype(jnp.bfloat16)
    block_out = (h_one + matmul(act, w_down)).astype(jnp.bfloat16)
    regathered = (
        lax.all_gather(skip_weight, "seq", axis=0, tiled=True),
        lax.all_gather(cond_weight, "seq", axis=0, tiled=True),
        lax.all_gather(qkv_weight, "seq", axis=0, tiled=True),
        lax.all_gather(out_weight, "seq", axis=0, tiled=True),
        lax.all_gather(up_weight, "seq", axis=0, tiled=True),
        lax.all_gather(down_weight, "seq", axis=0, tiled=True),
    )
    w_skip, w_cond, w_qkv, w_out, w_up, w_down = regathered
    d_act = contract(cotangent, w_down, 1, 1)
    d_act, shard_down = scatter_first(d_act, contract(act, cotangent, 0, 0))
    unused, gelu_back = jax.vjp(lambda inner: jax.nn.gelu(inner, approximate=False), pre)
    d_pre = gelu_back(d_act)[0].astype(jnp.bfloat16)
    d_pre, shard_up = scatter_first(d_pre, contract(normed_two, d_pre, 0, 0))
    d_normed_two = contract(d_pre, w_up, 1, 1)
    unused, norm_back_two = jax.vjp(scale_norm, h_one, cond_ffn)
    d_h_norm, d_cond_ffn = norm_back_two(d_normed_two)
    d_h_one = cotangent.astype(jnp.float32) + d_h_norm
    d_h_low = d_h_one.astype(jnp.bfloat16)
    d_h_low, shard_out = scatter_first(d_h_low, contract(attended, d_h_low, 0, 0))
    d_attended = contract(d_h_low, w_out, 1, 1).astype(jnp.bfloat16)
    row_delta = jnp.sum(
        (d_attended.astype(jnp.float32) * attended_full).reshape(tok_rows, head_count, head_size),
        axis=-1,
    )
    do_heads = d_attended.reshape(tok_rows, head_count, head_size)
    keys_all, values_all = (
        lax.all_gather(keys, "seq", axis=0, tiled=True),
        lax.all_gather(values, "seq", axis=0, tiled=True),
    )
    key_total = keys_all.shape[0]
    block_size = math.gcd(key_total, 1024)
    number = key_total // block_size

    def body_scan_step(d_query, scan_in):
        key_block, value_block, offset = scan_in
        key_heads = key_block.reshape(block_size, head_count, head_size)
        value_heads = value_block.reshape(block_size, head_count, head_size)
        key_owner = owner_of(offset + jnp.arange(block_size, dtype=jnp.int32), utt_ends)
        probs_low, d_scores = grad_terms(
            q_heads,
            do_heads,
            log_total,
            row_delta,
            key_heads,
            value_heads,
            same_owner(query_owner, key_owner),
            score_scale,
        )
        d_query = d_query + jnp.einsum(
            "qhk,khd->qhd", d_scores, key_heads, preferred_element_type=jnp.float32
        )
        d_key = jnp.einsum(
            "qhk,qhd->khd", d_scores, q_heads, preferred_element_type=jnp.float32
        ).reshape(block_size, model_width)
        d_value = jnp.einsum(
            "qhk,qhd->khd", probs_low, do_heads, preferred_element_type=jnp.float32
        ).reshape(block_size, model_width)
        return (d_query, (d_key, d_value))

    d_query, terms = lax.scan(
        body_scan_step,
        jnp.zeros((tok_rows, head_count, head_size), jnp.float32),
        (
            keys_all.reshape(number, block_size, model_width),
            values_all.reshape(number, block_size, model_width),
            block_size * jnp.arange(number, dtype=jnp.int32),
        ),
    )
    value_terms, d_key = scatter_first(terms[1], terms[0].reshape(key_total, model_width))
    d_value = lax.psum_scatter(
        value_terms.reshape(key_total, model_width), "seq", scatter_dimension=0, tiled=True
    )
    d_qkv = jnp.concatenate(
        [
            rotate(d_query.reshape(tok_rows, model_width), positions, head_count, -1.0),
            rotate(d_key, positions, head_count, -1.0),
            d_value,
        ],
        axis=1,
    ).astype(jnp.bfloat16)
    d_qkv, shard_qkv = scatter_first(d_qkv, contract(normed, d_qkv, 0, 0))
    d_normed = contract(d_qkv, w_qkv, 1, 1)
    unused, norm_back_one = jax.vjp(scale_norm, h_zero, cond_attn)
    d_h_first, d_cond_attn = norm_back_one(d_normed)
    d_h_zero = (d_h_one + d_h_first).astype(jnp.bfloat16)
    d_cond = jnp.concatenate([d_cond_attn, d_cond_ffn], axis=1).astype(jnp.bfloat16)
    d_cond, shard_cond = scatter_first(d_cond, contract(emb, d_cond, 0, 0))
    grad_skip_w = jnp.concatenate(
        [contract(hidden_in, d_h_zero, 0, 0), contract(skips, d_h_zero, 0, 0)], axis=0
    )
    in_grad = contract(d_h_zero, w_skip[:model_width], 1, 1).astype(jnp.bfloat16)
    skip_grad = contract(d_h_zero, w_skip[model_width:], 1, 1).astype(jnp.bfloat16)
    shards = (
        lax.psum_scatter(grad_skip_w, "seq", scatter_dimension=0, tiled=True),
        shard_cond,
        shard_qkv,
        shard_out,
        shard_up,
        shard_down,
    )
    summed = (
        lax.psum(shards[0].astype(jnp.bfloat16), "grp").astype(jnp.float32),
        lax.psum(shards[1].astype(jnp.bfloat16), "grp").astype(jnp.float32),
        lax.psum(shards[2].astype(jnp.bfloat16), "grp").astype(jnp.float32),
        lax.psum(shards[3].astype(jnp.bfloat16), "grp").astype(jnp.float32),
        lax.psum(shards[4].astype(jnp.bfloat16), "grp").astype(jnp.float32),
        lax.psum(shards[5].astype(jnp.bfloat16), "grp").astype(jnp.float32),
    )
    return (
        block_out,
        in_grad,
        skip_grad,
        summed[0],
        summed[1],
        summed[2],
        summed[3],
        summed[4],
        summed[5],
    )


ORDER = (0, 2, 1, 3)
BF16 = jnp.bfloat16
VMEM_MIB = 44
F32 = jnp.float32
ANY = pl.BlockSpec(memory_space=pl.ANY)
VMEM = pl.BlockSpec(memory_space=pltpu.VMEM)
HBM = pl.BlockSpec(memory_space=pltpu.HBM)
SMEM = pl.BlockSpec(memory_space=pltpu.SMEM)


def swapped(axis, mask, size):
    return [(index, index ^ mask) for index in range(size)]


def from_seq(array, mask):
    return lax.ppermute(array, "seq", swapped("seq", mask, 8))


def from_grp(array, mask):
    return lax.ppermute(array, "grp", swapped("grp", mask, 4))


def run_copies(pairs, sems):
    copies = [pltpu.make_async_copy(src, dst, sems.at[i]) for i, (src, dst) in enumerate(pairs)]
    for copy in copies:
        copy.start()
    for copy in copies:
        copy.wait()


def call(kernel, out_shapes, in_specs, scratch, args, deps=(), out_spec=VMEM, cost_us=0.0):
    moved = sum(a.size * a.dtype.itemsize for a in args)
    moved += sum(o.size * o.dtype.itemsize for o in out_shapes)
    given, extra = len(args), len(deps)

    def with_deps(*refs):
        kernel(*refs[:given], *refs[given + extra :])

    return pl.pallas_call(
        with_deps,
        out_shape=tuple(out_shapes),
        in_specs=list(in_specs) + [ANY] * extra,
        out_specs=(out_spec,) * len(out_shapes),
        scratch_shapes=scratch,
        compiler_params=pltpu.CompilerParams(vmem_limit_bytes=VMEM_MIB * 1024 * 1024),
        cost_estimate=pl.CostEstimate(
            flops=int(cost_us * 1.15e9), bytes_accessed=0, transcendentals=0
        ),
    )(*args, *deps)


def sds(shape, dtype):
    return jax.ShapeDtypeStruct(shape, dtype)


MARK = sds((8, 128), F32)


def aligned(index, size):
    return pl.ds(pl.multiple_of(index * size, size), size)


def nt(left, right):
    return lax.dot_general(left, right, (((1,), (1,)), ((), ())), preferred_element_type=F32)


def tn(left, right):
    return lax.dot_general(left, right, (((0,), (0,)), ((), ())), preferred_element_type=F32)


def nn(left, right):
    return jnp.dot(left, right, preferred_element_type=F32)


def frame_blocks(ids, blocks, dst):
    tok = blocks.shape[1]
    return [(blocks.at[ids[1] ^ ORDER[f]], dst.at[pl.ds(f * tok, tok), :]) for f in range(4)]


def h_zero_kernel(ids, inputs, own, own_x, near, far, notes, out, whole, held, wide, shares, sems):
    rows = wide.shape[0] // 8
    frames = held.shape[0]
    pairs = frame_blocks(ids, inputs, held)
    for r in range(8):
        if r < 2:
            piece = (own, own_x)[r].at[pl.ds(0, rows), :]
        else:
            piece = (near, far)[r % 2].at[pl.ds((r // 2 - 1) * rows, rows), :]
        pairs.append((piece, wide.at[aligned(ids[0] ^ r, rows), :]))
    for k, (piece, first) in enumerate(((own, rows), (own_x, rows), (near, 3 * rows), (far, 3 * rows))):
        pairs.append((piece.at[pl.ds(first, 64), :], shares.at[k]))
    run_copies(pairs, sems)
    out[0:frames, :] = nn(held[...], wide[...]).astype(BF16)
    out[frames : frames + 64, :] = (
        shares[0].astype(F32) + shares[1].astype(F32) + shares[2].astype(F32) + shares[3].astype(F32)
    ).astype(BF16)
    out[frames + 64 :, :] = notes[...]
    whole[...] = wide[...]


def qkv_kernel(ids, *refs):
    pieces, weight = refs[:4], refs[4]
    normed_out, hidden_out, packed, told, held, raw, sems = refs[5:]
    tok = packed.shape[1]
    cols = pieces[0].shape[1]
    pairs = [(pieces[ORDER[f]].at[pl.ds(4 * tok, 80), :], raw.at[f]) for f in range(4)]
    for q in range(4):
        for f in range(4):
            pairs.append(
                (
                    pieces[q].at[pl.ds(ORDER[ORDER[f] ^ q] * tok, tok), :],
                    held.at[pl.ds(f * tok, tok), aligned(ids[1] ^ q, cols)],
                )
            )
    run_copies(pairs, sems)
    for f in range(4):
        rows = raw[f].astype(F32)
        told[f, 0:8, :] = unpacked_rows(rows[0:64])
        counts = jnp.concatenate(
            [32.0 * rows[64:65] + rows[65:66], 32.0 * rows[66:67] + rows[67:68], jnp.zeros((6, cols), F32)], axis=0
        )
        told[f, 8:16, :] = jnp.concatenate([counts, jnp.zeros((8, told.shape[2] - cols), F32)], axis=1)
    for f in range(4):
        rows = pl.ds(f * tok, tok)
        hidden = held[rows, :].astype(F32)
        inverse = lax.rsqrt(jnp.mean(hidden * hidden, axis=1, keepdims=True) + EPS)
        normed = (hidden * inverse * scale_of(ids, told.at[f], tok, 0, hidden.shape[1])).astype(BF16)
        normed_out[rows, :] = normed
        if f < 2:
            hidden_out[rows, :] = held[rows, :]
        qkv = nn(normed, weight[...]).astype(BF16)
        group = ids[1] ^ ORDER[f]
        for pair in range(2):
            for part in range(3):
                packed[2 * group + pair, :, pl.ds(part * 128, 128)] = qkv[
                    :, (2 * part + pair) * 128 : (2 * part + pair + 1) * 128
                ]


def turn(vectors, cosine, sine):
    lane = lax.broadcasted_iota(jnp.int32, vectors.shape, 1)
    first = (lane & 63) < 32
    other = jnp.where(first, pltpu.roll(vectors, 96, 1), pltpu.roll(vectors, 32, 1))
    return vectors * cosine + other * sine


CHUNK = 512


def rotated(qkv, cosine, sine):
    total = qkv.shape[0] * qkv.shape[1]
    queries = qkv[:, :, 0:128].reshape(total, 128).astype(F32)
    keys = qkv[:, :, 128:256].reshape(total, 128).astype(F32)
    low_q = (turn(queries, cosine[...], sine[...])).astype(BF16) * jnp.asarray(0.125, BF16)
    low_k = turn(keys, cosine[...], sine[...]).astype(BF16)
    return low_q, low_k


def owners_of(ids, told, total):
    utts = told.shape[1] // 2
    group = ids[1] ^ (ids[0] >> 1)
    lens = jnp.zeros((2 * utts, utts), F32)
    for f in range(4):
        lens = lens + jnp.where(group == ORDER[f], told[f, :, 0:utts], 0.0)
    _, end, _, end_col = utt_bounds(lens, utts)
    down = lax.broadcasted_iota(jnp.int32, (total, utts), 0).astype(F32)
    across = lax.broadcasted_iota(jnp.int32, (utts, total), 1).astype(F32)
    col = jnp.sum(jnp.where(down >= end, 1.0, 0.0), axis=1, keepdims=True)
    row = jnp.sum(jnp.where(across >= end_col, 1.0, 0.0), axis=0, keepdims=True)
    return col, row


def attend_kernel(ids, qkv, turns, told, out, log_out, owner_row):
    total = turns.shape[0]
    cosine, sine = turns.at[:, 0:128], turns.at[:, 128:256]
    owner_col, owner_row[...] = owners_of(ids, told, total)
    tok = qkv.shape[1]
    queries, keys = rotated(qkv, cosine, sine)
    values = qkv[:, :, 256:384].reshape(total, 128)
    for chunk in range(total // CHUNK):
        rows = slice(chunk * CHUNK, (chunk + 1) * CHUNK)
        same = owner_col == owner_row[:, rows]
        both = []
        for head in range(2):
            lanes = slice(64 * head, 64 * head + 64)
            scores = jnp.where(same, nt(keys[:, lanes], queries[rows, lanes]), -1e30)
            top = jnp.max(scores, axis=0, keepdims=True)
            weights = jnp.exp(scores - top)
            total_w = jnp.sum(weights, axis=0, keepdims=True)
            log_out[head : head + 1, rows] = top + jnp.log(total_w)
            mixed = tn(values[:, lanes], weights.astype(BF16)) * (1.0 / total_w)
            both.append(mixed.T)
        joined = jnp.concatenate(both, axis=1).astype(BF16)
        for block in range(CHUNK // tok):
            out[chunk * (CHUNK // tok) + block] = joined[block * tok : (block + 1) * tok]


def attend_back_kernel(
    ids, qkv, d_att, turns, log_total, told, out, d_keys, d_values, owner_row
):
    total = turns.shape[0]
    cosine, sine = turns.at[:, 0:128], turns.at[:, 128:256]
    owner_col, owner_row[...] = owners_of(ids, told, total)
    tok = qkv.shape[1]
    queries, keys = rotated(qkv, cosine, sine)
    values = qkv[:, :, 256:384].reshape(total, 128)
    back = d_att[...].reshape(total, 128)
    keys_t = [keys[:, 64 * head : 64 * head + 64].astype(F32).T.astype(BF16) for head in range(2)]
    for chunk in range(total // CHUNK):
        rows = slice(chunk * CHUNK, (chunk + 1) * CHUNK)
        same = owner_col == owner_row[:, rows]
        d_queries, k_terms, v_terms = [], [], []
        for head in range(2):
            lanes = slice(64 * head, 64 * head + 64)
            scores = nt(keys[:, lanes], queries[rows, lanes])
            probs = jnp.where(same, jnp.exp(scores - log_total[head : head + 1, rows]), 0.0)
            d_probs = nt(values[:, lanes], back[rows, lanes])
            delta = jnp.sum(probs * d_probs, axis=0, keepdims=True)
            d_scores = (probs * (d_probs - delta)).astype(BF16)
            v_terms.append(nn(probs.astype(BF16), back[rows, lanes]))
            k_terms.append(nn(d_scores, queries[rows, lanes]))
            d_queries.append(nn(keys_t[head], d_scores).T * 0.125)
        k_new = jnp.concatenate(k_terms, axis=1)
        v_new = jnp.concatenate(v_terms, axis=1)
        if chunk == 0:
            d_keys[...] = k_new
            d_values[...] = v_new
        else:
            d_keys[...] += k_new
            d_values[...] += v_new
        d_q = jnp.concatenate(d_queries, axis=1)
        d_q = turn(d_q, cosine[rows, :], -sine[rows, :]).astype(BF16)
        for block in range(CHUNK // tok):
            out[chunk * (CHUNK // tok) + block, :, 0:128] = d_q[block * tok : (block + 1) * tok]
    d_k = turn(d_keys[...], cosine[...], -sine[...]).astype(BF16)
    out[:, :, 128:256] = d_k.reshape(total // tok, tok, 128)
    out[:, :, 256:384] = d_values[...].astype(BF16).reshape(total // tok, tok, 128)


def attended_pairs(ids, blocks, dst, tok, parts):
    pairs = []
    for f in range(4):
        for pair in range(2):
            for part in range(parts):
                pairs.append(
                    (
                        blocks.at[2 * (ids[1] ^ ORDER[f]) + pair, :, pl.ds(part * 128, 128)],
                        dst.at[pl.ds(f * tok, tok), pl.ds((2 * part + pair) * 128, 128)],
                    )
                )
    return pairs


def packed_rows(wide):
    return jnp.concatenate([wide[:, k : k + 256] for k in range(0, wide.shape[1], 256)], axis=0)


def unpacked_rows(rows):
    return jnp.concatenate([rows[k : k + 8] for k in range(0, rows.shape[0], 8)], axis=1)


def cut_skip_kernel(ids, weight, emb, cond_weight, piece):
    rows = weight.shape[0]
    piece[0:rows, :] = weight[:, aligned(ids[1], piece.shape[1])]
    piece[rows:, :] = packed_rows(nn(emb[...], cond_weight[...])).astype(BF16)


def gather_kernel(p1, p2, p3, out):
    rows = (out.shape[0] - 64) // 3
    total = jnp.zeros((64, out.shape[1]), F32)
    for k, piece in enumerate((p1, p2, p3)):
        out[k * rows : (k + 1) * rows, :] = piece[0:rows, :]
        total = total + piece[rows:, :].astype(F32)
    out[3 * rows :, :] = total.astype(BF16)


def join_kernel(left, right, joined):
    width = left.shape[1]
    for k in range(joined.shape[0]):
        joined[k, :, 0:width] = left[...]
        joined[k, :, width:] = right[...]


def near_kernel(even, odd, *outs):
    for k, out in enumerate(outs):
        out[...] = (even[k].astype(F32) + odd[k].astype(F32)).astype(BF16)


def add_kernel(left, right, out, mark):
    out[...] = (left[...].astype(F32) + right[...].astype(F32)).astype(out.dtype)
    mark[...] = jnp.zeros_like(mark)


def add_twice_kernel(left, right, out, again):
    total = (left[...].astype(F32) + right[...].astype(F32)).astype(out.dtype)
    out[...] = total
    again[...] = total


def add_three_kernel(first, second, third, out):
    total = first[...].astype(F32) + second[...].astype(F32) + third[...].astype(F32)
    out[...] = total.astype(out.dtype)


def choose_kernel(ids, own, other, out, mark):
    mine = (ids[0] & 1) == (ids[1] & 1)

    @pl.when(mine)
    def _():
        out[...] = own[...]

    @pl.when(jnp.logical_not(mine))
    def _():
        out[...] = other[...]

    mark[...] = jnp.zeros_like(mark)


def pick_kernel(ids, own, near, far, farther, out):
    z, y = ids[0] >> 1, ids[1] >> 1
    rows = own.shape[0]
    low = z >> 1
    source = (z & 1) == y
    first, second = aligned(low, rows), aligned(1 - low, rows)

    @pl.when(source)
    def _():
        out[first, :] = own[...]
        out[second, :] = far[...]

    @pl.when(jnp.logical_not(source))
    def _():
        out[first, :] = near[...]
        out[second, :] = farther[...]


def copy_kernel(source, out):
    out[...] = source[...]


def stack_kernel(*refs):
    out, mark = refs[-2:]
    for k, ref in enumerate(refs[:-2]):
        out[k] = ref[...]
    mark[...] = jnp.zeros_like(mark)


def cut_qkv_kernel(ids, qkv, piece):
    for block in range(piece.shape[1] // 128):
        piece[:, pl.ds(block * 128, 128)] = qkv[:, aligned(4 * block + ids[1], 128)]


def cut_feed_kernel(ids, up, down, piece, sem):
    fetch = pltpu.make_async_copy(down.at[aligned(ids[1], 128), :], piece.at[:, up.shape[1] // 4 :], sem)
    fetch.start()
    for block in range(up.shape[1] // 512):
        piece[:, pl.ds(block * 128, 128)] = up[:, aligned(4 * block + ids[1], 128)]
    fetch.wait()


def utt_bounds(told, utts):
    row = lax.broadcasted_iota(jnp.int32, (utts, utts), 0)
    col = lax.broadcasted_iota(jnp.int32, (utts, utts), 1)
    lens = told[utts : utts + 1, 0:utts]
    spread = jnp.broadcast_to(lens, (utts, utts))
    lens_col = jnp.sum(jnp.where(row == col, spread, 0.0), axis=1, keepdims=True)
    ends = jnp.sum(jnp.where(row <= col, lens_col, 0.0), axis=0, keepdims=True)
    ends_col = jnp.sum(jnp.where(col <= row, spread, 0.0), axis=1, keepdims=True)
    return ends - lens, ends, ends_col - lens_col, ends_col


def scale_of(ids, told, tok, first_col, width):
    utts = told.shape[0] // 2
    begin, end, _, _ = utt_bounds(told, utts)
    frame = (ids[0] * tok + lax.broadcasted_iota(jnp.int32, (tok, utts), 0)).astype(F32)
    onehot = jnp.where((frame >= begin) & (frame < end), 1.0, 0.0).astype(BF16)
    cond = told[0:utts, first_col : first_col + width]
    high = cond.astype(BF16)
    rest = cond - high.astype(F32)
    low = rest.astype(BF16)
    return 1.0 + (nn(onehot, high) + nn(onehot, low))


def utt_picks(ids, told, tok):
    utts = told.shape[0] // 2
    _, _, begin, end = utt_bounds(told, utts)
    frame = (ids[0] * tok + lax.broadcasted_iota(jnp.int32, (utts, tok), 1)).astype(F32)
    return jnp.where((frame >= begin) & (frame < end), 1.0, 0.0).astype(BF16)


def project_kernel(ids, blocks, weight, keep, send, attended, sems):
    tok = blocks.shape[1]
    run_copies(attended_pairs(ids, blocks, attended, tok, 1), sems)
    send[...] = nn(attended[2 * tok :, :], weight[...]).astype(BF16)
    keep[...] = nn(attended[0 : 2 * tok, :], weight[...])


def residual_kernel(ids, hidden, part, other, told, h_one_out, normed_out):
    tok = hidden.shape[0] // 2
    for f in range(2):
        rows, swap = pl.ds(f * tok, tok), pl.ds((1 - f) * tok, tok)
        h_one = hidden[rows, :].astype(F32) + part[rows, :].astype(F32) + other[swap, :].astype(F32)
        inverse = lax.rsqrt(jnp.mean(h_one * h_one, axis=1, keepdims=True) + EPS)
        h_one_out[rows, :] = h_one
        scale = scale_of(ids, told.at[f], tok, h_one.shape[1], h_one.shape[1])
        normed_out[rows, :] = (h_one * inverse * scale).astype(BF16)


def gelu_parts(pre):
    size = jnp.abs(pre)
    decay = jnp.exp(-0.5 * pre * pre)
    t = 1.0 / (1.0 + (0.3275911 * 2.0**-0.5) * size)
    series = t * (0.254829592 + t * (-0.284496736 + t * (1.421413741 + t * (-1.453152027 + t * 1.061405429))))
    tail = 0.5 * series * decay
    half = jnp.where(pre < 0.0, tail, 1.0 - tail)
    return pre * half, half + pre * decay * ((2.0 * math.pi) ** -0.5)


def feed_kernel(ids, *refs):
    normed, normed_c, cots, weight = refs[:4]
    act_out, d_pre_out, keep, send = refs[4:]
    tok = cots.shape[1]
    hidden = act_out.shape[1]
    for f in range(4):
        block = pl.ds(f * tok, tok)
        rows = pl.ds((f % 2) * tok, tok)
        pre = nn((normed, normed_c)[f // 2][rows, :], weight[:, 0:hidden])
        act, slope = gelu_parts(pre)
        act_out[block, :] = act.astype(BF16)
        d_pre = (nt(cots[f], weight[:, hidden:]) * slope).astype(BF16)
        d_pre_out[block, :] = d_pre
        d_normed = nt(d_pre, weight[:, 0:hidden])
        if f < 2:
            keep[block, :] = d_normed
        else:
            send[rows, :] = d_normed.astype(BF16)


def feed_grad_kernel(normed, normed_c, cots, act, d_pre, out, held, sems):
    tok = cots.shape[1]
    run_copies([(normed, held.at[pl.ds(0, 2 * tok), :]), (normed_c, held.at[pl.ds(2 * tok, 2 * tok), :])], sems)
    cots_all = cots[...].reshape(4 * tok, cots.shape[2])
    cols = act.shape[1]
    for r in range(8):
        block = pl.ds(r * 128, 128)
        out[block, 0:cols] = tn(held[:, block], d_pre[...]).astype(BF16)
        out[block, cols:] = tn(act[:, block], cots_all).astype(BF16)


def feed_out_kernel(act, weight, keep, send):
    half = keep.shape[0]
    hidden = act.shape[1]
    keep[...] = nn(act[0:half, :], weight[:, hidden:])
    send[...] = nn(act[half:, :], weight[:, hidden:]).astype(BF16)


def norm_back(hidden, scale, d_normed):
    inverse = lax.rsqrt(jnp.mean(hidden * hidden, axis=1, keepdims=True) + EPS)
    y = hidden * inverse
    d_y = d_normed * scale
    d_hidden = inverse * (d_y - y * jnp.mean(d_y * y, axis=1, keepdims=True))
    return d_hidden, d_normed * y


def norm_back_kernel(first_col, ids, hidden, part, other, base, told, low_out, sums_out):
    tok = hidden.shape[0] // 2
    width = hidden.shape[1]
    for f in range(2):
        rows, swap = pl.ds(f * tok, tok), pl.ds((1 - f) * tok, tok)
        d_normed = part[rows, :].astype(F32) + other[swap, :].astype(F32)
        scale = scale_of(ids, told.at[f], tok, first_col, width)
        d_hidden, d_scale = norm_back(hidden[rows, :].astype(F32), scale, d_normed)
        added = base[f].astype(F32) + d_hidden
        low_out[rows, :] = added.astype(low_out.dtype)
        if f == 0:
            sums_out[...] = nn(utt_picks(ids, told.at[0], tok), d_scale.astype(BF16))


def d_attended_kernel(ids, d_h, d_h_c, weight, packed):
    tok = packed.shape[1]
    for f in range(4):
        rows = pl.ds((f % 2) * tok, tok)
        part = nt((d_h, d_h_c)[f // 2][rows, :], weight[...]).astype(BF16)
        group = ids[1] ^ ORDER[f]
        for pair in range(2):
            packed[2 * group + pair] = part[:, pair * 128 : (pair + 1) * 128]


def qkv_back_kernel(ids, blocks, weight, keep, send, joined, sems):
    tok = blocks.shape[1]
    run_copies(attended_pairs(ids, blocks, joined, tok, 3), sems)
    half = keep.shape[0]
    send[...] = nt(joined[half:, :], weight[...]).astype(BF16)
    keep[...] = nt(joined[0:half, :], weight[...])


def qkv_grad_kernel(ids, normed, joined, d_h, d_h_c, a0, a2, a1, a3, even, odd, attended, sems):
    tok = a0.shape[0] // 4
    half = d_h.shape[0]
    pairs = []
    for q, piece in enumerate((a0, a1, a2, a3)):
        for f in range(4):
            for pair in range(2):
                pairs.append(
                    (
                        piece.at[pl.ds(ORDER[ORDER[f] ^ q] * tok, tok), pl.ds(pair * 128, 128)],
                        attended.at[pl.ds(f * tok, tok), aligned((ids[1] ^ q) + 4 * pair, 128)],
                    )
                )
    run_copies(pairs, sems)
    cols = joined.shape[1]
    mine = aligned(ids[1], 256)
    for r in (1, 3, 5, 7, 0, 2, 4, 6):
        block = aligned(ids[0] ^ r, 128)
        target = (even, odd)[r % 2]
        target[r // 2, :, 0:cols] = tn(normed[:, block], joined[...]).astype(BF16)
        target[r // 2, :, cols:] = (
            tn(attended[0:half, block], d_h[:, mine]) + tn(attended[half:, block], d_h_c[:, mine])
        ).astype(BF16)


def skip_back_kernel(ids, d_h, d_h_c, inputs, sums_attn, sums_ffn, even, odd, sums, held, sems):
    tok = inputs.shape[1]
    run_copies(frame_blocks(ids, inputs, held), sems)
    mine = aligned(ids[1], 256)
    near, far = d_h[:, mine], d_h_c[:, mine]
    half = 2 * tok
    for r in (1, 3, 5, 7, 0, 2, 4, 6):
        block = aligned(ids[0] ^ r, 256)
        grad = (tn(held[0:half, block], near) + tn(held[half:, block], far)).astype(BF16)
        if r % 2:
            odd[(r // 2) * 256 : (r // 2) * 256 + 256, :] = grad
        else:
            even[r // 2] = grad
    low = packed_rows(jnp.concatenate([sums_attn[...], sums_ffn[...]], axis=1)).astype(BF16)
    odd[1024:, :] = low
    sums[...] = low


def skip_near_kernel(even, sums, arrived, *outs):
    both = (sums[...].astype(F32) + arrived[1024:, :].astype(F32)).astype(BF16)
    for k, out in enumerate(outs):
        out[0:256, :] = (even[k].astype(F32) + arrived[k * 256 : (k + 1) * 256, :].astype(F32)).astype(BF16)
        out[256:, :] = both


def in_back_kernel(ids, d_h, near, far, in_out, skip_out):
    tok, width = in_out.shape
    total = jnp.zeros((tok, 2 * width), F32)
    for q in range(4):
        weight = (near, far)[q % 2].at[q // 2]
        total = total + nt(d_h[0:tok, aligned(ids[1] ^ q, 256)], weight[...])
    in_out[...] = total[:, 0:width].astype(BF16)
    skip_out[...] = total[:, width:].astype(BF16)


def spread_feed_kernel(ids, near, far, up_o, down_o, mark):
    hidden = near.shape[2] - down_o.shape[1]
    for q in range(4):
        part = ids[1] ^ q
        feed = (near, far)[q % 2].at[q // 2]
        for block in range(hidden // 128):
            up_o[:, aligned(4 * block + part, 128)] = feed[:, pl.ds(block * 128, 128)].astype(F32)
        down_o[aligned(part, 128), :] = feed[:, hidden:].astype(F32)
    mark[...] = jnp.zeros_like(mark)


def last_kernel(p0, p1, p2, p3, q0, q1, q2, q3, out):
    qkv = q0[...].astype(F32) + q1[...].astype(F32) + q2[...].astype(F32) + q3[...].astype(F32)
    skip = p0[...].astype(F32) + p1[...].astype(F32) + p2[...].astype(F32) + p3[...].astype(F32)
    out[:, 0:1024] = qkv.astype(BF16)
    out[:, 1024:1280] = skip[0:128].astype(BF16)
    out[:, 1280:1536] = skip[128:256].astype(BF16)
    out[0:64, 1536:1792] = skip[256:].astype(BF16)
    out[64:, 1536:1792] = jnp.zeros((64, 256), BF16)


def spread_kernel(ids, near, far, emb, qkv_o, out_o, skip_o, cond_o):
    rows = qkv_o.shape[0]
    utts = emb.shape[0] // 4
    for q in range(4):
        part = ids[1] ^ q
        piece = (near, far)[q % 2].at[q // 2]
        for block in range(6):
            qkv_o[:, aligned(4 * block + part, 128)] = piece[0:rows, pl.ds(block * 128, 128)].astype(F32)
        out_o[:, aligned(part, 256)] = piece[0:rows, pl.ds(768, 256)].astype(F32)
        skip_o[0:rows, aligned(part, 256)] = piece[0:rows, pl.ds(1024, 256)].astype(F32)
        skip_o[rows:, aligned(part, 256)] = piece[0:rows, pl.ds(1280, 256)].astype(F32)
    steps = emb[...].astype(F32)
    total = jnp.zeros(cond_o.shape, F32)
    for f in range(4):
        sums = unpacked_rows((near, far)[f // 2][f % 2, 0:64, 1536:1792].astype(F32)).astype(BF16)
        total = total + tn(steps[f * utts : (f + 1) * utts, :].astype(BF16), sums)
    cond_o[...] = total


def stack(arrays, deps=()):
    shape = (len(arrays),) + arrays[0].shape
    return call(stack_kernel, [sds(shape, arrays[0].dtype), MARK], [VMEM] * len(arrays), [], list(arrays), deps=deps)


def around(piece):
    return [piece, from_grp(piece, 2), from_grp(piece, 1), from_grp(piece, 3)]


def gather_groups(piece):
    along_y = from_grp(piece, 2)
    return [piece, along_y, from_grp(piece, 1), from_grp(along_y, 1)]


def gather_pairs(piece, deps=()):
    near, _ = stack([piece, from_grp(piece, 2)], deps)
    return near, from_grp(near, 1)


def scatter_near(even, odd, deps):
    arrived = from_seq(odd, 1)
    return call(near_kernel, [sds(even.shape[1:], BF16)] * 4, [VMEM] * 2, [], [even, arrived], deps=deps)


def by_mask(pieces):
    return [pieces[0], pieces[2], pieces[1], pieces[3]]


def halves_sum(keep, send):
    kept, sent = call(
        add_twice_kernel, [sds(keep.shape, BF16)] * 2, [VMEM] * 2, [], [keep, from_grp(send, 1)]
    )
    return kept, from_grp(sent, 2)


def add_two(left, right, deps=()):
    return call(add_kernel, [sds(left.shape, BF16), MARK], [VMEM] * 2, [], [left, right], deps=deps)


def exchange(array, cols):
    return lax.all_to_all(array, "seq", 0, 0, tiled=True)


def out_moves(mask, keep):
    pairs = []
    for t in range(4):
        for slot in range(8):
            if keep(slot, t):
                pairs.append((t * 8 + slot, t * 8 + (slot ^ mask)))
    return pairs


def out_along_z(piece):
    def holds(slot, t):
        return (slot & 1) == (t & 1) and ((slot >> 1) & 1) == (t >> 1)

    return [lax.ppermute(piece, ("grp", "seq"), out_moves(2 * k, holds)) for k in range(1, 4)]


def out_along_x(rows):
    return lax.ppermute(rows, ("grp", "seq"), out_moves(1, lambda slot, t: (slot & 1) == (t & 1)))


def tp_body(
    hidden_in, skips, lengths, times, skip_weight, cond_weight, qkv_weight, out_weight,
    up_weight, down_weight, cotangent,
):
    tok, width = hidden_in.shape
    ff = up_weight.shape[1]
    frames = 8 * tok
    slot = lax.axis_index("seq")
    part = lax.axis_index("grp")
    ids = jnp.stack([slot, part]).astype(jnp.int32)
    sem = pltpu.SemaphoreType.DMA

    half_width = width // 2
    rows_here = cond_weight.shape[0]
    utts = times.shape[1]

    def embed_here(time_rows):
        column = (slot * rows_here + jnp.arange(rows_here, dtype=jnp.int32)) % half_width
        freqs = jnp.exp(-math.log(10000.0) * column.astype(F32) / half_width)
        angles = time_rows[:, None] * freqs[None, :]
        return jnp.where(slot * rows_here < half_width, jnp.sin(angles), jnp.cos(angles)).astype(BF16)

    skip_rows = skip_weight.shape[0]
    (skip_piece,) = call(
        cut_skip_kernel,
        [sds((skip_rows + 64, 256), BF16)],
        [SMEM] + [VMEM] * 3,
        [],
        [ids, skip_weight, embed_here(times[0].astype(F32)), cond_weight],
    )
    (qkv_piece,) = call(cut_qkv_kernel, [sds((128, 768), BF16)], [SMEM, VMEM], [], [ids, qkv_weight])
    (skip_same,) = call(
        gather_kernel,
        [sds((3 * skip_rows + 64, 256), BF16)],
        [VMEM] * 3,
        [],
        [from_seq(skip_piece, 2 * k) for k in range(1, 4)],
        deps=[qkv_piece],
    )
    skip_other = from_seq(skip_same, 1)
    (joined,) = call(
        join_kernel, [sds((4, tok, 2 * width), BF16)], [VMEM] * 2, [], [hidden_in, skips], deps=[skip_piece]
    )
    inputs = lax.all_to_all(joined, "grp", 0, 0, tiled=True)
    w_qkv = lax.all_gather(qkv_piece, "seq", axis=0, tiled=True)
    (feed_piece,) = call(
        cut_feed_kernel,
        [sds((128, ff // 4 + width), BF16)],
        [SMEM, VMEM, ANY],
        [sem],
        [ids, up_weight, down_weight],
        deps=[qkv_piece],
    )
    w_feed = lax.all_gather(feed_piece, "seq", axis=0, tiled=True)

    counts = jnp.stack([lengths[0] >> 5, lengths[0] & 31, times[0] >> 5, times[0] & 31])
    notes = jnp.zeros((16, 256), BF16).at[0:4, 0:utts].set(counts.astype(BF16))

    (out_piece,) = call(copy_kernel, [sds(out_weight.shape, BF16)], [VMEM], [], [out_weight], deps=[skip_same])
    out_came = out_along_z(out_piece)

    inverse = jnp.exp(-math.log(10000.0) * jnp.arange(32, dtype=F32) / 32)
    turn_angles = jnp.arange(frames, dtype=F32)[:, None] * inverse[None, :]
    cos_half, sin_half = jnp.cos(turn_angles), jnp.sin(turn_angles)
    turns = jnp.concatenate([cos_half] * 4 + [-sin_half, sin_half] * 2, axis=1)

    h_cols, w_skip = call(
        h_zero_kernel,
        [sds((4 * tok + 80, 256), BF16), sds((2 * width, 256), BF16)],
        [SMEM] + [ANY] * 5 + [VMEM],
        [
            pltpu.VMEM((4 * tok, 2 * width), BF16),
            pltpu.VMEM((2 * width, 256), BF16),
            pltpu.VMEM((4, 64, 256), BF16),
            sem((16,)),
        ],
        [ids, inputs, skip_piece, from_seq(skip_piece, 1), skip_same, skip_other, notes],
        deps=out_came,
        cost_us=100.0,
    )
    h_pieces = gather_groups(h_cols)
    h_pieces = [h_pieces[0], h_pieces[2], h_pieces[1], h_pieces[3]]
    normed, h_zero, packed, told = call(
        qkv_kernel,
        [
            sds((4 * tok, width), BF16),
            sds((2 * tok, width), BF16),
            sds((8, tok, 384), BF16),
            sds((4, 2 * utts, 2 * width), F32),
        ],
        [SMEM] + [ANY] * 4 + [VMEM],
        [pltpu.VMEM((4 * tok, width), BF16), pltpu.VMEM((4, 80, 256), BF16), sem((20,))],
        [ids] + h_pieces + [w_qkv],
    )
    emb_all = embed_here(told[:, utts + 1, :utts].reshape(4 * utts))
    qkv = exchange(packed, 384)
    (out_picked,) = call(
        pick_kernel, [sds((2 * tok, width), BF16)], [SMEM] + [VMEM] * 4, [], [ids, out_piece] + out_came
    )
    (w_skip,) = call(copy_kernel, [sds(w_skip.shape, BF16)], [VMEM], [], [w_skip], deps=[packed])
    skip_y = from_grp(w_skip, 2)
    w_out, out_mark = call(
        choose_kernel,
        [sds((2 * tok, width), BF16), MARK],
        [SMEM] + [VMEM] * 2,
        [],
        [ids, out_picked, out_along_x(out_picked)],
    )
    skip_near, skip_mark = stack([w_skip, skip_y], [packed])
    skip_far = from_grp(skip_near, 1)
    mixed, log_total = call(
        attend_kernel,
        [sds((8, tok, 128), BF16), sds((2, frames), F32)],
        [SMEM] + [VMEM] * 3,
        [pltpu.VMEM((1, frames), F32)],
        [ids, qkv, turns, told],
        deps=[out_mark, skip_mark],
    )
    attended_blocks = exchange(mixed, 128)
    (cot_piece,) = call(
        copy_kernel, [sds((tok, width), BF16)], [VMEM], [], [cotangent], deps=[mixed]
    )
    cots, cot_mark = stack(around(cot_piece))
    keep, send, attended = call(
        project_kernel,
        [
            sds((2 * tok, width), F32),
            sds((2 * tok, width), BF16),
            sds((4 * tok, 256), BF16),
        ],
        [SMEM, ANY, VMEM],
        [sem((8,))],
        [ids, attended_blocks, w_out],
        deps=[cot_mark],
    )
    h_part, h_part_y = halves_sum(keep, send)
    h_one, normed_two = call(
        residual_kernel,
        [sds((2 * tok, width), F32), sds((2 * tok, width), BF16)],
        [SMEM] + [VMEM] * 4,
        [],
        [ids, h_zero, h_part, h_part_y, told],
    )
    normed_two_c = from_grp(normed_two, 1)
    quarter = ff // 4
    act, d_pre, keep, send = call(
        feed_kernel,
        [
            sds((4 * tok, quarter), BF16),
            sds((4 * tok, quarter), BF16),
            sds((2 * tok, width), F32),
            sds((2 * tok, width), BF16),
        ],
        [SMEM] + [VMEM] * 4,
        [],
        [ids, normed_two, normed_two_c, cots, w_feed],
    )

    d_part, d_part_y = halves_sum(keep, send)
    (feed_terms,) = call(
        feed_grad_kernel,
        [sds((width, quarter + width), BF16)],
        [ANY] * 2 + [VMEM] * 3,
        [pltpu.VMEM((4 * tok, width), BF16), sem((2,))],
        [normed_two, normed_two_c, cots, act, d_pre],
        deps=[d_part],
    )
    out_keep, out_send = call(
        feed_out_kernel,
        [sds((2 * tok, width), F32), sds((2 * tok, width), BF16)],
        [VMEM, VMEM],
        [],
        [act, w_feed],
        deps=[feed_terms],
    )
    d_h_one, sums_ffn = call(
        functools.partial(norm_back_kernel, width),
        [sds((2 * tok, width), BF16), sds((utts, width), F32)],
        [SMEM] + [VMEM] * 5,
        [],
        [ids, h_one, d_part, d_part_y, cots, told],
        deps=[out_send],
        cost_us=100.0,
    )
    d_h_one_c = from_grp(d_h_one, 1)
    (d_att_packed,) = call(
        d_attended_kernel,
        [sds((8, tok, 128), BF16)],
        [SMEM, VMEM, VMEM, VMEM],
        [],
        [ids, d_h_one, d_h_one_c, w_out],
    )
    d_att = exchange(d_att_packed, 128)

    feed_own = lax.psum_scatter(feed_terms, "seq", scatter_dimension=0, tiled=True)
    att_pieces = around(attended)
    out_part, out_done = add_two(out_keep, from_grp(out_send, 1), [d_att_packed])
    (d_packed,) = call(
        attend_back_kernel,
        [sds((8, tok, 384), BF16)],
        [SMEM] + [VMEM] * 5,
        [pltpu.VMEM((frames, 128), F32), pltpu.VMEM((frames, 128), F32), pltpu.VMEM((1, frames), F32)],
        [ids, qkv, d_att, turns, log_total, told],
        deps=[out_done],
    )
    d_qkv_blocks = exchange(d_packed, 384)
    (block_out,) = call(
        add_three_kernel,
        [sds((tok, width), BF16)],
        [VMEM] * 3,
        [],
        [h_one[:tok], out_part[:tok], from_grp(out_part[tok:], 2)],
        deps=[d_packed] + att_pieces[1:],
    )
    keep, send, d_qkv = call(
        qkv_back_kernel,
        [sds((2 * tok, width), F32), sds((2 * tok, width), BF16), sds((4 * tok, 768), BF16)],
        [SMEM, ANY, VMEM],
        [sem((24,))],
        [ids, d_qkv_blocks, w_qkv],
        deps=[block_out],
    )
    d_part, d_part_y = halves_sum(keep, send)
    qkv_even, qkv_odd = call(
        qkv_grad_kernel,
        [sds((4, 128, 1024), BF16)] * 2,
        [SMEM] + [VMEM] * 4 + [ANY] * 4,
        [pltpu.VMEM((4 * tok, width), BF16), sem((32,))],
        [ids, normed, d_qkv, d_h_one, d_h_one_c] + att_pieces,
        deps=[d_part],
    )
    d_h_zero, sums_attn = call(
        functools.partial(norm_back_kernel, 0),
        [sds((2 * tok, width), BF16), sds((utts, width), F32)],
        [SMEM] + [VMEM] * 5,
        [],
        [ids, h_zero, d_part, d_part_y, d_h_one.reshape(2, tok, width), told],
        deps=[qkv_odd],
    )
    d_h_zero_c = from_grp(d_h_zero, 1)
    skip_even, skip_odd, skip_sums = call(
        skip_back_kernel,
        [sds((4, 256, 256), BF16), sds((1024 + 64, 256), BF16), sds((64, 256), BF16)],
        [SMEM, VMEM, VMEM, ANY, VMEM, VMEM],
        [pltpu.VMEM((4 * tok, 2 * width), BF16), sem((4,))],
        [ids, d_h_zero, d_h_zero_c, inputs, sums_attn, sums_ffn],
    )
    qkv_near = scatter_near(qkv_even, qkv_odd, [skip_odd])
    qkv_came = [from_seq(qkv_near[k], 2 * k) for k in range(1, 4)]
    last_near = call(
        skip_near_kernel,
        [sds((256 + 64, 256), BF16)] * 4,
        [VMEM] * 3,
        [],
        [skip_even, skip_sums, from_seq(skip_odd, 1)],
        deps=[qkv_near[0]],
    )
    last_came = [from_seq(last_near[k], 2 * k) for k in range(1, 4)]
    in_grad, skip_grad = call(
        in_back_kernel,
        [sds((tok, width), BF16)] * 2,
        [SMEM] + [VMEM] * 3,
        [],
        [ids, d_h_zero, skip_near, skip_far],
        deps=qkv_came + [last_near[0]],
    )
    (last_own,) = call(
        last_kernel,
        [sds((128, 1792), BF16)],
        [VMEM] * 8,
        [],
        [last_near[0]] + last_came + [qkv_near[0]] + qkv_came,
        deps=[in_grad],
    )
    feed_near, feed_far = gather_pairs(feed_own, [last_own])
    up_grad, down_grad, up_mark = call(
        spread_feed_kernel,
        [sds((128, ff), F32), sds((ff // 8, width), F32), MARK],
        [SMEM] + [VMEM] * 2,
        [],
        [ids, feed_near, feed_far],
    )
    all_near, all_far = gather_pairs(last_own, [up_mark])
    qkv_grad, out_grad, skip_grad_w, cond_grad = call(
        spread_kernel,
        [
            sds((128, 3 * width), F32),
            sds((128, width), F32),
            sds((256, width), F32),
            sds((rows_here, 2 * width), F32),
        ],
        [SMEM] + [VMEM] * 3,
        [],
        [ids, all_near, all_far, emb_all],
    )
    return (
        block_out, in_grad, skip_grad, skip_grad_w, cond_grad, qkv_grad,
        out_grad, up_grad, down_grad,
    )


def solution(mesh):
    placed = (
        P(("grp", "seq"), None),
        P(("grp", "seq"), None),
        P("grp", None),
        P("grp", None),
        P("seq", None),
        P("seq", None),
        P("seq", None),
        P("seq", None),
        P("seq", None),
        P("seq", None),
        P(("grp", "seq"), None),
    )
    body = tp_body if (mesh.shape["grp"], mesh.shape["seq"]) == (4, 8) else plain_body
    return jax.shard_map(
        body,
        mesh=mesh,
        in_specs=placed,
        out_specs=(
            P(("grp", "seq"), None),
            P(("grp", "seq"), None),
            P(("grp", "seq"), None),
            P("seq", None),
            P("seq", None),
            P("seq", None),
            P("seq", None),
            P("seq", None),
            P("seq", None),
        ),
        check_vma=False,
    )
```

```python
import functools
import math

import jax
import jax.numpy as jnp
from jax import lax
from jax.experimental import pallas as pl
from jax.experimental.pallas import tpu as pltpu
from jax.sharding import PartitionSpec as P

HEADS = 16


EPS = 1e-06


def contract(left, right, left_dim, right_dim):
    return lax.dot_general(
        left, right, (((left_dim,), (right_dim,)), ((), ())), preferred_element_type=jnp.float32
    )


def matmul(left, right):
    return jnp.dot(left, right, preferred_element_type=jnp.float32)


def owner_of(frames, utt_ends):
    return jnp.sum((frames[:, None] >= utt_ends[None, :]).astype(jnp.int32), axis=1)


def same_owner(query_owner, key_owner):
    return (query_owner[:, None] == key_owner[None, :])[:, None, :]


def embed_steps(time_steps, model_width):
    half_width = model_width // 2
    freqs = jnp.exp(-math.log(10000.0) * jnp.arange(half_width, dtype=jnp.float32) / half_width)
    angles = time_steps[:, None] * freqs[None, :]
    return jnp.concatenate([jnp.sin(angles), jnp.cos(angles)], axis=1)


def rotate(vectors, positions, head_count, direction):
    tok_rows, model_width = vectors.shape
    head_size = model_width // head_count
    half_size = head_size // 2
    inverse = jnp.exp(-math.log(10000.0) * jnp.arange(half_size, dtype=jnp.float32) / half_size)
    angles = positions[:, None] * inverse[None, :]
    cosine = jnp.cos(angles)[:, None, :]
    sine = direction * jnp.sin(angles)[:, None, :]
    split = vectors.reshape(tok_rows, head_count, head_size)
    first_half = split[..., :half_size]
    second_half = split[..., half_size:]
    turned = jnp.concatenate(
        [first_half * cosine - second_half * sine, first_half * sine + second_half * cosine],
        axis=-1,
    )
    return turned.reshape(tok_rows, model_width)


def scale_norm(hidden, cond_part):
    return (
        hidden
        * lax.rsqrt(jnp.mean(hidden * hidden, axis=1, keepdims=True) + EPS)
        * (1.0 + cond_part)
    )


def over_blocks(update, running, arrays, first_row, block_cap):
    row_count = arrays[0].shape[0]
    block_size = math.gcd(row_count, block_cap)
    number = row_count // block_size
    if number == 1:
        return update(running, arrays, first_row)
    stacked = tuple((array.reshape((number, block_size) + array.shape[1:]) for array in arrays))
    offsets = first_row + block_size * jnp.arange(number, dtype=jnp.int32)

    def over_scan_step(inner, scan_in):
        return (update(inner, scan_in[0], scan_in[1]), None)

    result, unused = lax.scan(over_scan_step, running, (stacked, offsets))
    return result


def grad_terms(
    q_heads, do_heads, log_total, row_delta, key_heads, value_heads, same_utt, score_scale
):
    scores = (
        jnp.einsum("qhd,khd->qhk", q_heads, key_heads, preferred_element_type=jnp.float32)
        * score_scale
    )
    probs = jnp.where(same_utt, jnp.exp(scores - log_total[..., None]), 0.0)
    d_probs = jnp.einsum("qhd,khd->qhk", do_heads, value_heads, preferred_element_type=jnp.float32)
    d_scores = (probs * (d_probs - row_delta[..., None]) * score_scale).astype(jnp.bfloat16)
    return (probs.astype(jnp.bfloat16), d_scores)


def scatter_first(after, grad):
    return lax.optimization_barrier(
        (after, lax.psum_scatter(grad, "seq", scatter_dimension=0, tiled=True))
    )


def plain_body(
    hidden_in,
    skips,
    lengths,
    times,
    skip_weight,
    cond_weight,
    qkv_weight,
    out_weight,
    up_weight,
    down_weight,
    cotangent,
):
    tok_rows, model_width = hidden_in.shape
    head_count = HEADS
    head_size = model_width // head_count
    score_scale = head_size ** (-0.5)
    first_frame = lax.axis_index("seq") * tok_rows
    utt_lengths = lengths[0]
    utt_ends = jnp.cumsum(utt_lengths)
    starts = utt_ends - utt_lengths
    frames = first_frame + jnp.arange(tok_rows, dtype=jnp.int32)
    query_owner = owner_of(frames, utt_ends)
    onehot = query_owner[:, None] == jnp.arange(utt_lengths.shape[0], dtype=jnp.int32)[None, :]
    positions = (frames - jnp.sum(jnp.where(onehot, starts[None, :], 0), axis=1)).astype(
        jnp.float32
    )
    time_steps = jnp.sum(jnp.where(onehot, times[0][None, :], 0), axis=1).astype(jnp.float32)
    gathered = (
        lax.all_gather(skip_weight, "seq", axis=0, tiled=True),
        lax.all_gather(cond_weight, "seq", axis=0, tiled=True),
        lax.all_gather(qkv_weight, "seq", axis=0, tiled=True),
        lax.all_gather(out_weight, "seq", axis=0, tiled=True),
        lax.all_gather(up_weight, "seq", axis=0, tiled=True),
        lax.all_gather(down_weight, "seq", axis=0, tiled=True),
    )
    w_skip, w_cond, w_qkv, w_out, w_up, w_down = gathered
    h_zero = matmul(hidden_in, w_skip[:model_width]) + matmul(skips, w_skip[model_width:])
    emb = embed_steps(time_steps, model_width).astype(jnp.bfloat16)
    cond = matmul(emb, w_cond)
    cond_attn = cond[:, :model_width]
    cond_ffn = cond[:, model_width:]
    normed = scale_norm(h_zero, cond_attn).astype(jnp.bfloat16)
    qkv = matmul(normed, w_qkv)
    queries = rotate(qkv[:, :model_width], positions, head_count, 1.0).astype(jnp.bfloat16)
    keys = rotate(qkv[:, model_width : 2 * model_width], positions, head_count, 1.0).astype(
        jnp.bfloat16
    )
    values = qkv[:, 2 * model_width :].astype(jnp.bfloat16)
    q_heads = queries.reshape(tok_rows, head_count, head_size)

    def forward_step(running, blocks, first_row):
        weighted, run_max, run_sum = running
        key_heads = blocks[0].reshape(-1, head_count, head_size)
        value_heads = blocks[1].reshape(-1, head_count, head_size)
        key_owner = owner_of(first_row + jnp.arange(key_heads.shape[0], dtype=jnp.int32), utt_ends)
        same_utt = same_owner(query_owner, key_owner)
        scores = (
            jnp.einsum("qhd,khd->qhk", q_heads, key_heads, preferred_element_type=jnp.float32)
            * score_scale
        )
        new_max = jnp.maximum(run_max, jnp.max(jnp.where(same_utt, scores, -1e30), axis=-1))
        weights_b = jnp.where(same_utt, jnp.exp(scores - new_max[..., None]), 0.0)
        factor = jnp.exp(run_max - new_max)
        run_sum = run_sum * factor + jnp.sum(weights_b, axis=-1)
        weighted = weighted * factor[..., None] + jnp.einsum(
            "qhk,khd->qhd",
            weights_b.astype(jnp.bfloat16),
            value_heads,
            preferred_element_type=jnp.float32,
        )
        return (weighted, new_max, run_sum)

    start_state = (
        jnp.zeros((tok_rows, head_count, head_size), jnp.float32),
        jnp.full((tok_rows, head_count), -1e30, jnp.float32),
        jnp.zeros((tok_rows, head_count), jnp.float32),
    )
    weighted, run_max, run_sum = over_blocks(
        forward_step,
        start_state,
        (
            lax.all_gather(keys, "seq", axis=0, tiled=True),
            lax.all_gather(values, "seq", axis=0, tiled=True),
        ),
        jnp.int32(0),
        1024,
    )
    attended_full = (weighted / run_sum[..., None]).reshape(tok_rows, model_width)
    log_total = run_max + jnp.log(run_sum)
    attended = attended_full.astype(jnp.bfloat16)
    h_one = h_zero + matmul(attended, w_out)
    normed_two = scale_norm(h_one, cond_ffn).astype(jnp.bfloat16)
    pre = matmul(normed_two, w_up)
    act = jax.nn.gelu(pre, approximate=False).astype(jnp.bfloat16)
    block_out = (h_one + matmul(act, w_down)).astype(jnp.bfloat16)
    regathered = (
        lax.all_gather(skip_weight, "seq", axis=0, tiled=True),
        lax.all_gather(cond_weight, "seq", axis=0, tiled=True),
        lax.all_gather(qkv_weight, "seq", axis=0, tiled=True),
        lax.all_gather(out_weight, "seq", axis=0, tiled=True),
        lax.all_gather(up_weight, "seq", axis=0, tiled=True),
        lax.all_gather(down_weight, "seq", axis=0, tiled=True),
    )
    w_skip, w_cond, w_qkv, w_out, w_up, w_down = regathered
    d_act = contract(cotangent, w_down, 1, 1)
    d_act, shard_down = scatter_first(d_act, contract(act, cotangent, 0, 0))
    unused, gelu_back = jax.vjp(lambda inner: jax.nn.gelu(inner, approximate=False), pre)
    d_pre = gelu_back(d_act)[0].astype(jnp.bfloat16)
    d_pre, shard_up = scatter_first(d_pre, contract(normed_two, d_pre, 0, 0))
    d_normed_two = contract(d_pre, w_up, 1, 1)
    unused, norm_back_two = jax.vjp(scale_norm, h_one, cond_ffn)
    d_h_norm, d_cond_ffn = norm_back_two(d_normed_two)
    d_h_one = cotangent.astype(jnp.float32) + d_h_norm
    d_h_low = d_h_one.astype(jnp.bfloat16)
    d_h_low, shard_out = scatter_first(d_h_low, contract(attended, d_h_low, 0, 0))
    d_attended = contract(d_h_low, w_out, 1, 1).astype(jnp.bfloat16)
    row_delta = jnp.sum(
        (d_attended.astype(jnp.float32) * attended_full).reshape(tok_rows, head_count, head_size),
        axis=-1,
    )
    do_heads = d_attended.reshape(tok_rows, head_count, head_size)
    keys_all, values_all = (
        lax.all_gather(keys, "seq", axis=0, tiled=True),
        lax.all_gather(values, "seq", axis=0, tiled=True),
    )
    key_total = keys_all.shape[0]
    block_size = math.gcd(key_total, 1024)
    number = key_total // block_size

    def body_scan_step(d_query, scan_in):
        key_block, value_block, offset = scan_in
        key_heads = key_block.reshape(block_size, head_count, head_size)
        value_heads = value_block.reshape(block_size, head_count, head_size)
        key_owner = owner_of(offset + jnp.arange(block_size, dtype=jnp.int32), utt_ends)
        probs_low, d_scores = grad_terms(
            q_heads,
            do_heads,
            log_total,
            row_delta,
            key_heads,
            value_heads,
            same_owner(query_owner, key_owner),
            score_scale,
        )
        d_query = d_query + jnp.einsum(
            "qhk,khd->qhd", d_scores, key_heads, preferred_element_type=jnp.float32
        )
        d_key = jnp.einsum(
            "qhk,qhd->khd", d_scores, q_heads, preferred_element_type=jnp.float32
        ).reshape(block_size, model_width)
        d_value = jnp.einsum(
            "qhk,qhd->khd", probs_low, do_heads, preferred_element_type=jnp.float32
        ).reshape(block_size, model_width)
        return (d_query, (d_key, d_value))

    d_query, terms = lax.scan(
        body_scan_step,
        jnp.zeros((tok_rows, head_count, head_size), jnp.float32),
        (
            keys_all.reshape(number, block_size, model_width),
            values_all.reshape(number, block_size, model_width),
            block_size * jnp.arange(number, dtype=jnp.int32),
        ),
    )
    value_terms, d_key = scatter_first(terms[1], terms[0].reshape(key_total, model_width))
    d_value = lax.psum_scatter(
        value_terms.reshape(key_total, model_width), "seq", scatter_dimension=0, tiled=True
    )
    d_qkv = jnp.concatenate(
        [
            rotate(d_query.reshape(tok_rows, model_width), positions, head_count, -1.0),
            rotate(d_key, positions, head_count, -1.0),
            d_value,
        ],
        axis=1,
    ).astype(jnp.bfloat16)
    d_qkv, shard_qkv = scatter_first(d_qkv, contract(normed, d_qkv, 0, 0))
    d_normed = contract(d_qkv, w_qkv, 1, 1)
    unused, norm_back_one = jax.vjp(scale_norm, h_zero, cond_attn)
    d_h_first, d_cond_attn = norm_back_one(d_normed)
    d_h_zero = (d_h_one + d_h_first).astype(jnp.bfloat16)
    d_cond = jnp.concatenate([d_cond_attn, d_cond_ffn], axis=1).astype(jnp.bfloat16)
    d_cond, shard_cond = scatter_first(d_cond, contract(emb, d_cond, 0, 0))
    grad_skip_w = jnp.concatenate(
        [contract(hidden_in, d_h_zero, 0, 0), contract(skips, d_h_zero, 0, 0)], axis=0
    )
    in_grad = contract(d_h_zero, w_skip[:model_width], 1, 1).astype(jnp.bfloat16)
    skip_grad = contract(d_h_zero, w_skip[model_width:], 1, 1).astype(jnp.bfloat16)
    shards = (
        lax.psum_scatter(grad_skip_w, "seq", scatter_dimension=0, tiled=True),
        shard_cond,
        shard_qkv,
        shard_out,
        shard_up,
        shard_down,
    )
    summed = (
        lax.psum(shards[0].astype(jnp.bfloat16), "grp").astype(jnp.float32),
        lax.psum(shards[1].astype(jnp.bfloat16), "grp").astype(jnp.float32),
        lax.psum(shards[2].astype(jnp.bfloat16), "grp").astype(jnp.float32),
        lax.psum(shards[3].astype(jnp.bfloat16), "grp").astype(jnp.float32),
        lax.psum(shards[4].astype(jnp.bfloat16), "grp").astype(jnp.float32),
        lax.psum(shards[5].astype(jnp.bfloat16), "grp").astype(jnp.float32),
    )
    return (
        block_out,
        in_grad,
        skip_grad,
        summed[0],
        summed[1],
        summed[2],
        summed[3],
        summed[4],
        summed[5],
    )


ORDER = (0, 2, 1, 3)
BF16 = jnp.bfloat16
VMEM_MIB = 44
F32 = jnp.float32
ANY = pl.BlockSpec(memory_space=pl.ANY)
VMEM = pl.BlockSpec(memory_space=pltpu.VMEM)
HBM = pl.BlockSpec(memory_space=pltpu.HBM)
SMEM = pl.BlockSpec(memory_space=pltpu.SMEM)


def swapped(axis, mask, size):
    return [(index, index ^ mask) for index in range(size)]


def from_seq(array, mask):
    return lax.ppermute(array, "seq", swapped("seq", mask, 8))


def from_grp(array, mask):
    return lax.ppermute(array, "grp", swapped("grp", mask, 4))


def run_copies(pairs, sems):
    copies = [pltpu.make_async_copy(src, dst, sems.at[i]) for i, (src, dst) in enumerate(pairs)]
    for copy in copies:
        copy.start()
    for copy in copies:
        copy.wait()


def call(kernel, out_shapes, in_specs, scratch, args, deps=(), out_spec=VMEM, cost_us=0.0):
    moved = sum(a.size * a.dtype.itemsize for a in args)
    moved += sum(o.size * o.dtype.itemsize for o in out_shapes)
    given, extra = len(args), len(deps)

    def with_deps(*refs):
        kernel(*refs[:given], *refs[given + extra :])

    return pl.pallas_call(
        with_deps,
        out_shape=tuple(out_shapes),
        in_specs=list(in_specs) + [ANY] * extra,
        out_specs=(out_spec,) * len(out_shapes),
        scratch_shapes=scratch,
        compiler_params=pltpu.CompilerParams(vmem_limit_bytes=VMEM_MIB * 1024 * 1024),
        cost_estimate=pl.CostEstimate(
            flops=int(cost_us * 1.15e9), bytes_accessed=0, transcendentals=0
        ),
    )(*args, *deps)


def sds(shape, dtype):
    return jax.ShapeDtypeStruct(shape, dtype)


MARK = sds((8, 128), F32)


def aligned(index, size):
    return pl.ds(pl.multiple_of(index * size, size), size)


def nt(left, right):
    return lax.dot_general(left, right, (((1,), (1,)), ((), ())), preferred_element_type=F32)


def tn(left, right):
    return lax.dot_general(left, right, (((0,), (0,)), ((), ())), preferred_element_type=F32)


def nn(left, right):
    return jnp.dot(left, right, preferred_element_type=F32)


def frame_blocks(ids, blocks, dst):
    tok = blocks.shape[1]
    return [(blocks.at[ids[1] ^ ORDER[f]], dst.at[pl.ds(f * tok, tok), :]) for f in range(4)]


def h_zero_kernel(ids, inputs, own, own_x, near, far, notes, out, whole, held, wide, shares, sems):
    rows = wide.shape[0] // 8
    frames = held.shape[0]
    pairs = frame_blocks(ids, inputs, held)
    for r in range(8):
        if r < 2:
            piece = (own, own_x)[r].at[pl.ds(0, rows), :]
        else:
            piece = (near, far)[r % 2].at[pl.ds((r // 2 - 1) * rows, rows), :]
        pairs.append((piece, wide.at[aligned(ids[0] ^ r, rows), :]))
    for k, (piece, first) in enumerate(((own, rows), (own_x, rows), (near, 3 * rows), (far, 3 * rows))):
        pairs.append((piece.at[pl.ds(first, 64), :], shares.at[k]))
    run_copies(pairs, sems)
    out[0:frames, :] = nn(held[...], wide[...]).astype(BF16)
    out[frames : frames + 64, :] = (
        shares[0].astype(F32) + shares[1].astype(F32) + shares[2].astype(F32) + shares[3].astype(F32)
    ).astype(BF16)
    out[frames + 64 :, :] = notes[...]
    whole[...] = wide[...]


def qkv_kernel(ids, *refs):
    pieces, weight = refs[:4], refs[4]
    normed_out, hidden_out, packed, told, held, raw, sems = refs[5:]
    tok = packed.shape[1]
    cols = pieces[0].shape[1]
    pairs = [(pieces[ORDER[f]].at[pl.ds(4 * tok, 80), :], raw.at[f]) for f in range(4)]
    for q in range(4):
        for f in range(4):
            pairs.append(
                (
                    pieces[q].at[pl.ds(ORDER[ORDER[f] ^ q] * tok, tok), :],
                    held.at[pl.ds(f * tok, tok), aligned(ids[1] ^ q, cols)],
                )
            )
    run_copies(pairs, sems)
    for f in range(4):
        rows = raw[f].astype(F32)
        told[f, 0:8, :] = unpacked_rows(rows[0:64])
        counts = jnp.concatenate(
            [32.0 * rows[64:65] + rows[65:66], 32.0 * rows[66:67] + rows[67:68], jnp.zeros((6, cols), F32)], axis=0
        )
        told[f, 8:16, :] = jnp.concatenate([counts, jnp.zeros((8, told.shape[2] - cols), F32)], axis=1)
    for f in range(4):
        rows = pl.ds(f * tok, tok)
        hidden = held[rows, :].astype(F32)
        inverse = lax.rsqrt(jnp.mean(hidden * hidden, axis=1, keepdims=True) + EPS)
        normed = (hidden * inverse * scale_of(ids, told.at[f], tok, 0, hidden.shape[1])).astype(BF16)
        normed_out[rows, :] = normed
        if f < 2:
            hidden_out[rows, :] = held[rows, :]
        qkv = nn(normed, weight[...]).astype(BF16)
        group = ids[1] ^ ORDER[f]
        for pair in range(2):
            for part in range(3):
                packed[2 * group + pair, :, pl.ds(part * 128, 128)] = qkv[
                    :, (2 * part + pair) * 128 : (2 * part + pair + 1) * 128
                ]


def turn(vectors, cosine, sine):
    lane = lax.broadcasted_iota(jnp.int32, vectors.shape, 1)
    first = (lane & 63) < 32
    other = jnp.where(first, pltpu.roll(vectors, 96, 1), pltpu.roll(vectors, 32, 1))
    return vectors * cosine + other * sine


CHUNK = 1024


def rotated(qkv, cosine, sine):
    total = qkv.shape[0] * qkv.shape[1]
    queries = qkv[:, :, 0:128].reshape(total, 128).astype(F32)
    keys = qkv[:, :, 128:256].reshape(total, 128).astype(F32)
    low_q = (turn(queries, cosine[...], sine[...])).astype(BF16) * jnp.asarray(0.125, BF16)
    low_k = turn(keys, cosine[...], sine[...]).astype(BF16)
    return low_q, low_k


def owners_of(ids, told, total):
    utts = told.shape[1] // 2
    group = ids[1] ^ (ids[0] >> 1)
    lens = jnp.zeros((2 * utts, utts), F32)
    for f in range(4):
        lens = lens + jnp.where(group == ORDER[f], told[f, :, 0:utts], 0.0)
    _, end, _, end_col = utt_bounds(lens, utts)
    down = lax.broadcasted_iota(jnp.int32, (total, utts), 0).astype(F32)
    across = lax.broadcasted_iota(jnp.int32, (utts, total), 1).astype(F32)
    col = jnp.sum(jnp.where(down >= end, 1.0, 0.0), axis=1, keepdims=True)
    row = jnp.sum(jnp.where(across >= end_col, 1.0, 0.0), axis=0, keepdims=True)
    return col, row


def attend_kernel(ids, qkv, turns, told, out, log_out, owner_row):
    total = turns.shape[0]
    cosine, sine = turns.at[:, 0:128], turns.at[:, 128:256]
    owner_col, owner_row[...] = owners_of(ids, told, total)
    tok = qkv.shape[1]
    queries, keys = rotated(qkv, cosine, sine)
    values = qkv[:, :, 256:384].reshape(total, 128)
    for chunk in range(total // CHUNK):
        rows = slice(chunk * CHUNK, (chunk + 1) * CHUNK)
        same = owner_col == owner_row[:, rows]
        both = []
        for head in range(2):
            lanes = slice(64 * head, 64 * head + 64)
            scores = jnp.where(same, nt(keys[:, lanes], queries[rows, lanes]), -1e30)
            top = jnp.max(scores, axis=0, keepdims=True)
            weights = jnp.exp(scores - top)
            total_w = jnp.sum(weights, axis=0, keepdims=True)
            log_out[head : head + 1, rows] = top + jnp.log(total_w)
            mixed = tn(values[:, lanes], weights.astype(BF16)) * (1.0 / total_w)
            both.append(mixed.T)
        joined = jnp.concatenate(both, axis=1).astype(BF16)
        for block in range(CHUNK // tok):
            out[chunk * (CHUNK // tok) + block] = joined[block * tok : (block + 1) * tok]


def attend_back_kernel(
    ids, qkv, d_att, turns, log_total, told, out, d_keys, d_values, owner_row
):
    total = turns.shape[0]
    cosine, sine = turns.at[:, 0:128], turns.at[:, 128:256]
    owner_col, owner_row[...] = owners_of(ids, told, total)
    tok = qkv.shape[1]
    queries, keys = rotated(qkv, cosine, sine)
    values = qkv[:, :, 256:384].reshape(total, 128)
    back = d_att[...].reshape(total, 128)
    keys_t = [keys[:, 64 * head : 64 * head + 64].astype(F32).T.astype(BF16) for head in range(2)]
    for chunk in range(total // CHUNK):
        rows = slice(chunk * CHUNK, (chunk + 1) * CHUNK)
        same = owner_col == owner_row[:, rows]
        d_queries, k_terms, v_terms = [], [], []
        for head in range(2):
            lanes = slice(64 * head, 64 * head + 64)
            scores = nt(keys[:, lanes], queries[rows, lanes])
            probs = jnp.where(same, jnp.exp(scores - log_total[head : head + 1, rows]), 0.0)
            d_probs = nt(values[:, lanes], back[rows, lanes])
            delta = jnp.sum(probs * d_probs, axis=0, keepdims=True)
            d_scores = (probs * (d_probs - delta)).astype(BF16)
            v_terms.append(nn(probs.astype(BF16), back[rows, lanes]))
            k_terms.append(nn(d_scores, queries[rows, lanes]))
            d_queries.append(nn(keys_t[head], d_scores).T * 0.125)
        k_new = jnp.concatenate(k_terms, axis=1)
        v_new = jnp.concatenate(v_terms, axis=1)
        if chunk == 0:
            d_keys[...] = k_new
            d_values[...] = v_new
        else:
            d_keys[...] += k_new
            d_values[...] += v_new
        d_q = jnp.concatenate(d_queries, axis=1)
        d_q = turn(d_q, cosine[rows, :], -sine[rows, :]).astype(BF16)
        for block in range(CHUNK // tok):
            out[chunk * (CHUNK // tok) + block, :, 0:128] = d_q[block * tok : (block + 1) * tok]
    d_k = turn(d_keys[...], cosine[...], -sine[...]).astype(BF16)
    out[:, :, 128:256] = d_k.reshape(total // tok, tok, 128)
    out[:, :, 256:384] = d_values[...].astype(BF16).reshape(total // tok, tok, 128)


def attended_pairs(ids, blocks, dst, tok, parts):
    pairs = []
    for f in range(4):
        for pair in range(2):
            for part in range(parts):
                pairs.append(
                    (
                        blocks.at[2 * (ids[1] ^ ORDER[f]) + pair, :, pl.ds(part * 128, 128)],
                        dst.at[pl.ds(f * tok, tok), pl.ds((2 * part + pair) * 128, 128)],
                    )
                )
    return pairs


def packed_rows(wide):
    return jnp.concatenate([wide[:, k : k + 256] for k in range(0, wide.shape[1], 256)], axis=0)


def unpacked_rows(rows):
    return jnp.concatenate([rows[k : k + 8] for k in range(0, rows.shape[0], 8)], axis=1)


def cut_skip_kernel(ids, weight, emb, cond_weight, piece):
    rows = weight.shape[0]
    piece[0:rows, :] = weight[:, aligned(ids[1], piece.shape[1])]
    piece[rows:, :] = packed_rows(nn(emb[...], cond_weight[...])).astype(BF16)


def gather_kernel(p1, p2, p3, out):
    rows = (out.shape[0] - 64) // 3
    total = jnp.zeros((64, out.shape[1]), F32)
    for k, piece in enumerate((p1, p2, p3)):
        out[k * rows : (k + 1) * rows, :] = piece[0:rows, :]
        total = total + piece[rows:, :].astype(F32)
    out[3 * rows :, :] = total.astype(BF16)


def join_kernel(left, right, joined):
    width = left.shape[1]
    for k in range(joined.shape[0]):
        joined[k, :, 0:width] = left[...]
        joined[k, :, width:] = right[...]


def near_kernel(even, odd, *outs):
    for k, out in enumerate(outs):
        out[...] = (even[k].astype(F32) + odd[k].astype(F32)).astype(BF16)


def add_kernel(left, right, out, mark):
    out[...] = (left[...].astype(F32) + right[...].astype(F32)).astype(out.dtype)
    mark[...] = jnp.zeros_like(mark)


def add_twice_kernel(left, right, out, again):
    total = (left[...].astype(F32) + right[...].astype(F32)).astype(out.dtype)
    out[...] = total
    again[...] = total


def add_three_kernel(first, second, third, out):
    total = first[...].astype(F32) + second[...].astype(F32) + third[...].astype(F32)
    out[...] = total.astype(out.dtype)


def choose_kernel(ids, own, other, out, mark):
    mine = (ids[0] & 1) == (ids[1] & 1)

    @pl.when(mine)
    def _():
        out[...] = own[...]

    @pl.when(jnp.logical_not(mine))
    def _():
        out[...] = other[...]

    mark[...] = jnp.zeros_like(mark)


def pick_kernel(ids, own, near, far, farther, out):
    z, y = ids[0] >> 1, ids[1] >> 1
    rows = own.shape[0]
    low = z >> 1
    source = (z & 1) == y
    first, second = aligned(low, rows), aligned(1 - low, rows)

    @pl.when(source)
    def _():
        out[first, :] = own[...]
        out[second, :] = far[...]

    @pl.when(jnp.logical_not(source))
    def _():
        out[first, :] = near[...]
        out[second, :] = farther[...]


def copy_kernel(source, out):
    out[...] = source[...]


def stack_kernel(*refs):
    out, mark = refs[-2:]
    for k, ref in enumerate(refs[:-2]):
        out[k] = ref[...]
    mark[...] = jnp.zeros_like(mark)


def cut_qkv_kernel(ids, qkv, piece):
    for block in range(piece.shape[1] // 128):
        piece[:, pl.ds(block * 128, 128)] = qkv[:, aligned(4 * block + ids[1], 128)]


def cut_feed_kernel(ids, up, down, piece, sem):
    fetch = pltpu.make_async_copy(down.at[aligned(ids[1], 128), :], piece.at[:, up.shape[1] // 4 :], sem)
    fetch.start()
    for block in range(up.shape[1] // 512):
        piece[:, pl.ds(block * 128, 128)] = up[:, aligned(4 * block + ids[1], 128)]
    fetch.wait()


def utt_bounds(told, utts):
    row = lax.broadcasted_iota(jnp.int32, (utts, utts), 0)
    col = lax.broadcasted_iota(jnp.int32, (utts, utts), 1)
    lens = told[utts : utts + 1, 0:utts]
    spread = jnp.broadcast_to(lens, (utts, utts))
    lens_col = jnp.sum(jnp.where(row == col, spread, 0.0), axis=1, keepdims=True)
    ends = jnp.sum(jnp.where(row <= col, lens_col, 0.0), axis=0, keepdims=True)
    ends_col = jnp.sum(jnp.where(col <= row, spread, 0.0), axis=1, keepdims=True)
    return ends - lens, ends, ends_col - lens_col, ends_col


def scale_of(ids, told, tok, first_col, width):
    utts = told.shape[0] // 2
    begin, end, _, _ = utt_bounds(told, utts)
    frame = (ids[0] * tok + lax.broadcasted_iota(jnp.int32, (tok, utts), 0)).astype(F32)
    onehot = jnp.where((frame >= begin) & (frame < end), 1.0, 0.0).astype(BF16)
    cond = told[0:utts, first_col : first_col + width]
    high = cond.astype(BF16)
    rest = cond - high.astype(F32)
    low = rest.astype(BF16)
    return 1.0 + (nn(onehot, high) + nn(onehot, low))


def utt_picks(ids, told, tok):
    utts = told.shape[0] // 2
    _, _, begin, end = utt_bounds(told, utts)
    frame = (ids[0] * tok + lax.broadcasted_iota(jnp.int32, (utts, tok), 1)).astype(F32)
    return jnp.where((frame >= begin) & (frame < end), 1.0, 0.0).astype(BF16)


def project_kernel(ids, blocks, weight, keep, send, attended, sems):
    tok = blocks.shape[1]
    run_copies(attended_pairs(ids, blocks, attended, tok, 1), sems)
    send[...] = nn(attended[2 * tok :, :], weight[...]).astype(BF16)
    keep[...] = nn(attended[0 : 2 * tok, :], weight[...])


def residual_kernel(ids, hidden, part, other, told, h_one_out, normed_out):
    tok = hidden.shape[0] // 2
    for f in range(2):
        rows, swap = pl.ds(f * tok, tok), pl.ds((1 - f) * tok, tok)
        h_one = hidden[rows, :].astype(F32) + part[rows, :].astype(F32) + other[swap, :].astype(F32)
        inverse = lax.rsqrt(jnp.mean(h_one * h_one, axis=1, keepdims=True) + EPS)
        h_one_out[rows, :] = h_one
        scale = scale_of(ids, told.at[f], tok, h_one.shape[1], h_one.shape[1])
        normed_out[rows, :] = (h_one * inverse * scale).astype(BF16)


def gelu_parts(pre):
    size = jnp.abs(pre)
    decay = jnp.exp(-0.5 * pre * pre)
    t = 1.0 / (1.0 + (0.3275911 * 2.0**-0.5) * size)
    series = t * (0.254829592 + t * (-0.284496736 + t * (1.421413741 + t * (-1.453152027 + t * 1.061405429))))
    tail = 0.5 * series * decay
    half = jnp.where(pre < 0.0, tail, 1.0 - tail)
    return pre * half, half + pre * decay * ((2.0 * math.pi) ** -0.5)


def feed_kernel(ids, *refs):
    normed, normed_c, cots, weight = refs[:4]
    act_out, d_pre_out, keep, send = refs[4:]
    tok = cots.shape[1]
    hidden = act_out.shape[1]
    for f in range(4):
        block = pl.ds(f * tok, tok)
        rows = pl.ds((f % 2) * tok, tok)
        pre = nn((normed, normed_c)[f // 2][rows, :], weight[:, 0:hidden])
        act, slope = gelu_parts(pre)
        act_out[block, :] = act.astype(BF16)
        d_pre = (nt(cots[f], weight[:, hidden:]) * slope).astype(BF16)
        d_pre_out[block, :] = d_pre
        d_normed = nt(d_pre, weight[:, 0:hidden])
        if f < 2:
            keep[block, :] = d_normed
        else:
            send[rows, :] = d_normed.astype(BF16)


def feed_grad_kernel(normed, normed_c, cots, act, d_pre, out, held, sems):
    tok = cots.shape[1]
    run_copies([(normed, held.at[pl.ds(0, 2 * tok), :]), (normed_c, held.at[pl.ds(2 * tok, 2 * tok), :])], sems)
    cots_all = cots[...].reshape(4 * tok, cots.shape[2])
    cols = act.shape[1]
    for r in range(8):
        block = pl.ds(r * 128, 128)
        out[block, 0:cols] = tn(held[:, block], d_pre[...]).astype(BF16)
        out[block, cols:] = tn(act[:, block], cots_all).astype(BF16)


def feed_out_kernel(act, weight, keep, send):
    half = keep.shape[0]
    hidden = act.shape[1]
    keep[...] = nn(act[0:half, :], weight[:, hidden:])
    send[...] = nn(act[half:, :], weight[:, hidden:]).astype(BF16)


def norm_back(hidden, scale, d_normed):
    inverse = lax.rsqrt(jnp.mean(hidden * hidden, axis=1, keepdims=True) + EPS)
    y = hidden * inverse
    d_y = d_normed * scale
    d_hidden = inverse * (d_y - y * jnp.mean(d_y * y, axis=1, keepdims=True))
    return d_hidden, d_normed * y


def norm_back_kernel(first_col, ids, hidden, part, other, base, told, low_out, sums_out):
    tok = hidden.shape[0] // 2
    width = hidden.shape[1]
    for f in range(2):
        rows, swap = pl.ds(f * tok, tok), pl.ds((1 - f) * tok, tok)
        d_normed = part[rows, :].astype(F32) + other[swap, :].astype(F32)
        scale = scale_of(ids, told.at[f], tok, first_col, width)
        d_hidden, d_scale = norm_back(hidden[rows, :].astype(F32), scale, d_normed)
        added = base[f].astype(F32) + d_hidden
        low_out[rows, :] = added.astype(low_out.dtype)
        if f == 0:
            sums_out[...] = nn(utt_picks(ids, told.at[0], tok), d_scale.astype(BF16))


def d_attended_kernel(ids, d_h, d_h_c, weight, packed):
    tok = packed.shape[1]
    for f in range(4):
        rows = pl.ds((f % 2) * tok, tok)
        part = nt((d_h, d_h_c)[f // 2][rows, :], weight[...]).astype(BF16)
        group = ids[1] ^ ORDER[f]
        for pair in range(2):
            packed[2 * group + pair] = part[:, pair * 128 : (pair + 1) * 128]


def qkv_back_kernel(ids, blocks, weight, keep, send, joined, sems):
    tok = blocks.shape[1]
    run_copies(attended_pairs(ids, blocks, joined, tok, 3), sems)
    half = keep.shape[0]
    send[...] = nt(joined[half:, :], weight[...]).astype(BF16)
    keep[...] = nt(joined[0:half, :], weight[...])


def qkv_grad_kernel(ids, normed, joined, d_h, d_h_c, a0, a2, a1, a3, even, odd, attended, sems):
    tok = a0.shape[0] // 4
    half = d_h.shape[0]
    pairs = []
    for q, piece in enumerate((a0, a1, a2, a3)):
        for f in range(4):
            for pair in range(2):
                pairs.append(
                    (
                        piece.at[pl.ds(ORDER[ORDER[f] ^ q] * tok, tok), pl.ds(pair * 128, 128)],
                        attended.at[pl.ds(f * tok, tok), aligned((ids[1] ^ q) + 4 * pair, 128)],
                    )
                )
    run_copies(pairs, sems)
    cols = joined.shape[1]
    mine = aligned(ids[1], 256)
    for r in (1, 3, 5, 7, 0, 2, 4, 6):
        block = aligned(ids[0] ^ r, 128)
        target = (even, odd)[r % 2]
        target[r // 2, :, 0:cols] = tn(normed[:, block], joined[...]).astype(BF16)
        target[r // 2, :, cols:] = (
            tn(attended[0:half, block], d_h[:, mine]) + tn(attended[half:, block], d_h_c[:, mine])
        ).astype(BF16)


def skip_back_kernel(ids, d_h, d_h_c, inputs, sums_attn, sums_ffn, even, odd, sums, held, sems):
    tok = inputs.shape[1]
    run_copies(frame_blocks(ids, inputs, held), sems)
    mine = aligned(ids[1], 256)
    near, far = d_h[:, mine], d_h_c[:, mine]
    half = 2 * tok
    for r in (1, 3, 5, 7, 0, 2, 4, 6):
        block = aligned(ids[0] ^ r, 256)
        grad = (tn(held[0:half, block], near) + tn(held[half:, block], far)).astype(BF16)
        if r % 2:
            odd[(r // 2) * 256 : (r // 2) * 256 + 256, :] = grad
        else:
            even[r // 2] = grad
    low = packed_rows(jnp.concatenate([sums_attn[...], sums_ffn[...]], axis=1)).astype(BF16)
    odd[1024:, :] = low
    sums[...] = low


def skip_near_kernel(even, sums, arrived, *outs):
    both = (sums[...].astype(F32) + arrived[1024:, :].astype(F32)).astype(BF16)
    for k, out in enumerate(outs):
        out[0:256, :] = (even[k].astype(F32) + arrived[k * 256 : (k + 1) * 256, :].astype(F32)).astype(BF16)
        out[256:, :] = both


def in_back_kernel(ids, d_h, near, far, in_out, skip_out):
    tok, width = in_out.shape
    total = jnp.zeros((tok, 2 * width), F32)
    for q in range(4):
        weight = (near, far)[q % 2].at[q // 2]
        total = total + nt(d_h[0:tok, aligned(ids[1] ^ q, 256)], weight[...])
    in_out[...] = total[:, 0:width].astype(BF16)
    skip_out[...] = total[:, width:].astype(BF16)


def spread_feed_kernel(ids, near, far, up_o, down_o, mark):
    hidden = near.shape[2] - down_o.shape[1]
    for q in range(4):
        part = ids[1] ^ q
        feed = (near, far)[q % 2].at[q // 2]
        for block in range(hidden // 128):
            up_o[:, aligned(4 * block + part, 128)] = feed[:, pl.ds(block * 128, 128)].astype(F32)
        down_o[aligned(part, 128), :] = feed[:, hidden:].astype(F32)
    mark[...] = jnp.zeros_like(mark)


def last_kernel(p0, p1, p2, p3, q0, q1, q2, q3, out):
    qkv = q0[...].astype(F32) + q1[...].astype(F32) + q2[...].astype(F32) + q3[...].astype(F32)
    skip = p0[...].astype(F32) + p1[...].astype(F32) + p2[...].astype(F32) + p3[...].astype(F32)
    out[:, 0:1024] = qkv.astype(BF16)
    out[:, 1024:1280] = skip[0:128].astype(BF16)
    out[:, 1280:1536] = skip[128:256].astype(BF16)
    out[0:64, 1536:1792] = skip[256:].astype(BF16)
    out[64:, 1536:1792] = jnp.zeros((64, 256), BF16)


def spread_kernel(ids, near, far, emb, qkv_o, out_o, skip_o, cond_o):
    rows = qkv_o.shape[0]
    utts = emb.shape[0] // 4
    for q in range(4):
        part = ids[1] ^ q
        piece = (near, far)[q % 2].at[q // 2]
        for block in range(6):
            qkv_o[:, aligned(4 * block + part, 128)] = piece[0:rows, pl.ds(block * 128, 128)].astype(F32)
        out_o[:, aligned(part, 256)] = piece[0:rows, pl.ds(768, 256)].astype(F32)
        skip_o[0:rows, aligned(part, 256)] = piece[0:rows, pl.ds(1024, 256)].astype(F32)
        skip_o[rows:, aligned(part, 256)] = piece[0:rows, pl.ds(1280, 256)].astype(F32)
    steps = emb[...].astype(F32)
    total = jnp.zeros(cond_o.shape, F32)
    for f in range(4):
        sums = unpacked_rows((near, far)[f // 2][f % 2, 0:64, 1536:1792].astype(F32)).astype(BF16)
        total = total + tn(steps[f * utts : (f + 1) * utts, :].astype(BF16), sums)
    cond_o[...] = total


def stack(arrays, deps=()):
    shape = (len(arrays),) + arrays[0].shape
    return call(stack_kernel, [sds(shape, arrays[0].dtype), MARK], [VMEM] * len(arrays), [], list(arrays), deps=deps)


def around(piece):
    return [piece, from_grp(piece, 2), from_grp(piece, 1), from_grp(piece, 3)]


def gather_groups(piece):
    along_y = from_grp(piece, 2)
    return [piece, along_y, from_grp(piece, 1), from_grp(along_y, 1)]


def gather_pairs(piece, deps=()):
    near, _ = stack([piece, from_grp(piece, 2)], deps)
    return near, from_grp(near, 1)


def scatter_near(even, odd, deps):
    arrived = from_seq(odd, 1)
    return call(near_kernel, [sds(even.shape[1:], BF16)] * 4, [VMEM] * 2, [], [even, arrived], deps=deps)


def by_mask(pieces):
    return [pieces[0], pieces[2], pieces[1], pieces[3]]


def halves_sum(keep, send):
    kept, sent = call(
        add_twice_kernel, [sds(keep.shape, BF16)] * 2, [VMEM] * 2, [], [keep, from_grp(send, 1)]
    )
    return kept, from_grp(sent, 2)


def add_two(left, right, deps=()):
    return call(add_kernel, [sds(left.shape, BF16), MARK], [VMEM] * 2, [], [left, right], deps=deps)


def exchange(array, cols):
    return lax.all_to_all(array, "seq", 0, 0, tiled=True)


def out_moves(mask, keep):
    pairs = []
    for t in range(4):
        for slot in range(8):
            if keep(slot, t):
                pairs.append((t * 8 + slot, t * 8 + (slot ^ mask)))
    return pairs


def out_along_z(piece):
    def holds(slot, t):
        return (slot & 1) == (t & 1) and ((slot >> 1) & 1) == (t >> 1)

    return [lax.ppermute(piece, ("grp", "seq"), out_moves(2 * k, holds)) for k in range(1, 4)]


def out_along_x(rows):
    return lax.ppermute(rows, ("grp", "seq"), out_moves(1, lambda slot, t: (slot & 1) == (t & 1)))


def tp_body(
    hidden_in, skips, lengths, times, skip_weight, cond_weight, qkv_weight, out_weight,
    up_weight, down_weight, cotangent,
):
    tok, width = hidden_in.shape
    ff = up_weight.shape[1]
    frames = 8 * tok
    slot = lax.axis_index("seq")
    part = lax.axis_index("grp")
    ids = jnp.stack([slot, part]).astype(jnp.int32)
    sem = pltpu.SemaphoreType.DMA

    half_width = width // 2
    rows_here = cond_weight.shape[0]
    utts = times.shape[1]

    def embed_here(time_rows):
        column = (slot * rows_here + jnp.arange(rows_here, dtype=jnp.int32)) % half_width
        freqs = jnp.exp(-math.log(10000.0) * column.astype(F32) / half_width)
        angles = time_rows[:, None] * freqs[None, :]
        return jnp.where(slot * rows_here < half_width, jnp.sin(angles), jnp.cos(angles)).astype(BF16)

    skip_rows = skip_weight.shape[0]
    (skip_piece,) = call(
        cut_skip_kernel,
        [sds((skip_rows + 64, 256), BF16)],
        [SMEM] + [VMEM] * 3,
        [],
        [ids, skip_weight, embed_here(times[0].astype(F32)), cond_weight],
    )
    (qkv_piece,) = call(cut_qkv_kernel, [sds((128, 768), BF16)], [SMEM, VMEM], [], [ids, qkv_weight])
    (skip_same,) = call(
        gather_kernel,
        [sds((3 * skip_rows + 64, 256), BF16)],
        [VMEM] * 3,
        [],
        [from_seq(skip_piece, 2 * k) for k in range(1, 4)],
        deps=[qkv_piece],
    )
    skip_other = from_seq(skip_same, 1)
    (joined,) = call(
        join_kernel, [sds((4, tok, 2 * width), BF16)], [VMEM] * 2, [], [hidden_in, skips], deps=[skip_piece]
    )
    inputs = lax.all_to_all(joined, "grp", 0, 0, tiled=True)
    w_qkv = lax.all_gather(qkv_piece, "seq", axis=0, tiled=True)
    (feed_piece,) = call(
        cut_feed_kernel,
        [sds((128, ff // 4 + width), BF16)],
        [SMEM, VMEM, ANY],
        [sem],
        [ids, up_weight, down_weight],
        deps=[qkv_piece],
    )
    w_feed = lax.all_gather(feed_piece, "seq", axis=0, tiled=True)

    counts = jnp.stack([lengths[0] >> 5, lengths[0] & 31, times[0] >> 5, times[0] & 31])
    notes = jnp.zeros((16, 256), BF16).at[0:4, 0:utts].set(counts.astype(BF16))

    (out_piece,) = call(copy_kernel, [sds(out_weight.shape, BF16)], [VMEM], [], [out_weight], deps=[skip_same])
    out_came = out_along_z(out_piece)

    inverse = jnp.exp(-math.log(10000.0) * jnp.arange(32, dtype=F32) / 32)
    turn_angles = jnp.arange(frames, dtype=F32)[:, None] * inverse[None, :]
    cos_half, sin_half = jnp.cos(turn_angles), jnp.sin(turn_angles)
    turns = jnp.concatenate([cos_half] * 4 + [-sin_half, sin_half] * 2, axis=1)

    h_cols, w_skip = call(
        h_zero_kernel,
        [sds((4 * tok + 80, 256), BF16), sds((2 * width, 256), BF16)],
        [SMEM] + [ANY] * 5 + [VMEM],
        [
            pltpu.VMEM((4 * tok, 2 * width), BF16),
            pltpu.VMEM((2 * width, 256), BF16),
            pltpu.VMEM((4, 64, 256), BF16),
            sem((16,)),
        ],
        [ids, inputs, skip_piece, from_seq(skip_piece, 1), skip_same, skip_other, notes],
        deps=out_came,
        cost_us=100.0,
    )
    h_pieces = gather_groups(h_cols)
    h_pieces = [h_pieces[0], h_pieces[2], h_pieces[1], h_pieces[3]]
    normed, h_zero, packed, told = call(
        qkv_kernel,
        [
            sds((4 * tok, width), BF16),
            sds((2 * tok, width), BF16),
            sds((8, tok, 384), BF16),
            sds((4, 2 * utts, 2 * width), F32),
        ],
        [SMEM] + [ANY] * 4 + [VMEM],
        [pltpu.VMEM((4 * tok, width), BF16), pltpu.VMEM((4, 80, 256), BF16), sem((20,))],
        [ids] + h_pieces + [w_qkv],
    )
    emb_all = embed_here(told[:, utts + 1, :utts].reshape(4 * utts))
    qkv = exchange(packed, 384)
    (out_picked,) = call(
        pick_kernel, [sds((2 * tok, width), BF16)], [SMEM] + [VMEM] * 4, [], [ids, out_piece] + out_came
    )
    (w_skip,) = call(copy_kernel, [sds(w_skip.shape, BF16)], [VMEM], [], [w_skip], deps=[packed])
    skip_y = from_grp(w_skip, 2)
    w_out, out_mark = call(
        choose_kernel,
        [sds((2 * tok, width), BF16), MARK],
        [SMEM] + [VMEM] * 2,
        [],
        [ids, out_picked, out_along_x(out_picked)],
    )
    skip_near, skip_mark = stack([w_skip, skip_y], [packed])
    skip_far = from_grp(skip_near, 1)
    mixed, log_total = call(
        attend_kernel,
        [sds((8, tok, 128), BF16), sds((2, frames), F32)],
        [SMEM] + [VMEM] * 3,
        [pltpu.VMEM((1, frames), F32)],
        [ids, qkv, turns, told],
        deps=[out_mark, skip_mark],
    )
    attended_blocks = exchange(mixed, 128)
    (cot_piece,) = call(
        copy_kernel, [sds((tok, width), BF16)], [VMEM], [], [cotangent], deps=[mixed]
    )
    cots, cot_mark = stack(around(cot_piece))
    keep, send, attended = call(
        project_kernel,
        [
            sds((2 * tok, width), F32),
            sds((2 * tok, width), BF16),
            sds((4 * tok, 256), BF16),
        ],
        [SMEM, ANY, VMEM],
        [sem((8,))],
        [ids, attended_blocks, w_out],
        deps=[cot_mark],
    )
    h_part, h_part_y = halves_sum(keep, send)
    h_one, normed_two = call(
        residual_kernel,
        [sds((2 * tok, width), F32), sds((2 * tok, width), BF16)],
        [SMEM] + [VMEM] * 4,
        [],
        [ids, h_zero, h_part, h_part_y, told],
    )
    normed_two_c = from_grp(normed_two, 1)
    quarter = ff // 4
    act, d_pre, keep, send = call(
        feed_kernel,
        [
            sds((4 * tok, quarter), BF16),
            sds((4 * tok, quarter), BF16),
            sds((2 * tok, width), F32),
            sds((2 * tok, width), BF16),
        ],
        [SMEM] + [VMEM] * 4,
        [],
        [ids, normed_two, normed_two_c, cots, w_feed],
    )

    d_part, d_part_y = halves_sum(keep, send)
    (feed_terms,) = call(
        feed_grad_kernel,
        [sds((width, quarter + width), BF16)],
        [ANY] * 2 + [VMEM] * 3,
        [pltpu.VMEM((4 * tok, width), BF16), sem((2,))],
        [normed_two, normed_two_c, cots, act, d_pre],
        deps=[d_part],
    )
    out_keep, out_send = call(
        feed_out_kernel,
        [sds((2 * tok, width), F32), sds((2 * tok, width), BF16)],
        [VMEM, VMEM],
        [],
        [act, w_feed],
        deps=[feed_terms],
    )
    d_h_one, sums_ffn = call(
        functools.partial(norm_back_kernel, width),
        [sds((2 * tok, width), BF16), sds((utts, width), F32)],
        [SMEM] + [VMEM] * 5,
        [],
        [ids, h_one, d_part, d_part_y, cots, told],
        deps=[out_send],
        cost_us=100.0,
    )
    d_h_one_c = from_grp(d_h_one, 1)
    (d_att_packed,) = call(
        d_attended_kernel,
        [sds((8, tok, 128), BF16)],
        [SMEM, VMEM, VMEM, VMEM],
        [],
        [ids, d_h_one, d_h_one_c, w_out],
    )
    d_att = exchange(d_att_packed, 128)

    feed_own = lax.psum_scatter(feed_terms, "seq", scatter_dimension=0, tiled=True)
    att_pieces = around(attended)
    out_part, out_done = add_two(out_keep, from_grp(out_send, 1), [d_att_packed])
    (d_packed,) = call(
        attend_back_kernel,
        [sds((8, tok, 384), BF16)],
        [SMEM] + [VMEM] * 5,
        [pltpu.VMEM((frames, 128), F32), pltpu.VMEM((frames, 128), F32), pltpu.VMEM((1, frames), F32)],
        [ids, qkv, d_att, turns, log_total, told],
        deps=[out_done],
    )
    d_qkv_blocks = exchange(d_packed, 384)
    (block_out,) = call(
        add_three_kernel,
        [sds((tok, width), BF16)],
        [VMEM] * 3,
        [],
        [h_one[:tok], out_part[:tok], from_grp(out_part[tok:], 2)],
        deps=[d_packed] + att_pieces[1:],
    )
    keep, send, d_qkv = call(
        qkv_back_kernel,
        [sds((2 * tok, width), F32), sds((2 * tok, width), BF16), sds((4 * tok, 768), BF16)],
        [SMEM, ANY, VMEM],
        [sem((24,))],
        [ids, d_qkv_blocks, w_qkv],
        deps=[block_out],
    )
    d_part, d_part_y = halves_sum(keep, send)
    qkv_even, qkv_odd = call(
        qkv_grad_kernel,
        [sds((4, 128, 1024), BF16)] * 2,
        [SMEM] + [VMEM] * 4 + [ANY] * 4,
        [pltpu.VMEM((4 * tok, width), BF16), sem((32,))],
        [ids, normed, d_qkv, d_h_one, d_h_one_c] + att_pieces,
        deps=[d_part],
    )
    d_h_zero, sums_attn = call(
        functools.partial(norm_back_kernel, 0),
        [sds((2 * tok, width), BF16), sds((utts, width), F32)],
        [SMEM] + [VMEM] * 5,
        [],
        [ids, h_zero, d_part, d_part_y, d_h_one.reshape(2, tok, width), told],
        deps=[qkv_odd],
    )
    d_h_zero_c = from_grp(d_h_zero, 1)
    skip_even, skip_odd, skip_sums = call(
        skip_back_kernel,
        [sds((4, 256, 256), BF16), sds((1024 + 64, 256), BF16), sds((64, 256), BF16)],
        [SMEM, VMEM, VMEM, ANY, VMEM, VMEM],
        [pltpu.VMEM((4 * tok, 2 * width), BF16), sem((4,))],
        [ids, d_h_zero, d_h_zero_c, inputs, sums_attn, sums_ffn],
    )
    qkv_near = scatter_near(qkv_even, qkv_odd, [skip_odd])
    qkv_came = [from_seq(qkv_near[k], 2 * k) for k in range(1, 4)]
    last_near = call(
        skip_near_kernel,
        [sds((256 + 64, 256), BF16)] * 4,
        [VMEM] * 3,
        [],
        [skip_even, skip_sums, from_seq(skip_odd, 1)],
        deps=[qkv_near[0]],
    )
    last_came = [from_seq(last_near[k], 2 * k) for k in range(1, 4)]
    in_grad, skip_grad = call(
        in_back_kernel,
        [sds((tok, width), BF16)] * 2,
        [SMEM] + [VMEM] * 3,
        [],
        [ids, d_h_zero, skip_near, skip_far],
        deps=[qkv_came[0], last_near[0]],
    )
    (last_own,) = call(
        last_kernel,
        [sds((128, 1792), BF16)],
        [VMEM] * 8,
        [],
        [last_near[0]] + last_came + [qkv_near[0]] + qkv_came,
        deps=[in_grad],
    )
    feed_near, feed_far = gather_pairs(feed_own, [last_own])
    up_grad, down_grad, up_mark = call(
        spread_feed_kernel,
        [sds((128, ff), F32), sds((ff // 8, width), F32), MARK],
        [SMEM] + [VMEM] * 2,
        [],
        [ids, feed_near, feed_far],
    )
    all_near, all_far = gather_pairs(last_own, [up_mark])
    qkv_grad, out_grad, skip_grad_w, cond_grad = call(
        spread_kernel,
        [
            sds((128, 3 * width), F32),
            sds((128, width), F32),
            sds((256, width), F32),
            sds((rows_here, 2 * width), F32),
        ],
        [SMEM] + [VMEM] * 3,
        [],
        [ids, all_near, all_far, emb_all],
    )
    return (
        block_out, in_grad, skip_grad, skip_grad_w, cond_grad, qkv_grad,
        out_grad, up_grad, down_grad,
    )


def solution(mesh):
    placed = (
        P(("grp", "seq"), None),
        P(("grp", "seq"), None),
        P("grp", None),
        P("grp", None),
        P("seq", None),
        P("seq", None),
        P("seq", None),
        P("seq", None),
        P("seq", None),
        P("seq", None),
        P(("grp", "seq"), None),
    )
    body = tp_body if (mesh.shape["grp"], mesh.shape["seq"]) == (4, 8) else plain_body
    return jax.shard_map(
        body,
        mesh=mesh,
        in_specs=placed,
        out_specs=(
            P(("grp", "seq"), None),
            P(("grp", "seq"), None),
            P(("grp", "seq"), None),
            P("seq", None),
            P("seq", None),
            P("seq", None),
            P("seq", None),
            P("seq", None),
            P("seq", None),
        ),
        check_vma=False,
    )
```
